32 devices in a mesh: stream: 8 (over y, x, core), strip: 4 (over z).
Axes of the slice: x: 2, y: 2, z: 4, core: 2. Of those that a mesh axis runs over, the one named last changes fastest.
Arguments:
- loader_rows: bfloat16 [8, 512, 48], P('stream', 'strip'), may hold values from -12 to 12
- load_owner: int32 [8, 512], P('stream', 'strip'), may hold values from 0 to 7, as said below
- load_slot: int32 [8, 512], P('stream', 'strip'), may hold values from 0 to 127, as said below
- valid_frames: int32 [8], P('stream'), may hold values from 1 to 8
- next_owner: int32 [8], P('stream'), may hold values from 0 to 7, as said below
- pixel_cache: bfloat16 [8, 2, 64, 48], P('stream', None, 'strip'), may hold values from -6 to 6
- act_cache: bfloat16 [8, 2, 64, 16, 128], P('stream', None, 'strip'), may hold values from -4 to 4
- res_cache: bfloat16 [8, 2, 64, 16, 128], P('stream', None, 'strip'), may hold values from -8 to 8
- stem_weight: bfloat16 [3, 3, 3, 3, 128], replicated, may hold values from -0.625 to 0.625
- norm_gain: float32 [128], replicated, may hold values from 0.1 to 1.9
- norm_bias: float32 [128], replicated, may hold values from -2.5 to 2.5
- conv_weight: bfloat16 [3, 3, 3, 128, 128], replicated, may hold values from -0.109375 to 0.109375
- down_weight: bfloat16 [3, 3, 3, 128, 256], replicated, may hold values from -0.109375 to 0.109375
Outputs:
- latents: bfloat16 [8, 4, 32, 8, 256], P('stream', None, 'strip')
- next_pixel_cache: bfloat16 [8, 2, 64, 48], P('stream', None, 'strip')
- next_act_cache: bfloat16 [8, 2, 64, 16, 128], P('stream', None, 'strip')
- next_res_cache: bfloat16 [8, 2, 64, 16, 128], P('stream', None, 'strip')
The draws below stay inside these ranges and needn't reach their ends.
Inputs may be any that keep to these rules, and one draw needn't show every extreme that they name: `load_owner`: among the 128 positions of one stream that fall in one strip, every stream is named by exactly 16. `load_slot`: over all loader rows of strip j that name the same owner, the slots are all different, so each owner receives every slot of strip j exactly once. `next_owner`: A permutation made by passes over the index bits 0, 1, 2 and so on in this order, each pass exchanging some pairs of indices that differ only in that bit.
All inputs are finite; a program needn't handle non-finite values.
Results may differ from the reference program's by a relative error of at most 0.0055.
Values may be sent and summed in bfloat16 or wider, within the bound.
No kernel may reach another device: no remote copies, remote signals or barrier semaphores. Data moves between devices by JAX's collectives and lax.ppermute only.
A program may use at most 64 MiB of HBM per device.

```python
import jax
import jax.numpy as jnp
from jax import lax

FRAMES = 8
R_DEV = 16
COLS = 16
C1 = 128
C2 = 256
GROUPS = 32
STREAMS = 8
ROWS = 64
N_STRIP = 4


def loader_plan(key):
    row_fill = FRAMES * R_DEV
    strip_count = ROWS // R_DEV
    per_peer = row_fill // STREAMS
    repeated = jnp.arange(row_fill, dtype=jnp.int32) // per_peer
    owner_keys = jax.random.split(jax.random.fold_in(key, 11), strip_count * STREAMS)
    owners = jax.vmap(lambda one_key: jax.random.permutation(one_key, repeated))(owner_keys)
    owners = owners.reshape(strip_count, STREAMS, row_fill)
    onehot = (owners[..., None] == jnp.arange(STREAMS, dtype=jnp.int32)).astype(jnp.int32)
    rank_in = jnp.sum(jnp.cumsum(onehot, axis=2) * onehot, axis=3) - 1
    position = jnp.arange(STREAMS, dtype=jnp.int32)[None, :, None] * per_peer + rank_in
    slot_keys = jax.random.split(jax.random.fold_in(key, 12), strip_count * STREAMS)
    tables = jax.vmap(lambda one_key: jax.random.permutation(one_key, row_fill))(slot_keys)
    tables = tables.reshape(strip_count, STREAMS, row_fill)
    strip_ids = jnp.arange(strip_count, dtype=jnp.int32)[:, None, None]
    slots = tables[strip_ids, owners, position]
    owner_out = owners.transpose(1, 0, 2).reshape(STREAMS, strip_count * row_fill)
    slot_out = slots.transpose(1, 0, 2).reshape(STREAMS, strip_count * row_fill)
    return (owner_out.astype(jnp.int32), slot_out.astype(jnp.int32))


def draw_load_owner(key, part):
    return loader_plan(key)[0]


def draw_load_slot(key, part):
    return loader_plan(key)[1]


def draw_loader_rows(key, part):
    owner_out, slot_out = loader_plan(key)
    row_fill = FRAMES * R_DEV
    strip_ids = jnp.arange(FRAMES * ROWS, dtype=jnp.int32) // row_fill
    global_row = (strip_ids[None, :] * R_DEV + slot_out % R_DEV).astype(jnp.int32)
    row_scale = 1.0 + 2.0 * global_row.astype(jnp.float32) / max(ROWS - 1, 1)
    shape_out = (STREAMS, FRAMES * ROWS, 3 * COLS)
    values = jnp.clip(jax.random.normal(jax.random.fold_in(key, 13), shape_out, jnp.float32), -4.0, 4.0)
    return (values * row_scale[..., None]).astype(jnp.bfloat16)


def draw_next_owner(key, part):
    section_count = STREAMS.bit_length() - 1
    position = jnp.arange(STREAMS, dtype=jnp.int32)
    for bit_pos in range(section_count):
        flags = jax.random.randint(jax.random.fold_in(key, 20 + bit_pos), (STREAMS,), 0, 2)
        pair_id = position - position // (1 << bit_pos) % 2 * (1 << bit_pos)
        flipped = flags[pair_id] == 1
        position = jnp.where(flipped, jnp.bitwise_xor(position, 1 << bit_pos), position)
    return position.astype(jnp.int32)


def place_ends(array, key, smallest, high):
    extent = array.shape
    spot = [jax.random.randint(jax.random.fold_in(key, axis), (), 0, extent[axis]) for axis in range(len(extent))]
    array = array.at[tuple(spot)].set(smallest)
    longest = extent.index(max(extent))
    spot[longest] = (spot[longest] + 1) % extent[longest]
    return array.at[tuple(spot)].set(high)


def block_levels(key, extent, shards, smallest, top_value):
    def one(dim, blocks):
        steps = jax.random.uniform(jax.random.fold_in(jax.random.fold_in(key, 6), dim), (blocks,), jnp.float32, smallest / len(shards), top_value / len(shards))
        return jnp.repeat(jnp.exp(steps), extent[dim] // blocks).reshape((-1,) + (1,) * (len(extent) - dim - 1))

    factor_of = one(*shards[0])
    for cut in shards[1:]:
        factor_of = factor_of * one(*cut)
    return factor_of


def gaussian(key, shape, scale, reach, pieces=(), kind=jnp.bfloat16):
    values = scale * jax.random.normal(key, shape, jnp.float32)
    if pieces:
        values = values * block_levels(key, shape, pieces, -0.22, 0.18)
    return jnp.clip(values, -reach, reach).astype(kind)


def setup_inputs(seed: int = 0) -> dict:
    streams_of = jax.random.split(jax.random.key(seed), 14)
    return {
        "loader_rows": draw_loader_rows(jax.random.fold_in(streams_of[13], 71), 0),
        "load_owner": draw_load_owner(jax.random.fold_in(streams_of[13], 71), 0),
        "load_slot": draw_load_slot(jax.random.fold_in(streams_of[13], 71), 0),
        "valid_frames": place_ends(jax.random.randint(streams_of[3], (STREAMS,), 1, FRAMES + 1), jax.random.fold_in(streams_of[3], 1), 1, FRAMES).astype(jnp.int32),
        "next_owner": draw_next_owner(jax.random.fold_in(streams_of[13], 71), 0),
        "pixel_cache": gaussian(streams_of[5], (STREAMS, 2, ROWS, 3 * COLS), 1.5, 6.0, ((0, 8), (2, 4))),
        "act_cache": gaussian(streams_of[6], (STREAMS, 2, ROWS, COLS, C1), 0.7, 4.0, ((0, 8), (2, 4))),
        "res_cache": gaussian(streams_of[7], (STREAMS, 2, ROWS, COLS, C1), 1.5, 8.0, ((0, 8), (2, 4))),
        "stem_weight": gaussian(streams_of[8], (3, 3, 3, 3, C1), 81 ** -0.5, 0.625),
        "norm_gain": jnp.clip(1.0 + 0.18 * jax.random.normal(streams_of[9], (C1,), jnp.float32), 0.1, 1.9),
        "norm_bias": gaussian(streams_of[10], (C1,), 0.5, 2.5, (), jnp.float32),
        "conv_weight": gaussian(streams_of[11], (3, 3, 3, C1, C1), (27 * C1) ** -0.5, 0.109375),
        "down_weight": gaussian(streams_of[12], (3, 3, 3, C1, C2), (27 * C1) ** -0.5, 0.109375),
    }


EPSILON = 1e-06

def conv_same(padded, weight):
    frame_count = padded.shape[0] - 2
    row_count = padded.shape[1] - 2
    col_count = padded.shape[2] - 2
    summed = jnp.zeros((frame_count, row_count, col_count, weight.shape[-1]), jnp.float32)
    for tap_t in range(3):
        for tap_h in range(3):
            stacked = jnp.concatenate([padded[tap_t:tap_t + frame_count, tap_h:tap_h + row_count, tap_w:tap_w + col_count, :] for tap_w in range(3)], axis=-1).astype(jnp.float32)
            kernel = weight[tap_t, tap_h].reshape(-1, weight.shape[-1]).astype(jnp.float32)
            summed = summed + jnp.einsum('trwc,co->trwo', stacked, kernel)
    return summed

def conv_down(padded, weight):
    out_t = (padded.shape[0] - 2) // 2
    out_h = (padded.shape[1] - 1) // 2
    out_w = (padded.shape[2] - 1) // 2
    summed = jnp.zeros((out_t, out_h, out_w, weight.shape[-1]), jnp.float32)
    for tap_t in range(3):
        for tap_h in range(3):
            stacked = jnp.concatenate([padded[tap_t:tap_t + 2 * out_t:2, tap_h:tap_h + 2 * out_h:2, tap_w:tap_w + 2 * out_w:2, :] for tap_w in range(3)], axis=-1).astype(jnp.float32)
            kernel = weight[tap_t, tap_h].reshape(-1, weight.shape[-1]).astype(jnp.float32)
            summed = summed + jnp.einsum('trwc,co->trwo', stacked, kernel)
    return summed

def normalize(hidden_in, mean_val, inv_std, gain_row, offset_row):
    dims_in = hidden_in.shape
    grouped = hidden_in.astype(jnp.float32).reshape(dims_in[:-1] + (mean_val.shape[1], dims_in[-1] // mean_val.shape[1]))
    centered = (grouped - mean_val[:, None, None, :, None]) * inv_std[:, None, None, :, None]
    scaled = centered.reshape(dims_in) * gain_row + offset_row
    return jax.nn.silu(scaled).astype(jnp.bfloat16)

def encode_stream(operands, stem_weight, norm_gain, norm_bias, conv_weight, down_weight):
    pixels, valid_count, pixel_prior, act_prior, res_prior = operands
    full_pix = jnp.concatenate([pixel_prior, pixels], 0)
    new_pix = lax.dynamic_slice_in_dim(full_pix, valid_count, 2, 0)
    planes = full_pix.reshape(FRAMES + 2, ROWS, 3, COLS).transpose(0, 1, 3, 2)
    planes = jnp.pad(planes, ((0, 0), (1, 1), (1, 1), (0, 0)))
    stem_out = conv_same(planes, stem_weight).astype(jnp.bfloat16)
    grouped = stem_out.astype(jnp.float32).reshape(FRAMES, ROWS, COLS, GROUPS, C1 // GROUPS)
    cell_count = ROWS * COLS * (C1 // GROUPS)
    mean_val = lax.optimization_barrier(jnp.sum(grouped, axis=(1, 2, 4))) / cell_count
    inv_std = lax.rsqrt(lax.optimization_barrier(jnp.sum(grouped * grouped, axis=(1, 2, 4))) / cell_count - mean_val * mean_val + EPSILON)
    act_now = normalize(stem_out, mean_val, inv_std, norm_gain, norm_bias)
    full_act = jnp.concatenate([act_prior, act_now], 0)
    new_act = lax.dynamic_slice_in_dim(full_act, valid_count, 2, 0)
    padded_act = jnp.pad(full_act, ((0, 0), (1, 1), (1, 1), (0, 0)))
    res_out = (stem_out.astype(jnp.float32) + conv_same(padded_act, conv_weight)).astype(jnp.bfloat16)
    full_res = jnp.concatenate([res_prior, res_out], 0)
    new_res = lax.dynamic_slice_in_dim(full_res, valid_count, 2, 0)
    padded_res = jnp.pad(full_res, ((0, 0), (1, 0), (1, 0), (0, 0)))
    latent = conv_down(padded_res, down_weight)
    live_frame = 2 * jnp.arange(FRAMES // 2, dtype=jnp.int32) < valid_count
    latent = jnp.where(live_frame[:, None, None, None], latent, jnp.zeros((), jnp.float32)).astype(jnp.bfloat16)
    return (latent, new_pix, new_act, new_res)

def reference(loader_rows, load_owner, load_slot, valid_frames, next_owner, pixel_cache, act_cache, res_cache, stem_weight, norm_gain, norm_bias, conv_weight, down_weight):
    row_fill = FRAMES * R_DEV
    strip_of = jnp.broadcast_to((jnp.arange(FRAMES * ROWS, dtype=jnp.int32) // row_fill)[None, :], load_owner.shape)
    placed = jnp.zeros((STREAMS, N_STRIP, row_fill, 3 * COLS), jnp.bfloat16)
    placed = placed.at[load_owner, strip_of, load_slot].set(loader_rows)
    pixels = placed.reshape(STREAMS, N_STRIP, FRAMES, R_DEV, 3 * COLS).transpose(0, 2, 1, 3, 4).reshape(STREAMS, FRAMES, ROWS, 3 * COLS)

    def encoder(operands):
        return encode_stream(operands, stem_weight, norm_gain, norm_bias, conv_weight, down_weight)
    latents, new_pix, new_act, new_res = lax.map(encoder, (pixels, valid_frames, pixel_cache, act_cache, res_cache))
    next_pixel_cache = jnp.zeros_like(new_pix).at[next_owner].set(new_pix)
    next_act_cache = jnp.zeros_like(new_act).at[next_owner].set(new_act)
    next_res_cache = jnp.zeros_like(new_res).at[next_owner].set(new_res)
    return (latents, next_pixel_cache, next_act_cache, next_res_cache)
```

```python
import functools

import jax
import jax.numpy as jnp
from jax import lax
from jax.experimental import pallas as pl
from jax.experimental.pallas import tpu as pltpu
from jax.sharding import PartitionSpec as P

FRAMES = 8
GROUPS = 32
EPSILON = 1e-06
F32 = jnp.float32
BF16 = jnp.bfloat16
VM = pl.BlockSpec(memory_space=pltpu.VMEM)
SM = pl.BlockSpec(memory_space=pltpu.SMEM)


def iota(shape, axis):
    return lax.broadcasted_iota(jnp.int32, shape, axis)


def dot(a, b):
    return jnp.dot(a, b, preferred_element_type=F32)


def dot_nt(a, b):
    return lax.dot_general(a, b, (((1,), (1,)), ((), ())), preferred_element_type=F32)


def sort_kernel(streams, rows_ref, owner_ref, slot_ref, out_ref, wide):
    fill = rows_ref.shape[0]
    per = fill // streams
    lines = fill // 2
    wide[...] = jnp.zeros(wide.shape, F32)
    wide[:, 0 : rows_ref.shape[1]] = rows_ref[...].astype(F32)
    owner = owner_ref[...]
    onehot = iota((streams, fill), 0) == owner
    hot = jnp.where(onehot, 1.0, 0.0)
    upper = jnp.where(iota((fill, fill), 0) <= iota((fill, fill), 1), 1.0, 0.0).astype(BF16)
    running = dot(hot.astype(BF16), upper)
    rank = jnp.sum(hot * running, axis=0, keepdims=True).astype(jnp.int32) - 1
    half = rank // (per // 2)
    line = owner * (per // 2) + rank - half * (per // 2)
    line = jnp.broadcast_to(line, (lines, fill))
    half = jnp.broadcast_to(half, (lines, fill))
    here = iota((lines, fill), 0) == line
    slot = jnp.broadcast_to(slot_ref[...].astype(F32), (lines, fill))
    data = wide[...].astype(BF16)
    parts = []
    for side in range(2):
        pick = jnp.where(here & (half == side), 1.0, 0.0)
        picked = dot(pick.astype(BF16), data)
        slots = jnp.sum(pick * slot, axis=1, keepdims=True)
        parts.append(jnp.where(iota((lines, 128), 1) == 48, slots, picked))
    out = jnp.where(iota((lines, 128), 1) < 64, parts[0], pltpu.roll(parts[1], 64, 1))
    out_ref[...] = out.astype(BF16)


def band_kernel(sw_ref, out_ref):
    cols = 16
    for tap in range(27):
        b, a, c = tap // 9, tap // 3 % 3, tap % 3
        for w in range(cols):
            row = iota((cols, 128), 0)
            block = jnp.zeros((cols, 128), F32)
            for e in range(3):
                line = (a * 9 + b * 3 + e) * 3 + c
                block = jnp.where(row == w + e - 1, sw_ref[line : line + 1, :], block)
            out_ref[tap * cols : (tap + 1) * cols, w * 128 : (w + 1) * 128] = block.astype(BF16)


def main_kernel(
    strips,
    valid_ref,
    recv_ref,
    pix0_ref,
    pix1_ref,
    pix2_ref,
    pix3_ref,
    band_ref,
    gain_ref,
    bias_ref,
    conv_ref,
    down_ref,
    act_cache_ref,
    res_cache_ref,
    below_ref,
    above_ref,
    lat_ref,
    new_pix_ref,
    new_act_ref,
    new_res_ref,
    pc,
    zs,
    xs,
    stem,
    act,
    res,
    cache,
    rcache,
    act3,
    res3,
    lat,
):
    j = lax.axis_index("strip")
    valid = valid_ref[0]
    rows_all = strips * 16
    pc[...] = jnp.zeros(pc.shape, F32)
    for k, ref in enumerate((pix0_ref, pix1_ref, pix2_ref, pix3_ref)):
        pc[lax.rem(j + strips - k, strips), :, 0:48] = ref[...].astype(F32)
    zs[...] = jnp.zeros(zs.shape, F32)
    lane = iota((128, 128), 1)
    sub = iota((128, 128), 0)
    slot_lane = jnp.where(iota((8, 128), 1) == 48, 1.0, 0.0).astype(BF16)
    crow, cframe = iota((128, 32), 1) % 16, iota((128, 32), 1) // 16
    csub = iota((128, 32), 0)
    for s in range(strips):
        line = recv_ref[s].astype(F32)
        both = jnp.concatenate([line, pltpu.roll(line, 64, 1)], axis=0)
        slots = dot_nt(slot_lane, both.astype(BF16)).astype(jnp.int32)
        frame, row = slots >> 4, slots & 15
        pixels = jnp.where(lane < 48, both, 0.0)
        source = jnp.concatenate([pixels, pc[s]], axis=0).astype(BF16)
        for a in range(3):
            t = frame + 2 - a
            place = jnp.where(t < FRAMES, row * 8 + (t & 1) * 4 + (t >> 1), -1)
            hit = jnp.where(sub.reshape(16, 8, 128) == place[None], 1.0, 0.0).reshape(128, 128)
            ct = cframe - a
            cplace = jnp.where(ct >= 0, crow * 8 + (ct & 1) * 4 + (ct >> 1), -1)
            chit = jnp.where(csub == cplace, 1.0, 0.0)
            placed = dot(jnp.concatenate([hit, chit], axis=1).astype(BF16), source)
            zs[a, 4 + s * 16 : 4 + (s + 1) * 16] = placed.reshape(16, 8, 128)
    line = recv_ref[j].astype(F32)
    both = jnp.concatenate([line, pltpu.roll(line, 64, 1)], axis=0)
    slots = dot_nt(slot_lane, both.astype(BF16)).astype(jnp.int32)
    goal = (slots >> 4) + 2 - valid
    place = jnp.where((goal >= 0) & (goal < 2), goal * 16 + (slots & 15), -1)
    hit = jnp.where(iota((4, 8, 128), 0) * 8 + iota((4, 8, 128), 1) == place[None], 1.0, 0.0)
    cgoal = iota((32, 32), 1) // 16 - valid
    cplace = jnp.where((cgoal >= 0) & (cgoal < 2), cgoal * 16 + iota((32, 32), 1) % 16, -1)
    chit = jnp.where(iota((32, 32), 0) == cplace, 1.0, 0.0)
    source = jnp.concatenate([jnp.where(lane < 48, both, 0.0), pc[j]], axis=0).astype(BF16)
    fresh = dot(jnp.concatenate([hit.reshape(32, 128), chit], axis=1).astype(BF16), source)
    new_pix_ref[...] = fresh[:, 0:48].astype(BF16)
    high = rows_all + 4
    for b in range(3):
        for a in range(3):
            q = (b * 3 + a) * 48
            xs[2 : high + 2, :, q : q + 48] = zs[a, 1 + b : high + 1 + b, :, 0:48]
    full = xs[4 : 4 + rows_all].reshape(rows_all * 8, 432).astype(BF16)
    base = j * 16 + 2
    first, second = xs[pl.ds(base, 11)], xs[pl.ds(base + 8, 11)]
    low = iota((11, 8, 432), 1) < 4
    own_even = jnp.where(low, first, pltpu.roll(second, 4, 1))
    own_odd = jnp.where(low, pltpu.roll(first, 4, 1), second)
    own = jnp.concatenate([own_even, own_odd], axis=0).reshape(176, 432).astype(BF16)
    s1 = jnp.zeros((8, 256), F32)
    s2 = jnp.zeros((8, 256), F32)
    for chunk in range(8):
        weight = band_ref[:, chunk * 256 : (chunk + 1) * 256]
        out = dot(full, weight).astype(BF16).astype(F32).reshape(rows_all, 8, 256)
        s1 = s1 + jnp.sum(out, axis=0)
        s2 = s2 + jnp.sum(out * out, axis=0)
        mine = dot(own, weight).astype(BF16).astype(F32).reshape(2, 11, 8, 256)
        for i in range(2):
            stem[:, 2 * chunk + i] = mine[:, :, :, i * 128 : (i + 1) * 128]
    s1 = s1[:, 0:128] + s1[:, 128:256]
    s2 = s2[:, 0:128] + s2[:, 128:256]
    same = jnp.where(iota((128, 128), 0) // 4 == iota((128, 128), 1) // 4, 1.0, 0.0)
    count = rows_all * 16 * 4
    exact = functools.partial(
        jnp.dot, preferred_element_type=F32, precision=lax.Precision.HIGHEST
    )
    mean = exact(s1, same) / count
    inv = lax.rsqrt(exact(s2, same) / count - mean * mean + EPSILON)
    low8 = iota((8, 128), 0) < 4
    scale = inv * gain_ref[...]
    shift = bias_ref[...] - mean * scale
    scales = (
        jnp.where(low8, scale, pltpu.roll(scale, 4, 0)),
        jnp.where(low8, pltpu.roll(scale, 4, 0), scale),
    )
    shifts = (
        jnp.where(low8, shift, pltpu.roll(shift, 4, 0)),
        jnp.where(low8, pltpu.roll(shift, 4, 0), shift),
    )
    cache[...] = jnp.zeros(cache.shape, F32)
    rcache[...] = jnp.zeros(rcache.shape, F32)
    has_above = jnp.where(j > 0, 1.0, 0.0)
    has_below = jnp.where(j < strips - 1, 1.0, 0.0)
    for f in range(2):
        cache[f, 0:32] = below_ref[f * 32 : f * 32 + 32].astype(F32) * has_above
        cache[f, 32:288] = act_cache_ref[f].reshape(256, 128).astype(F32)
        cache[f, 288:304] = above_ref[f * 16 : f * 16 + 16].astype(F32) * has_below
        rcache[f, 0:16] = below_ref[64 + f * 16 : 80 + f * 16].astype(F32) * has_above
        rcache[f, 16:272] = res_cache_ref[f].reshape(256, 128).astype(F32)
    half = iota((11, 8, 128), 1) // 4
    line_of = j * 16 + iota((11, 8, 128), 0) - 2 + 8 * half
    inside = jnp.where((line_of >= 0) & (line_of < rows_all), 1.0, 0.0)
    start = iota((11, 8, 128), 1) % 4 == 0
    act3[0] = jnp.zeros(act3.shape[1:], BF16)
    act3[17] = jnp.zeros(act3.shape[1:], BF16)

    def activate(w, carry):
        pair = []
        for p in range(2):
            v = stem[p, w] * scales[p] + shifts[p]
            v = (v / (1.0 + jnp.exp(-v)) * inside).astype(BF16).astype(F32)
            act[p, w] = v
            pair.append(v)
        even, odd = pair
        olds = []
        for f in range(2):
            olds.append(
                jnp.stack([cache[f, pl.ds(y * 16 + w, 8, stride=32)] for y in range(11)], axis=0)
            )
        even_late = jnp.where(start, olds[0], pltpu.roll(even, 1, 1))
        odd_late = jnp.where(start, olds[1], pltpu.roll(odd, 1, 1))
        taps = ((even_late, odd_late), (odd_late, even), (even, odd))
        for a in range(3):
            act3[w + 1, :, :, a * 128 : (a + 1) * 128] = jnp.concatenate(taps[a], axis=1).astype(BF16)
        return carry

    lax.fori_loop(0, 16, activate, 0)
    weights = [
        jnp.concatenate([conv_ref[a, b, e] for a in range(3)], axis=0)
        for b in range(3)
        for e in range(3)
    ]
    weights = jnp.concatenate(weights, axis=0)
    keep = jnp.where((j == 0) & (iota((9, 8, 128), 0) == 0) & (iota((9, 8, 128), 1) < 4), 0.0, 1.0)
    for g in range(4):
        w0 = g * 4
        left = jnp.concatenate(
            [
                act3[w0 + e : w0 + e + 4, b : b + 9].reshape(576, 384)
                for b in range(3)
                for e in range(3)
            ],
            axis=1,
        )
        out = dot(left, weights).reshape(4, 9, 16, 128)
        for p in range(2):
            value = out[:, :, p * 8 : (p + 1) * 8] + stem[p, w0 : w0 + 4, 1:10]
            res[p, w0 : w0 + 4] = (value * keep).astype(BF16).astype(F32)
    begin = iota((9, 8, 128), 1) % 4 == 0
    res3[0] = jnp.zeros(res3.shape[1:], F32)

    def delay(w, carry):
        even, odd = res[0, w], res[1, w]
        olds = []
        for f in range(2):
            olds.append(
                jnp.stack([rcache[f, pl.ds(y * 16 + w, 8, stride=32)] for y in range(9)], axis=0)
            )
        res3[w + 1, :, :, 0:128] = jnp.where(begin, olds[0], pltpu.roll(even, 1, 1))
        res3[w + 1, :, :, 128:256] = jnp.where(begin, olds[1], pltpu.roll(odd, 1, 1))
        res3[w + 1, :, :, 256:384] = even
        return carry

    lax.fori_loop(0, 16, delay, 0)
    total = jnp.zeros((256, 256), F32)
    for b in range(3):
        for e in range(3):
            left = jnp.concatenate(
                [res3[2 * k + e, 2 * i + b] for k in range(8) for i in range(4)], axis=0
            ).astype(BF16)
            right = jnp.concatenate([down_ref[a, b, e] for a in range(3)], axis=0)
            total = total + dot(left, right)
    live = 2 * (iota((256, 256), 0) % 4) < valid
    total = jnp.where(live, total, 0.0)
    for o in range(2):
        lat[o] = total[:, o * 128 : (o + 1) * 128]
    for t in range(4):
        for h in range(2):
            for i in range(4):
                for o in range(2):
                    block = lat[o, pl.ds(i * 8 + h * 4 + t, 8, stride=32)]
                    lat_ref[t, h * 4 + i, :, o * 128 : (o + 1) * 128] = block.astype(BF16)
    act_rows = act.reshape(2 * 16 * 11 * 8, 128)
    res_rows = res.reshape(2 * 16 * 9 * 8, 128)
    for i in range(2):
        g = valid + i
        f = jnp.maximum(g - 2, 0)
        parity, step = f & 1, f >> 1
        old = g < 2
        for y in range(16):
            h, y1 = y // 8, y % 8
            at = parity * (16 * 88) + (y1 + 2) * 8 + h * 4 + step
            block = act_rows[pl.ds(at, 16, stride=88)]
            new_act_ref[i, y] = jnp.where(old, act_cache_ref[1, y].astype(F32), block).astype(BF16)
            at = parity * (16 * 72) + (y1 + 1) * 8 + h * 4 + step
            block = res_rows[pl.ds(at, 16, stride=72)]
            new_res_ref[i, y] = jnp.where(old, res_cache_ref[1, y].astype(F32), block).astype(BF16)


def partner(value, axis, stride):
    pairs = [(source, source ^ stride) for source in range(lax.axis_size(axis))]
    return lax.ppermute(value, axis, pairs)


def shifted(value, axis, by):
    size = lax.axis_size(axis)
    return lax.ppermute(value, axis, [(i, (i + by) % size) for i in range(size)])


def body(
    loader_rows,
    load_owner,
    load_slot,
    valid_frames,
    next_owner,
    pixel_cache,
    act_cache,
    res_cache,
    stem_weight,
    norm_gain,
    norm_bias,
    conv_weight,
    down_weight,
):
    streams = lax.axis_size("stream")
    strips = lax.axis_size("strip")
    stream_pos = lax.axis_index("stream")
    sections = streams.bit_length() - 1
    fill = loader_rows.shape[1]
    per = fill // streams
    pix = pixel_cache[0].reshape(32, 48)
    acts, ress = act_cache[0], res_cache[0]
    below = jnp.concatenate([acts[:, 14:16].reshape(64, 128), ress[:, 15].reshape(32, 128)], 0)
    above = acts[:, 0].reshape(32, 128)
    below = shifted(below, "strip", 1)
    above = shifted(above, "strip", -1)
    others = [shifted(pix, "strip", k) for k in range(1, strips)]
    lines = pl.pallas_call(
        functools.partial(sort_kernel, streams),
        out_shape=jax.ShapeDtypeStruct((fill // 2, 128), BF16),
        in_specs=[VM] * 3,
        out_specs=VM,
        scratch_shapes=[pltpu.VMEM((fill, 128), F32)],
    )(loader_rows[0], load_owner, load_slot)
    lines = lines.reshape(1, streams, per // 2, 128)
    lines = jnp.broadcast_to(lines, (strips, streams, per // 2, 128))
    lines = lines.reshape(strips * streams, per // 2, 128)
    recv = lax.all_to_all(lines, ("strip", "stream"), 0, 0, tiled=True)
    recv = recv.reshape(strips, fill // 2, 128)
    band = pl.pallas_call(
        band_kernel,
        out_shape=jax.ShapeDtypeStruct((432, 2048), BF16),
        in_specs=[VM],
        out_specs=VM,
    )(stem_weight.reshape(81, 128).astype(F32))
    rows_all = strips * 16
    latent, new_pix, new_act, new_res = pl.pallas_call(
        functools.partial(main_kernel, strips),
        out_shape=(
            jax.ShapeDtypeStruct((4, 8, 8, 256), BF16),
            jax.ShapeDtypeStruct((32, 48), BF16),
            jax.ShapeDtypeStruct((2, 16, 16, 128), BF16),
            jax.ShapeDtypeStruct((2, 16, 16, 128), BF16),
        ),
        in_specs=[SM] + [VM] * 14,
        out_specs=(VM,) * 4,
        scratch_shapes=[
            pltpu.VMEM((strips, 32, 128), F32),
            pltpu.VMEM((3, rows_all + 8, 8, 128), F32),
            pltpu.VMEM((rows_all + 8, 8, 432), F32),
            pltpu.VMEM((2, 16, 11, 8, 128), F32),
            pltpu.VMEM((2, 16, 11, 8, 128), F32),
            pltpu.VMEM((2, 16, 9, 8, 128), F32),
            pltpu.VMEM((2, 416, 128), F32),
            pltpu.VMEM((2, 384, 128), F32),
            pltpu.VMEM((18, 11, 16, 384), BF16),
            pltpu.VMEM((17, 9, 8, 384), F32),
            pltpu.VMEM((2, 256, 128), F32),
        ],
        compiler_params=pltpu.CompilerParams(vmem_limit_bytes=48 * 1024 * 1024),
    )(
        valid_frames,
        recv,
        pix,
        *others,
        band,
        norm_gain.reshape(1, 128),
        norm_bias.reshape(1, 128),
        conv_weight,
        down_weight,
        acts,
        ress,
        below,
        above,
    )
    carried = (new_pix, new_act, new_res)
    target = next_owner[0]
    for bit in range(sections):
        other = [partner(v, "stream", 1 << bit) for v in carried + (target,)]
        mine = (target >> bit) & 1 == (stream_pos >> bit) & 1
        carried = tuple(jnp.where(mine, a, b) for a, b in zip(carried, other[:-1]))
        target = jnp.where(mine, target, other[-1])
    new_pix, new_act, new_res = carried
    return (latent[None], new_pix.reshape(1, 2, 16, 48), new_act[None], new_res[None])


def solution(mesh):
    in_specs = (
        P("stream", "strip", None),
        P("stream", "strip"),
        P("stream", "strip"),
        P("stream"),
        P("stream"),
        P("stream", None, "strip", None),
        P("stream", None, "strip", None, None),
        P("stream", None, "strip", None, None),
        P(),
        P(),
        P(),
        P(),
        P(),
    )
    out_specs = (
        P("stream", None, "strip", None, None),
        P("stream", None, "strip", None),
        P("stream", None, "strip", None, None),
        P("stream", None, "strip", None, None),
    )
    return jax.shard_map(body, mesh=mesh, in_specs=in_specs, out_specs=out_specs, check_vma=False)
```

```python
import functools

import jax
import jax.numpy as jnp
from jax import lax
from jax.experimental import pallas as pl
from jax.experimental.pallas import tpu as pltpu
from jax.sharding import PartitionSpec as P

FRAMES = 8
GROUPS = 32
EPSILON = 1e-06
F32 = jnp.float32
BF16 = jnp.bfloat16
VM = pl.BlockSpec(memory_space=pltpu.VMEM)
SM = pl.BlockSpec(memory_space=pltpu.SMEM)


def iota(shape, axis):
    return lax.broadcasted_iota(jnp.int32, shape, axis)


def dot(a, b):
    return jnp.dot(a, b, preferred_element_type=F32)


def dot_nt(a, b):
    return lax.dot_general(a, b, (((1,), (1,)), ((), ())), preferred_element_type=F32)


def sort_kernel(streams, cols_ref, owner_ref, slot_ref, out_ref, wide):
    width, fill = cols_ref.shape
    half_per = fill // streams // 2
    lines = fill // 2
    wide[...] = jnp.zeros(wide.shape, F32)
    pixels, slots = cols_ref[...].astype(F32), slot_ref[...].astype(F32)
    for side in range(2):
        at = side * 64
        wide[at : at + width, side * fill : (side + 1) * fill] = pixels
        wide[at + width : at + width + 1, side * fill : (side + 1) * fill] = slots
    owner = owner_ref[...]
    hot = jnp.where(iota((streams, fill), 0) == owner, 1.0, 0.0)
    upper = jnp.where(iota((fill, fill), 0) <= iota((fill, fill), 1), 1.0, 0.0).astype(BF16)
    running = dot(hot.astype(BF16), upper)
    rank = jnp.sum(hot * running, axis=0, keepdims=True).astype(jnp.int32) - 1
    half = rank // half_per
    line = owner * half_per + rank - half * half_per
    line = jnp.concatenate([jnp.where(half == side, line, -1) for side in range(2)], axis=1)
    pick = jnp.where(iota((lines, 2 * fill), 0) == jnp.broadcast_to(line, (lines, 2 * fill)), 1.0, 0.0)
    out = dot_nt(pick.astype(BF16), wide[...].astype(BF16)).astype(BF16)
    if len(out_ref.shape) == 2:
        out_ref[...] = out
    else:
        for strip in range(out_ref.shape[0]):
            out_ref[strip] = out.reshape(out_ref.shape[1:])


def pack_kernel(pix_ref, act_ref, res_ref, down_ref, up_ref, mid_ref):
    pix = jnp.concatenate(
        [pix_ref[...].reshape(32, 48).astype(F32), jnp.zeros((32, 80), F32)], axis=1
    ).astype(BF16)
    for f in range(2):
        down_ref[f * 32 : f * 32 + 32] = act_ref[f, 14:16].reshape(32, 128)
        down_ref[64 + f * 16 : 80 + f * 16] = res_ref[f, 15]
        up_ref[f * 16 : f * 16 + 16] = act_ref[f, 0]
    down_ref[96:128] = pix
    up_ref[32:64] = pix
    mid_ref[...] = pix


def band_kernel(sw_ref, out_ref, wide):
    wide[...] = jnp.zeros(wide.shape, F32)
    for tap in range(27):
        b, a, c = tap // 9, tap // 3 % 3, tap % 3
        for e in range(3):
            wide[tap, 16 + e : 17 + e] = sw_ref[a, b, e, c : c + 1].astype(F32)
    for w in range(16):
        block = wide[:, 17 - w : 33 - w].reshape(432, 128)
        out_ref[:, w * 128 : (w + 1) * 128] = block.astype(BF16)


def stem_kernel(
    strips,
    valid_ref,
    target_ref,
    recv_ref,
    pix_ref,
    below_ref,
    above_ref,
    mid_ref,
    band_ref,
    gain_ref,
    bias_ref,
    act_cache_ref,
    pay_ref,
    act3,
    stem_ref,
    pc,
    zs,
    xs,
    stem,
    act,
    cache,
):
    j = lax.axis_index("strip")
    valid = valid_ref[0]
    rows_all = strips * 16
    pc[...] = jnp.zeros(pc.shape, F32)
    pc[j, :, 0:48] = pix_ref[...].reshape(32, 48).astype(F32)
    pc[lax.rem(j + strips - 1, strips)] = below_ref[96:128].astype(F32)
    pc[lax.rem(j + 1, strips)] = above_ref[32:64].astype(F32)
    pc[lax.rem(j + 2, strips)] = mid_ref[...].astype(F32)
    zs[...] = jnp.zeros(zs.shape, F32)
    lane = iota((128, 128), 1)
    sub = iota((128, 128), 0)
    slot_lane = jnp.where(iota((8, 128), 1) == 48, 1.0, 0.0).astype(BF16)
    crow, cframe = iota((128, 32), 1) % 16, iota((128, 32), 1) // 16
    csub = iota((128, 32), 0)
    for s in range(strips):
        line = recv_ref[s].astype(F32)
        both = jnp.concatenate([line, pltpu.roll(line, 64, 1)], axis=0)
        slots = dot_nt(slot_lane, both.astype(BF16)).astype(jnp.int32)
        frame, row = slots >> 4, slots & 15
        pixels = jnp.where(lane < 48, both, 0.0)
        source = jnp.concatenate([pixels, pc[s]], axis=0).astype(BF16)
        for a in range(3):
            t = frame + 2 - a
            place = jnp.where(t < FRAMES, row * 8 + (t & 1) * 4 + (t >> 1), -1)
            hit = jnp.where(sub.reshape(16, 8, 128) == place[None], 1.0, 0.0).reshape(128, 128)
            ct = cframe - a
            cplace = jnp.where(ct >= 0, crow * 8 + (ct & 1) * 4 + (ct >> 1), -1)
            chit = jnp.where(csub == cplace, 1.0, 0.0)
            placed = dot(jnp.concatenate([hit, chit], axis=1).astype(BF16), source)
            zs[a, 4 + s * 16 : 4 + (s + 1) * 16] = placed.reshape(16, 8, 128)
    line = recv_ref[j].astype(F32)
    both = jnp.concatenate([line, pltpu.roll(line, 64, 1)], axis=0)
    slots = dot_nt(slot_lane, both.astype(BF16)).astype(jnp.int32)
    goal = (slots >> 4) + 2 - valid
    place = jnp.where((goal >= 0) & (goal < 2), goal * 16 + (slots & 15), -1)
    hit = jnp.where(iota((4, 8, 128), 0) * 8 + iota((4, 8, 128), 1) == place[None], 1.0, 0.0)
    cgoal = iota((32, 32), 1) // 16 - valid
    cplace = jnp.where((cgoal >= 0) & (cgoal < 2), cgoal * 16 + iota((32, 32), 1) % 16, -1)
    chit = jnp.where(iota((32, 32), 0) == cplace, 1.0, 0.0)
    source = jnp.concatenate([jnp.where(lane < 48, both, 0.0), pc[j]], axis=0).astype(BF16)
    fresh = dot(jnp.concatenate([hit.reshape(32, 128), chit], axis=1).astype(BF16), source)
    target = jnp.broadcast_to(target_ref[0].astype(F32), (16, 128))
    pay_ref[0:16] = target.astype(BF16)
    pay_ref[16:48] = fresh.astype(BF16)
    high = rows_all + 4
    for b in range(3):
        for a in range(3):
            q = (b * 3 + a) * 48
            xs[2 : high + 2, :, q : q + 48] = zs[a, 1 + b : high + 1 + b, :, 0:48]
    full = xs[4 : 4 + rows_all].reshape(rows_all * 8, 432).astype(BF16)
    base = j * 16 + 2
    first, second = xs[pl.ds(base, 11)], xs[pl.ds(base + 8, 11)]
    low = iota((11, 8, 432), 1) < 4
    own_even = jnp.where(low, first, pltpu.roll(second, 4, 1))
    own_odd = jnp.where(low, pltpu.roll(first, 4, 1), second)
    own = jnp.concatenate([own_even, own_odd], axis=0).reshape(176, 432).astype(BF16)
    s1 = jnp.zeros((8, 256), F32)
    s2 = jnp.zeros((8, 256), F32)
    for chunk in range(8):
        weight = band_ref[:, chunk * 256 : (chunk + 1) * 256]
        out = dot(full, weight).astype(BF16).astype(F32).reshape(rows_all, 8, 256)
        s1 = s1 + jnp.sum(out, axis=0)
        s2 = s2 + jnp.sum(out * out, axis=0)
        mine = dot(own, weight).astype(BF16).astype(F32).reshape(2, 11, 8, 256)
        for i in range(2):
            part = mine[:, :, :, i * 128 : (i + 1) * 128]
            stem[:, 2 * chunk + i] = part
            stem_ref[2 * chunk + i] = jnp.concatenate([part[0, 1:10], part[1, 1:10]], axis=1).astype(BF16)
    s1 = s1[:, 0:128] + s1[:, 128:256]
    s2 = s2[:, 0:128] + s2[:, 128:256]
    same = jnp.where(iota((128, 128), 0) // 4 == iota((128, 128), 1) // 4, 1.0, 0.0)
    count = rows_all * 16 * 4
    exact = functools.partial(
        jnp.dot, preferred_element_type=F32, precision=lax.Precision.HIGHEST
    )
    mean = exact(s1, same) / count
    inv = lax.rsqrt(exact(s2, same) / count - mean * mean + EPSILON)
    low8 = iota((8, 128), 0) < 4
    scale = inv * gain_ref[...]
    shift = bias_ref[...] - mean * scale
    scales = (
        jnp.where(low8, scale, pltpu.roll(scale, 4, 0)),
        jnp.where(low8, pltpu.roll(scale, 4, 0), scale),
    )
    shifts = (
        jnp.where(low8, shift, pltpu.roll(shift, 4, 0)),
        jnp.where(low8, pltpu.roll(shift, 4, 0), shift),
    )
    cache[...] = jnp.zeros(cache.shape, F32)
    has_above = jnp.where(j > 0, 1.0, 0.0)
    has_below = jnp.where(j < strips - 1, 1.0, 0.0)
    for f in range(2):
        cache[f, 0:32] = below_ref[f * 32 : f * 32 + 32].astype(F32) * has_above
        cache[f, 32:288] = act_cache_ref[f].reshape(256, 128).astype(F32)
        cache[f, 288:304] = above_ref[f * 16 : f * 16 + 16].astype(F32) * has_below
    half = iota((11, 8, 128), 1) // 4
    line_of = j * 16 + iota((11, 8, 128), 0) - 2 + 8 * half
    inside = jnp.where((line_of >= 0) & (line_of < rows_all), 1.0, 0.0)
    start = iota((11, 8, 128), 1) % 4 == 0
    act3[0] = jnp.zeros(act3.shape[1:], BF16)
    act3[17] = jnp.zeros(act3.shape[1:], BF16)

    def activate(w, carry):
        pair = []
        for p in range(2):
            v = stem[p, w] * scales[p] + shifts[p]
            v = (v / (1.0 + jnp.exp(-v)) * inside).astype(BF16).astype(F32)
            act[p, w] = v
            pair.append(v)
        even, odd = pair
        olds = []
        for f in range(2):
            olds.append(
                jnp.stack([cache[f, pl.ds(y * 16 + w, 8, stride=32)] for y in range(11)], axis=0)
            )
        even_late = jnp.where(start, olds[0], pltpu.roll(even, 1, 1))
        odd_late = jnp.where(start, olds[1], pltpu.roll(odd, 1, 1))
        taps = ((even_late, odd_late), (odd_late, even), (even, odd))
        for a in range(3):
            act3[w + 1, :, :, a * 128 : (a + 1) * 128] = jnp.concatenate(taps[a], axis=1).astype(BF16)
        return carry

    lax.fori_loop(0, 16, activate, 0)
    act_rows = act.reshape(2 * 16 * 11 * 8, 128)
    for i in range(2):
        g = valid + i
        f = jnp.maximum(g - 2, 0)
        for y in range(16):
            at = (f & 1) * (16 * 88) + (y % 8 + 2) * 8 + y // 8 * 4 + (f >> 1)
            block = act_rows[pl.ds(at, 16, stride=88)]
            block = jnp.where(g < 2, act_cache_ref[1, y].astype(F32), block)
            to = 48 + i * 256 + y * 16
            pay_ref[to : to + 16] = block.astype(BF16)


def conv_rows(first, last, act3_ref, stem_ref, conv_ref):
    j = lax.axis_index("strip")
    count = last - first
    weights = jnp.concatenate(
        [conv_ref[a, b, e] for b in range(3) for e in range(3) for a in range(3)], axis=0
    )
    line = first + iota((count, 16, 128), 0)
    outside = (j == 0) & (line == 0) & (iota((count, 16, 128), 1) % 8 < 4)
    keep = jnp.where(outside, 0.0, 1.0)
    groups = []
    for w0 in range(0, 16, 4):
        left = jnp.concatenate(
            [
                act3_ref[w0 + e : w0 + e + 4, first + b : last + b].reshape(4 * count * 16, 384)
                for b in range(3)
                for e in range(3)
            ],
            axis=1,
        )
        out = dot(left, weights).reshape(4, count, 16, 128)
        out = out + stem_ref[w0 : w0 + 4, first:last].astype(F32)
        groups.append((out * keep).astype(BF16))
    return groups


def conv_first_kernel(split, act3_ref, stem_ref, conv_ref, out_ref):
    for g, value in enumerate(conv_rows(0, split, act3_ref, stem_ref, conv_ref)):
        out_ref[g * 4 : g * 4 + 4] = value


def conv_second_kernel(
    split, valid_ref, act3_ref, stem_ref, conv_ref, part_ref, res_cache_ref, out_ref, pay_ref, res
):
    valid = valid_ref[0]
    part = part_ref[...].astype(F32)
    for p in range(2):
        res[p, :, 0:split] = part[:, :, p * 8 : p * 8 + 8]
    for g, value in enumerate(conv_rows(split, 9, act3_ref, stem_ref, conv_ref)):
        out_ref[g * 4 : g * 4 + 4] = value
        for p in range(2):
            res[p, g * 4 : g * 4 + 4, split:9] = value.astype(F32)[:, :, p * 8 : p * 8 + 8]
    res_rows = res.reshape(2 * 16 * 9 * 8, 128)
    for i in range(2):
        g = valid + i
        f = jnp.maximum(g - 2, 0)
        for y in range(16):
            at = (f & 1) * (16 * 72) + (y % 8 + 1) * 8 + y // 8 * 4 + (f >> 1)
            block = res_rows[pl.ds(at, 16, stride=72)]
            block = jnp.where(g < 2, res_cache_ref[1, y].astype(F32), block)
            to = i * 256 + y * 16
            pay_ref[to : to + 16] = block.astype(BF16)


def down_kernel(
    split, valid_ref, part_ref, rest_ref, down_ref, res_cache_ref, below_ref, lat_ref, rcache, res3, lat
):
    j = lax.axis_index("strip")
    valid = valid_ref[0]
    rcache[...] = jnp.zeros(rcache.shape, F32)
    has_above = jnp.where(j > 0, 1.0, 0.0)
    for f in range(2):
        rcache[f, 0:16] = below_ref[64 + f * 16 : 80 + f * 16].astype(F32) * has_above
        rcache[f, 16:272] = res_cache_ref[f].reshape(256, 128).astype(F32)
    begin = iota((9, 8, 128), 1) % 4 == 0
    res3[0] = jnp.zeros(res3.shape[1:], F32)

    def delay(w, carry):
        both = jnp.concatenate([part_ref[w], rest_ref[w]], axis=0).astype(F32)
        even, odd = both[:, 0:8], both[:, 8:16]
        olds = []
        for f in range(2):
            olds.append(
                jnp.stack([rcache[f, pl.ds(y * 16 + w, 8, stride=32)] for y in range(9)], axis=0)
            )
        res3[w + 1, :, :, 0:128] = jnp.where(begin, olds[0], pltpu.roll(even, 1, 1))
        res3[w + 1, :, :, 128:256] = jnp.where(begin, olds[1], pltpu.roll(odd, 1, 1))
        res3[w + 1, :, :, 256:384] = even
        return carry

    lax.fori_loop(0, 16, delay, 0)
    total = jnp.zeros((256, 256), F32)
    for b in range(3):
        for e in range(3):
            left = jnp.concatenate(
                [res3[2 * k + e, 2 * i + b] for k in range(8) for i in range(4)], axis=0
            ).astype(BF16)
            right = jnp.concatenate([down_ref[a, b, e] for a in range(3)], axis=0)
            total = total + dot(left, right)
    live = 2 * (iota((256, 256), 0) % 4) < valid
    total = jnp.where(live, total, 0.0)
    for o in range(2):
        lat[o] = total[:, o * 128 : (o + 1) * 128]
    for t in range(4):
        for h in range(2):
            for i in range(4):
                for o in range(2):
                    block = lat[o, pl.ds(i * 8 + h * 4 + t, 8, stride=32)]
                    lat_ref[t, h * 4 + i, :, o * 128 : (o + 1) * 128] = block.astype(BF16)


def partner(value, axis, stride):
    pairs = [(source, source ^ stride) for source in range(lax.axis_size(axis))]
    return lax.ppermute(value, axis, pairs)


def shifted(value, axis, by):
    size = lax.axis_size(axis)
    return lax.ppermute(value, axis, [(i, (i + by) % size) for i in range(size)])


def body(
    loader_rows,
    load_owner,
    load_slot,
    valid_frames,
    next_owner,
    pixel_cache,
    act_cache,
    res_cache,
    stem_weight,
    norm_gain,
    norm_bias,
    conv_weight,
    down_weight,
):
    streams = lax.axis_size("stream")
    strips = lax.axis_size("strip")
    stream_pos = lax.axis_index("stream")
    sections = streams.bit_length() - 1
    fill = loader_rows.shape[1]
    per = fill // streams
    pix, acts, ress = pixel_cache[0], act_cache[0], res_cache[0]
    mega = 1024 * 1024
    half_per = fill // streams // 2
    direct = half_per % 8 == 0
    line_shape = (strips, streams, half_per, 128) if direct else (fill // 2, 128)
    lines = pl.pallas_call(
        functools.partial(sort_kernel, streams),
        out_shape=jax.ShapeDtypeStruct(line_shape, BF16),
        in_specs=[VM] * 3,
        out_specs=VM,
        scratch_shapes=[pltpu.VMEM((128, 2 * fill), F32)],
    )(loader_rows[0].T, load_owner, load_slot)
    if not direct:
        lines = lines.reshape(1, streams, half_per, 128)
        lines = jnp.broadcast_to(lines, (strips, streams, half_per, 128))
    lines = lines.reshape(strips * streams, half_per, 128)
    recv = lax.all_to_all(lines, ("strip", "stream"), 0, 0, tiled=True)
    recv = recv.reshape(strips, fill // 2, 128)
    below, above, mid = pl.pallas_call(
        pack_kernel,
        out_shape=(
            jax.ShapeDtypeStruct((128, 128), BF16),
            jax.ShapeDtypeStruct((64, 128), BF16),
            jax.ShapeDtypeStruct((32, 128), BF16),
        ),
        in_specs=[VM] * 3,
        out_specs=(VM,) * 3,
    )(pix, acts, ress)
    below = shifted(below, "strip", 1)
    above = shifted(above, "strip", -1)
    mid = shifted(mid, "strip", 2)
    band = pl.pallas_call(
        band_kernel,
        out_shape=jax.ShapeDtypeStruct((432, 2048), BF16),
        in_specs=[VM],
        out_specs=VM,
        scratch_shapes=[pltpu.VMEM((27, 40, 128), F32)],
    )(stem_weight)
    rows_all = strips * 16
    first, act3, stem = pl.pallas_call(
        functools.partial(stem_kernel, strips),
        out_shape=(
            jax.ShapeDtypeStruct((560, 128), BF16),
            jax.ShapeDtypeStruct((18, 11, 16, 384), BF16),
            jax.ShapeDtypeStruct((16, 9, 16, 128), BF16),
        ),
        in_specs=[SM] * 2 + [VM] * 9,
        out_specs=(VM,) * 3,
        scratch_shapes=[
            pltpu.VMEM((strips, 32, 128), F32),
            pltpu.VMEM((3, rows_all + 8, 8, 128), F32),
            pltpu.VMEM((rows_all + 8, 8, 432), F32),
            pltpu.VMEM((2, 16, 11, 8, 128), F32),
            pltpu.VMEM((2, 16, 11, 8, 128), F32),
            pltpu.VMEM((2, 416, 128), F32),
        ],
        compiler_params=pltpu.CompilerParams(vmem_limit_bytes=24 * mega),
    )(
        valid_frames,
        next_owner,
        recv,
        pix,
        below,
        above,
        mid,
        band,
        norm_gain.reshape(1, 128),
        norm_bias.reshape(1, 128),
        acts,
    )
    split = 5
    cost = pl.CostEstimate(flops=2 * 10**9, bytes_accessed=4 * mega, transcendentals=0)
    part = pl.pallas_call(
        functools.partial(conv_first_kernel, split),
        out_shape=jax.ShapeDtypeStruct((16, split, 16, 128), BF16),
        in_specs=[VM] * 3,
        out_specs=VM,
        compiler_params=pltpu.CompilerParams(vmem_limit_bytes=24 * mega),
        cost_estimate=cost,
    )(act3, stem, conv_weight)
    rest, second = pl.pallas_call(
        functools.partial(conv_second_kernel, split),
        out_shape=(
            jax.ShapeDtypeStruct((16, 9 - split, 16, 128), BF16),
            jax.ShapeDtypeStruct((512, 128), BF16),
        ),
        in_specs=[SM] + [VM] * 5,
        out_specs=(VM,) * 2,
        scratch_shapes=[pltpu.VMEM((2, 16, 9, 8, 128), F32)],
        compiler_params=pltpu.CompilerParams(vmem_limit_bytes=24 * mega),
        cost_estimate=cost,
    )(valid_frames, act3, stem, conv_weight, part, ress)
    latent = pl.pallas_call(
        functools.partial(down_kernel, split),
        out_shape=jax.ShapeDtypeStruct((4, 8, 8, 256), BF16),
        in_specs=[SM] + [VM] * 5,
        out_specs=VM,
        scratch_shapes=[
            pltpu.VMEM((2, 384, 128), F32),
            pltpu.VMEM((17, 9, 8, 384), F32),
            pltpu.VMEM((2, 256, 128), F32),
        ],
        compiler_params=pltpu.CompilerParams(vmem_limit_bytes=24 * mega),
        cost_estimate=cost,
    )(valid_frames, part, rest, down_weight, ress, below)
    for bit in range(sections):
        mine = (first[0:1].astype(jnp.int32) >> bit) & 1 == (stream_pos >> bit) & 1
        first, second = (
            jnp.where(mine, v, partner(v, "stream", 1 << bit)) for v in (first, second)
        )
    new_pix = first[16:48, 0:48].reshape(1, 2, 16, 48)
    new_act = first[48:].reshape(1, 2, 16, 16, 128)
    return (latent[None], new_pix, new_act, second.reshape(1, 2, 16, 16, 128))


def solution(mesh):
    in_specs = (
        P("stream", "strip", None),
        P("stream", "strip"),
        P("stream", "strip"),
        P("stream"),
        P("stream"),
        P("stream", None, "strip", None),
        P("stream", None, "strip", None, None),
        P("stream", None, "strip", None, None),
        P(),
        P(),
        P(),
        P(),
        P(),
    )
    out_specs = (
        P("stream", None, "strip", None, None),
        P("stream", None, "strip", None),
        P("stream", None, "strip", None, None),
        P("stream", None, "strip", None, None),
    )
    return jax.shard_map(body, mesh=mesh, in_specs=in_specs, out_specs=out_specs, check_vma=False)
```

```python
import functools

import jax
import jax.numpy as jnp
from jax import lax
from jax.experimental import pallas as pl
from jax.experimental.pallas import tpu as pltpu
from jax.sharding import PartitionSpec as P

FRAMES = 8
GROUPS = 32
EPSILON = 1e-06
F32 = jnp.float32
BF16 = jnp.bfloat16
VM = pl.BlockSpec(memory_space=pltpu.VMEM)
ANY = pl.BlockSpec(memory_space=pl.ANY)


def iota(shape, axis):
    return lax.broadcasted_iota(jnp.int32, shape, axis)


def whole(scalars_ref, which):
    row = scalars_ref[...].astype(F32).reshape(1, 128)
    return jnp.sum(jnp.where(iota((1, 128), 1) == which, row, 0.0)).astype(jnp.int32)


def dot(a, b):
    return jnp.dot(a, b, preferred_element_type=F32)


def dot_nt(a, b):
    return lax.dot_general(a, b, (((1,), (1,)), ((), ())), preferred_element_type=F32)


def sort_kernel(streams, cols_ref, owner_ref, slot_ref, out_ref, wide):
    width, fill = cols_ref.shape
    half_per = fill // streams // 2
    lines = fill // 2
    wide[...] = jnp.zeros(wide.shape, F32)
    pixels, slots = cols_ref[...].astype(F32), slot_ref[...].astype(F32)
    for side in range(2):
        at = side * 64
        wide[at : at + width, side * fill : (side + 1) * fill] = pixels
        wide[at + width : at + width + 1, side * fill : (side + 1) * fill] = slots
    owner = owner_ref[...]
    hot = jnp.where(iota((streams, fill), 0) == owner, 1.0, 0.0)
    upper = jnp.where(iota((fill, fill), 0) <= iota((fill, fill), 1), 1.0, 0.0).astype(BF16)
    running = dot(hot.astype(BF16), upper)
    rank = jnp.sum(hot * running, axis=0, keepdims=True).astype(jnp.int32) - 1
    half = rank // half_per
    line = owner * half_per + rank - half * half_per
    line = jnp.concatenate([jnp.where(half == side, line, -1) for side in range(2)], axis=1)
    pick = jnp.where(iota((lines, 2 * fill), 0) == jnp.broadcast_to(line, (lines, 2 * fill)), 1.0, 0.0)
    out = dot_nt(pick.astype(BF16), wide[...].astype(BF16)).astype(BF16)
    if len(out_ref.shape) == 2:
        out_ref[...] = out
    else:
        for strip in range(out_ref.shape[0]):
            out_ref[strip] = out.reshape(out_ref.shape[1:])


def pack_kernel(after_ref, pix_ref, sw_ref, act_ref, res_ref, down_ref, up_ref, mid_ref, sw, sems):
    del after_ref
    copies = []
    for f in range(2):
        copies.append((act_ref.at[f, 14:16], down_ref.at[2 * f : 2 * f + 2]))
        copies.append((res_ref.at[f, 15:16], down_ref.at[4 + f : 5 + f]))
        copies.append((act_ref.at[f, 0:1], up_ref.at[f : f + 1]))
    copies = [pltpu.make_async_copy(a, b, sems.at[i]) for i, (a, b) in enumerate(copies)]
    for copy in copies:
        copy.start()
    pix = pix_ref[...].reshape(32, 48).astype(F32)
    pix = jnp.concatenate([pix, jnp.zeros((32, 80), F32)], axis=1)
    pix = pix.astype(BF16).reshape(2, 16, 128)
    down_ref[6:8] = pix
    up_ref[2:4] = pix
    mid_ref[0:2] = pix
    sw[...] = jnp.zeros(sw.shape, F32)
    for k in range(2):
        for e in range(3):
            for a in range(3):
                for b in range(3):
                    at = 27 * (k + e) + 9 * a + 3 * b
                    sw[at : at + 3, k * 128 : k * 128 + 128] = sw_ref[a, b, e].astype(F32)
    for k in range(2):
        half = sw[:, k * 128 : k * 128 + 128].astype(BF16)
        mid_ref[2 + 8 * k : 10 + 8 * k] = half.reshape(8, 16, 128)
    for copy in copies:
        copy.wait()


def stem_kernel(
    strips,
    scalars_ref,
    gain_ref,
    bias_ref,
    recv_ref,
    pix_ref,
    old_ref,
    below_ref,
    above_ref,
    mid_ref,
    pay_ref,
    act3,
    stem_ref,
    pc,
    zs,
    xs,
    ys,
    stem,
    act,
    cache,
):
    j = lax.axis_index("strip")
    valid = whole(scalars_ref, 0)
    rows_all = strips * 16
    pc[j] = jnp.zeros((32, 128), F32)
    pc[j, :, 0:48] = pix_ref[...].reshape(32, 48).astype(F32)
    pc[lax.rem(j + strips - 1, strips)] = below_ref[6:8].reshape(32, 128).astype(F32)
    pc[lax.rem(j + 1, strips)] = above_ref[2:4].reshape(32, 128).astype(F32)
    pc[lax.rem(j + 2, strips)] = mid_ref[0:2].reshape(32, 128).astype(F32)
    zs[...] = jnp.zeros(zs.shape, F32)
    lane = iota((128, 128), 1)
    sub = iota((128, 128), 0)
    slot_lane = jnp.where(iota((8, 128), 1) == 48, 1.0, 0.0).astype(BF16)
    crow, cframe = iota((128, 32), 1) % 16, iota((128, 32), 1) // 16
    csub = iota((128, 32), 0)
    for s in range(strips):
        line = recv_ref[s].astype(F32)
        both = jnp.concatenate([line, pltpu.roll(line, 64, 1)], axis=0)
        slots = dot_nt(slot_lane, both.astype(BF16)).astype(jnp.int32)
        frame, row = slots >> 4, slots & 15
        pixels = jnp.where(lane < 48, both, 0.0)
        source = jnp.concatenate([pixels, pc[s]], axis=0).astype(BF16)
        for a in range(3):
            t = frame + 2 - a
            place = jnp.where(t < FRAMES, row * 8 + (t & 1) * 4 + (t >> 1), -1)
            hit = jnp.where(sub.reshape(16, 8, 128) == place[None], 1.0, 0.0).reshape(128, 128)
            ct = cframe - a
            cplace = jnp.where(ct >= 0, crow * 8 + (ct & 1) * 4 + (ct >> 1), -1)
            chit = jnp.where(csub == cplace, 1.0, 0.0)
            placed = dot(jnp.concatenate([hit, chit], axis=1).astype(BF16), source)
            zs[a, 4 + s * 16 : 4 + (s + 1) * 16] = placed.reshape(16, 8, 128)
    line = recv_ref[j].astype(F32)
    both = jnp.concatenate([line, pltpu.roll(line, 64, 1)], axis=0)
    slots = dot_nt(slot_lane, both.astype(BF16)).astype(jnp.int32)
    goal = (slots >> 4) + 2 - valid
    place = jnp.where((goal >= 0) & (goal < 2), goal * 16 + (slots & 15), -1)
    hit = jnp.where(iota((4, 8, 128), 0) * 8 + iota((4, 8, 128), 1) == place[None], 1.0, 0.0)
    cgoal = iota((32, 32), 1) // 16 - valid
    cplace = jnp.where((cgoal >= 0) & (cgoal < 2), cgoal * 16 + iota((32, 32), 1) % 16, -1)
    chit = jnp.where(iota((32, 32), 0) == cplace, 1.0, 0.0)
    source = jnp.concatenate([jnp.where(lane < 48, both, 0.0), pc[j]], axis=0).astype(BF16)
    fresh = dot(jnp.concatenate([hit.reshape(32, 128), chit], axis=1).astype(BF16), source)
    target = whole(scalars_ref, 1).astype(F32)
    pay_ref[0:16] = jnp.full((16, 128), target, F32).astype(BF16)
    pay_ref[16:48] = fresh.astype(BF16)
    high = rows_all + 4
    for b in range(3):
        for a in range(3):
            q = (b * 3 + a) * 48
            xs[2 : high + 2, :, q : q + 48] = zs[a, 1 + b : high + 1 + b, :, 0:48]
    lanes = iota((8, 1024), 1)
    pair, m = lanes >> 7, lanes & 127
    col = (m * 2428) >> 16
    tap = m - 27 * col
    a = (tap * 7282) >> 16
    b = ((tap - 9 * a) * 21846) >> 16
    c = tap - 9 * a - 3 * b
    w = 2 * pair - 1 + col
    source = jnp.where((m < 108) & (w >= 0) & (w < 16), (b * 3 + a) * 48 + c * 16 + w, -1)
    line = iota((54, 8, 1024), 0) * 8 + iota((54, 8, 1024), 1)
    spread = jnp.where(line == source[None], 1.0, 0.0).reshape(432, 1024).astype(BF16)
    patches = xs[2 : high + 2].reshape(high * 8, 432).astype(BF16)
    ys[...] = dot(patches, spread).reshape(high, 8, 1024)
    full = ys[2 : 2 + rows_all].reshape(rows_all * 8, 1024).astype(BF16)
    base = j * 16
    first, second = ys[pl.ds(base, 11)], ys[pl.ds(base + 8, 11)]
    low = iota((11, 8, 1024), 1) < 4
    own_even = jnp.where(low, first, pltpu.roll(second, 4, 1))
    own_odd = jnp.where(low, pltpu.roll(first, 4, 1), second)
    own = jnp.concatenate([own_even, own_odd], axis=0).reshape(176, 1024).astype(BF16)
    weight = jnp.concatenate(
        [mid_ref[2 + 8 * k : 10 + 8 * k].reshape(128, 128) for k in range(2)], axis=1
    )
    s1 = jnp.zeros((8, 256), F32)
    s2 = jnp.zeros((8, 256), F32)
    for chunk in range(8):
        out = dot(full[:, chunk * 128 : chunk * 128 + 128], weight).astype(BF16).astype(F32).reshape(rows_all, 8, 256)
        s1 = s1 + jnp.sum(out, axis=0)
        s2 = s2 + jnp.sum(out * out, axis=0)
        mine = dot(own[:, chunk * 128 : chunk * 128 + 128], weight).astype(BF16).astype(F32).reshape(2, 11, 8, 256)
        for i in range(2):
            part = mine[:, :, :, i * 128 : (i + 1) * 128]
            stem[:, 2 * chunk + i] = part
            stem_ref[2 * chunk + i] = jnp.concatenate([part[0, 1:10], part[1, 1:10]], axis=1).astype(BF16)
    s1 = s1[:, 0:128] + s1[:, 128:256]
    s2 = s2[:, 0:128] + s2[:, 128:256]
    same = jnp.where(iota((128, 128), 0) // 4 == iota((128, 128), 1) // 4, 1.0, 0.0)
    count = rows_all * 16 * 4
    exact = functools.partial(
        jnp.dot, preferred_element_type=F32, precision=lax.Precision.HIGHEST
    )
    mean = exact(s1, same) / count
    inv = lax.rsqrt(exact(s2, same) / count - mean * mean + EPSILON)
    low8 = iota((8, 128), 0) < 4
    scale = inv * gain_ref[...].reshape(1, 128)
    shift = bias_ref[...].reshape(1, 128) - mean * scale
    scales = (
        jnp.where(low8, scale, pltpu.roll(scale, 4, 0)),
        jnp.where(low8, pltpu.roll(scale, 4, 0), scale),
    )
    shifts = (
        jnp.where(low8, shift, pltpu.roll(shift, 4, 0)),
        jnp.where(low8, pltpu.roll(shift, 4, 0), shift),
    )
    has_above = jnp.where(j > 0, 1.0, 0.0)
    has_below = jnp.where(j < strips - 1, 1.0, 0.0)
    for f in range(2):
        cache[f, 304:416] = jnp.zeros((112, 128), F32)
        cache[f, 32:288] = old_ref[f].reshape(256, 128).astype(F32)
        cache[f, 0:32] = below_ref[2 * f : 2 * f + 2].reshape(32, 128).astype(F32) * has_above
        cache[f, 288:304] = above_ref[f].astype(F32) * has_below
    half = iota((11, 8, 128), 1) // 4
    line_of = j * 16 + iota((11, 8, 128), 0) - 2 + 8 * half
    inside = jnp.where((line_of >= 0) & (line_of < rows_all), 1.0, 0.0)
    start = iota((11, 8, 128), 1) % 4 == 0
    act3[0] = jnp.zeros(act3.shape[1:], BF16)
    act3[17] = jnp.zeros(act3.shape[1:], BF16)

    def activate(w, carry):
        pair = []
        for p in range(2):
            v = stem[p, w] * scales[p] + shifts[p]
            v = (v / (1.0 + jnp.exp(-v)) * inside).astype(BF16).astype(F32)
            act[p, w] = v
            pair.append(v)
        even, odd = pair
        olds = []
        for f in range(2):
            olds.append(
                jnp.stack([cache[f, pl.ds(y * 16 + w, 8, stride=32)] for y in range(11)], axis=0)
            )
        even_late = jnp.where(start, olds[0], pltpu.roll(even, 1, 1))
        odd_late = jnp.where(start, olds[1], pltpu.roll(odd, 1, 1))
        taps = ((even_late, odd_late), (odd_late, even), (even, odd))
        for a in range(3):
            act3[w + 1, :, :, a * 128 : (a + 1) * 128] = jnp.concatenate(taps[a], axis=1).astype(BF16)
        return carry

    lax.fori_loop(0, 16, activate, 0)
    act_rows = act.reshape(2 * 16 * 11 * 8, 128)
    for i in range(2):
        g = valid + i
        f = jnp.maximum(g - 2, 0)
        for y in range(16):
            at = (f & 1) * (16 * 88) + (y % 8 + 2) * 8 + y // 8 * 4 + (f >> 1)
            block = act_rows[pl.ds(at, 16, stride=88)]
            block = jnp.where(g < 2, old_ref[1, y].astype(F32), block)
            to = 48 + i * 256 + y * 16
            pay_ref[to : to + 16] = block.astype(BF16)


def conv_rows(first, last, act3_ref, stem_ref, conv_ref):
    j = lax.axis_index("strip")
    count = last - first
    zero = jnp.zeros((384, 128), BF16)

    def weight(col, b, e):
        if not 0 <= e <= 2:
            return zero
        return jnp.concatenate([conv_ref[a, b, e] for a in range(3)], axis=0)

    weights = jnp.concatenate(
        [
            jnp.concatenate([weight(col, b, col - k) for k in range(2)], axis=1)
            for col in range(4)
            for b in range(3)
        ],
        axis=0,
    )
    line = first + iota((count, 16, 128), 0)
    outside = (j == 0) & (line == 0) & (iota((count, 16, 128), 1) % 8 < 4)
    keep = jnp.where(outside, 0.0, 1.0)
    pairs = []
    for w0 in range(0, 16, 8):
        left = jnp.concatenate(
            [
                jnp.concatenate(
                    [
                        act3_ref[w0 + 2 * k + col, first + b : last + b].reshape(count * 16, 384)
                        for k in range(4)
                    ],
                    axis=0,
                )
                for col in range(4)
                for b in range(3)
            ],
            axis=1,
        )
        out = dot(left, weights).reshape(4, count, 16, 256)
        for k in range(4):
            for i in range(2):
                w = w0 + 2 * k + i
                value = out[k, :, :, i * 128 : i * 128 + 128]
                value = value + stem_ref[w, first:last].astype(F32)
                pairs.append((value * keep).astype(BF16))
    return pairs


def conv_first_kernel(split, act3_ref, stem_ref, conv_ref, out_ref):
    for w, value in enumerate(conv_rows(0, split, act3_ref, stem_ref, conv_ref)):
        out_ref[w] = value


def conv_second_kernel(
    split,
    scalars_ref,
    act3_ref,
    stem_ref,
    conv_ref,
    part_ref,
    res_cache_ref,
    after_ref,
    out_ref,
    pay_ref,
    res,
):
    del after_ref
    valid = whole(scalars_ref, 0)
    part = part_ref[...].astype(F32)
    for p in range(2):
        res[p, :, 0:split] = part[:, :, p * 8 : p * 8 + 8]
    for w, value in enumerate(conv_rows(split, 9, act3_ref, stem_ref, conv_ref)):
        out_ref[w] = value
        for p in range(2):
            res[p, w, split:9] = value.astype(F32)[:, p * 8 : p * 8 + 8]
    res_rows = res.reshape(2 * 16 * 9 * 8, 128)
    for i in range(2):
        g = valid + i
        f = jnp.maximum(g - 2, 0)
        for y in range(16):
            at = (f & 1) * (16 * 72) + (y % 8 + 1) * 8 + y // 8 * 4 + (f >> 1)
            block = res_rows[pl.ds(at, 16, stride=72)]
            block = jnp.where(g < 2, res_cache_ref[1, y].astype(F32), block)
            to = i * 256 + y * 16
            pay_ref[to : to + 16] = block.astype(BF16)


def down_kernel(
    split,
    scalars_ref,
    part_ref,
    rest_ref,
    down_ref,
    res_cache_ref,
    below_ref,
    after_ref,
    lat_ref,
    rcache,
    res3,
    lat,
):
    del after_ref
    j = lax.axis_index("strip")
    valid = whole(scalars_ref, 0)
    rcache[...] = jnp.zeros(rcache.shape, F32)
    has_above = jnp.where(j > 0, 1.0, 0.0)
    for f in range(2):
        rcache[f, 0:16] = below_ref[4 + f].astype(F32) * has_above
        rcache[f, 16:272] = res_cache_ref[f].reshape(256, 128).astype(F32)
    begin = iota((9, 8, 128), 1) % 4 == 0
    res3[0] = jnp.zeros(res3.shape[1:], F32)

    def delay(w, carry):
        both = jnp.concatenate([part_ref[w], rest_ref[w]], axis=0).astype(F32)
        even, odd = both[:, 0:8], both[:, 8:16]
        olds = []
        for f in range(2):
            olds.append(
                jnp.stack([rcache[f, pl.ds(y * 16 + w, 8, stride=32)] for y in range(9)], axis=0)
            )
        res3[w + 1, :, :, 0:128] = jnp.where(begin, olds[0], pltpu.roll(even, 1, 1))
        res3[w + 1, :, :, 128:256] = jnp.where(begin, olds[1], pltpu.roll(odd, 1, 1))
        res3[w + 1, :, :, 256:384] = even
        return carry

    lax.fori_loop(0, 16, delay, 0)
    total = jnp.zeros((256, 256), F32)
    for b in range(3):
        for e in range(3):
            left = jnp.concatenate(
                [res3[2 * k + e, 2 * i + b] for k in range(8) for i in range(4)], axis=0
            ).astype(BF16)
            right = jnp.concatenate([down_ref[a, b, e] for a in range(3)], axis=0)
            total = total + dot(left, right)
    live = 2 * (iota((256, 256), 0) % 4) < valid
    total = jnp.where(live, total, 0.0)
    for o in range(2):
        lat[o] = total[:, o * 128 : (o + 1) * 128]
    for t in range(4):
        for h in range(2):
            for i in range(4):
                for o in range(2):
                    block = lat[o, pl.ds(i * 8 + h * 4 + t, 8, stride=32)]
                    lat_ref[t, h * 4 + i, :, o * 128 : (o + 1) * 128] = block.astype(BF16)


def partner(value, axis, stride):
    pairs = [(source, source ^ stride) for source in range(lax.axis_size(axis))]
    return lax.ppermute(value, axis, pairs)


def shifted(value, axis, by):
    size = lax.axis_size(axis)
    return lax.ppermute(value, axis, [(i, (i + by) % size) for i in range(size)])


def body(
    loader_rows,
    load_owner,
    load_slot,
    valid_frames,
    next_owner,
    pixel_cache,
    act_cache,
    res_cache,
    stem_weight,
    norm_gain,
    norm_bias,
    conv_weight,
    down_weight,
):
    streams = lax.axis_size("stream")
    strips = lax.axis_size("strip")
    stream_pos = lax.axis_index("stream")
    sections = streams.bit_length() - 1
    fill = loader_rows.shape[1]
    per = fill // streams
    pix, acts, ress = pixel_cache[0], act_cache[0], res_cache[0]
    mega = 1024 * 1024
    cost = pl.CostEstimate(flops=2 * 10**9, bytes_accessed=4 * mega, transcendentals=0)
    half_per = fill // streams // 2
    direct = half_per % 8 == 0
    line_shape = (strips, streams, half_per, 128) if direct else (fill // 2, 128)
    lines = pl.pallas_call(
        functools.partial(sort_kernel, streams),
        out_shape=jax.ShapeDtypeStruct(line_shape, BF16),
        in_specs=[VM] * 3,
        out_specs=VM,
        scratch_shapes=[pltpu.VMEM((128, 2 * fill), F32)],
        cost_estimate=cost,
    )(loader_rows[0].T, load_owner, load_slot)
    if not direct:
        lines = lines.reshape(1, streams, half_per, 128)
        lines = jnp.broadcast_to(lines, (strips, streams, half_per, 128))
    lines = lines.reshape(strips * streams, half_per, 128)
    recv = lax.all_to_all(lines, ("strip", "stream"), 0, 0, tiled=True)
    recv = recv.reshape(strips, fill // 2, 128)
    below, above, mid = pl.pallas_call(
        pack_kernel,
        out_shape=(
            jax.ShapeDtypeStruct((8, 16, 128), BF16),
            jax.ShapeDtypeStruct((4, 16, 128), BF16),
            jax.ShapeDtypeStruct((18, 16, 128), BF16),
        ),
        in_specs=[ANY] + [VM] * 2 + [ANY] * 2,
        out_specs=(VM,) * 3,
        scratch_shapes=[pltpu.VMEM((128, 256), F32), pltpu.SemaphoreType.DMA((6,))],
        compiler_params=pltpu.CompilerParams(vmem_limit_bytes=4 * mega),
    )(lines, pix, stem_weight, acts, ress)
    below = shifted(below, "strip", 1)
    above = shifted(above, "strip", -1)
    mid = shifted(mid, "strip", 2)
    scalars = jnp.concatenate([valid_frames, next_owner, jnp.zeros((126,), jnp.int32)])
    rows_all = strips * 16
    first, act3, stem = pl.pallas_call(
        functools.partial(stem_kernel, strips),
        out_shape=(
            jax.ShapeDtypeStruct((560, 128), BF16),
            jax.ShapeDtypeStruct((18, 11, 16, 384), BF16),
            jax.ShapeDtypeStruct((16, 9, 16, 128), BF16),
        ),
        in_specs=[VM] * 9,
        out_specs=(VM,) * 3,
        scratch_shapes=[
            pltpu.VMEM((strips, 32, 128), F32),
            pltpu.VMEM((3, rows_all + 8, 8, 128), F32),
            pltpu.VMEM((rows_all + 8, 8, 432), F32),
            pltpu.VMEM((rows_all + 4, 8, 1024), F32),
            pltpu.VMEM((2, 16, 11, 8, 128), F32),
            pltpu.VMEM((2, 16, 11, 8, 128), F32),
            pltpu.VMEM((2, 416, 128), F32),
        ],
        compiler_params=pltpu.CompilerParams(vmem_limit_bytes=24 * mega),
        cost_estimate=cost,
    )(
        scalars,
        norm_gain,
        norm_bias,
        recv,
        pix,
        acts,
        below,
        above,
        mid,
    )
    split = 5
    part = pl.pallas_call(
        functools.partial(conv_first_kernel, split),
        out_shape=jax.ShapeDtypeStruct((16, split, 16, 128), BF16),
        in_specs=[VM] * 3,
        out_specs=VM,
        compiler_params=pltpu.CompilerParams(vmem_limit_bytes=24 * mega),
        cost_estimate=cost,
    )(act3, stem, conv_weight)
    keeps = []

    def passed(value):
        bit = len(keeps)
        keeps.append((value[0:1].astype(jnp.int32) >> bit) & 1 == (stream_pos >> bit) & 1)
        return jnp.where(keeps[bit], value, partner(value, "stream", 1 << bit))

    first = passed(first)
    rest, second = pl.pallas_call(
        functools.partial(conv_second_kernel, split),
        out_shape=(
            jax.ShapeDtypeStruct((16, 9 - split, 16, 128), BF16),
            jax.ShapeDtypeStruct((512, 128), BF16),
        ),
        in_specs=[VM] * 6 + [ANY],
        out_specs=(VM,) * 2,
        scratch_shapes=[pltpu.VMEM((2, 16, 9, 8, 128), F32)],
        compiler_params=pltpu.CompilerParams(vmem_limit_bytes=24 * mega),
        cost_estimate=cost,
    )(scalars, act3, stem, conv_weight, part, ress, first)
    for bit in range(1, sections - 1):
        first = passed(first)
    latent = pl.pallas_call(
        functools.partial(down_kernel, split),
        out_shape=jax.ShapeDtypeStruct((4, 8, 8, 256), BF16),
        in_specs=[VM] * 6 + [ANY],
        out_specs=VM,
        scratch_shapes=[
            pltpu.VMEM((2, 384, 128), F32),
            pltpu.VMEM((17, 9, 8, 384), F32),
            pltpu.VMEM((2, 256, 128), F32),
        ],
        compiler_params=pltpu.CompilerParams(vmem_limit_bytes=24 * mega),
        cost_estimate=cost,
    )(scalars, part, rest, down_weight, ress, below, first)
    if sections > 1:
        first = passed(first)
    for bit in range(sections):
        second = jnp.where(keeps[bit], second, partner(second, "stream", 1 << bit))
    new_pix = first[16:48, 0:48].reshape(1, 2, 16, 48)
    new_act = first[48:].reshape(1, 2, 16, 16, 128)
    return (latent[None], new_pix, new_act, second.reshape(1, 2, 16, 16, 128))


def solution(mesh):
    in_specs = (
        P("stream", "strip", None),
        P("stream", "strip"),
        P("stream", "strip"),
        P("stream"),
        P("stream"),
        P("stream", None, "strip", None),
        P("stream", None, "strip", None, None),
        P("stream", None, "strip", None, None),
        P(),
        P(),
        P(),
        P(),
        P(),
    )
    out_specs = (
        P("stream", None, "strip", None, None),
        P("stream", None, "strip", None),
        P("stream", None, "strip", None, None),
        P("stream", None, "strip", None, None),
    )
    return jax.shard_map(body, mesh=mesh, in_specs=in_specs, out_specs=out_specs, check_vma=False)
```

```python
import functools

import jax
import jax.numpy as jnp
from jax import lax
from jax.experimental import pallas as pl
from jax.experimental.pallas import tpu as pltpu
from jax.sharding import PartitionSpec as P

FRAMES = 8
GROUPS = 32
EPSILON = 1e-06
F32 = jnp.float32
BF16 = jnp.bfloat16
VM = pl.BlockSpec(memory_space=pltpu.VMEM)
ANY = pl.BlockSpec(memory_space=pl.ANY)


def iota(shape, axis):
    return lax.broadcasted_iota(jnp.int32, shape, axis)


def whole(scalars_ref, which):
    row = scalars_ref[...].astype(F32).reshape(1, 128)
    return jnp.sum(jnp.where(iota((1, 128), 1) == which, row, 0.0)).astype(jnp.int32)


def dot(a, b):
    return jnp.dot(a, b, preferred_element_type=F32)


def dot_nt(a, b):
    return lax.dot_general(a, b, (((1,), (1,)), ((), ())), preferred_element_type=F32)


def sort_kernel(streams, cols_ref, owner_ref, slot_ref, out_ref, wide):
    width, fill = cols_ref.shape
    half_per = fill // streams // 2
    lines = fill // 2
    wide[...] = jnp.zeros(wide.shape, F32)
    pixels, slots = cols_ref[...].astype(F32), slot_ref[...].astype(F32)
    for side in range(2):
        at = side * 64
        wide[at : at + width, side * fill : (side + 1) * fill] = pixels
        wide[at + width : at + width + 1, side * fill : (side + 1) * fill] = slots
    owner = owner_ref[...]
    hot = jnp.where(iota((streams, fill), 0) == owner, 1.0, 0.0)
    upper = jnp.where(iota((fill, fill), 0) <= iota((fill, fill), 1), 1.0, 0.0).astype(BF16)
    running = dot(hot.astype(BF16), upper)
    rank = jnp.sum(hot * running, axis=0, keepdims=True).astype(jnp.int32) - 1
    half = rank // half_per
    line = owner * half_per + rank - half * half_per
    line = jnp.concatenate([jnp.where(half == side, line, -1) for side in range(2)], axis=1)
    pick = jnp.where(iota((lines, 2 * fill), 0) == jnp.broadcast_to(line, (lines, 2 * fill)), 1.0, 0.0)
    out = dot_nt(pick.astype(BF16), wide[...].astype(BF16)).astype(BF16)
    if len(out_ref.shape) == 2:
        out_ref[...] = out
    else:
        for strip in range(out_ref.shape[0]):
            out_ref[strip] = out.reshape(out_ref.shape[1:])


def pack_kernel(pix_ref, sw_ref, act_ref, res_ref, down_ref, up_ref, mid_ref, sw, sems):
    copies = []
    for f in range(2):
        copies.append((act_ref.at[f, 14:16], down_ref.at[2 * f : 2 * f + 2]))
        copies.append((res_ref.at[f, 15:16], down_ref.at[4 + f : 5 + f]))
        copies.append((act_ref.at[f, 0:1], up_ref.at[f : f + 1]))
    copies = [pltpu.make_async_copy(a, b, sems.at[i]) for i, (a, b) in enumerate(copies)]
    for copy in copies:
        copy.start()
    pix = pix_ref[...].reshape(32, 48).astype(F32)
    pix = jnp.concatenate([pix, jnp.zeros((32, 80), F32)], axis=1)
    pix = pix.astype(BF16).reshape(2, 16, 128)
    down_ref[6:8] = pix
    up_ref[2:4] = pix
    mid_ref[0:2] = pix
    sw[...] = jnp.zeros(sw.shape, F32)
    for k in range(2):
        for e in range(3):
            for a in range(3):
                for b in range(3):
                    at = 27 * (k + e) + 9 * a + 3 * b
                    sw[at : at + 3, k * 128 : k * 128 + 128] = sw_ref[a, b, e].astype(F32)
    for k in range(2):
        half = sw[:, k * 128 : k * 128 + 128].astype(BF16)
        mid_ref[2 + 8 * k : 10 + 8 * k] = half.reshape(8, 16, 128)
    for copy in copies:
        copy.wait()


def received(line):
    line = line.astype(F32)
    both = jnp.concatenate([line, pltpu.roll(line, 64, 1)], axis=0)
    slot_lane = jnp.where(iota((8, 128), 1) == 48, 1.0, 0.0).astype(BF16)
    slots = dot_nt(slot_lane, both.astype(BF16)).astype(jnp.int32)
    return jnp.where(iota((128, 128), 1) < 48, both, 0.0), slots


def gather_pixels(strips, j, pc, pix_ref, below_ref, above_ref, mid_ref):
    pc[j] = jnp.zeros((32, 128), F32)
    pc[j, :, 0:48] = pix_ref[...].reshape(32, 48).astype(F32)
    pc[lax.rem(j + strips - 1, strips)] = below_ref[6:8].reshape(32, 128).astype(F32)
    pc[lax.rem(j + 1, strips)] = above_ref[2:4].reshape(32, 128).astype(F32)
    pc[lax.rem(j + 2, strips)] = mid_ref[0:2].reshape(32, 128).astype(F32)


def widen_cache(strips, j, cache, old_ref, below_ref, above_ref):
    has_above = jnp.where(j > 0, 1.0, 0.0)
    has_below = jnp.where(j < strips - 1, 1.0, 0.0)
    for f in range(2):
        cache[f, 304:416] = jnp.zeros((112, 128), F32)
        cache[f, 32:288] = old_ref[f].reshape(256, 128).astype(F32)
        cache[f, 0:32] = below_ref[2 * f : 2 * f + 2].reshape(32, 128).astype(F32) * has_above
        cache[f, 288:304] = above_ref[f].astype(F32) * has_below


def stem_weight_of(mid_ref):
    return jnp.concatenate(
        [mid_ref[2 + 8 * k : 10 + 8 * k].reshape(128, 128) for k in range(2)], axis=1
    )


def spread_matrix():
    lanes = iota((8, 1024), 1)
    pair, m = lanes >> 7, lanes & 127
    col = (m * 2428) >> 16
    tap = m - 27 * col
    a = (tap * 7282) >> 16
    b = ((tap - 9 * a) * 21846) >> 16
    c = tap - 9 * a - 3 * b
    w = 2 * pair - 1 + col
    source = jnp.where((m < 108) & (w >= 0) & (w < 16), (b * 3 + a) * 48 + c * 16 + w, -1)
    line = iota((54, 8, 1024), 0) * 8 + iota((54, 8, 1024), 1)
    return jnp.where(line == source[None], 1.0, 0.0).reshape(432, 1024).astype(BF16)


def norm_rows(strips, s1, s2, gain_ref, bias_ref):
    same = jnp.where(iota((128, 128), 0) // 4 == iota((128, 128), 1) // 4, 1.0, 0.0)
    count = strips * 16 * 16 * 4
    exact = functools.partial(
        jnp.dot, preferred_element_type=F32, precision=lax.Precision.HIGHEST
    )
    mean = exact(s1, same) / count
    inv = lax.rsqrt(exact(s2, same) / count - mean * mean + EPSILON)
    scale = inv * gain_ref[...].reshape(1, 128)
    return scale, bias_ref[...].reshape(1, 128) - mean * scale


def silu(v):
    h = 0.5 * v
    return h + h * jnp.tanh(h)


def pair_weight(conv_ref):
    zero = jnp.zeros((384, 128), BF16)

    def weight(b, e):
        if not 0 <= e <= 2:
            return zero
        return jnp.concatenate([conv_ref[a, b, e] for a in range(3)], axis=0)

    return jnp.concatenate(
        [
            jnp.concatenate([weight(b, col - k) for k in range(2)], axis=1)
            for col in range(4)
            for b in range(3)
        ],
        axis=0,
    )


def row_at(t, y):
    t = jnp.maximum(t, 0)
    h = 1 if y >= 8 else 0
    return (t & 1) * (16 * 88) + (y + 2 - 8 * h) * 8 + h * 4 + (t >> 1)


def stem_kernel(
    strips,
    scalars_ref,
    gain_ref,
    bias_ref,
    recv_ref,
    pix_ref,
    old_ref,
    below_ref,
    above_ref,
    mid_ref,
    pay_ref,
    act,
    stem,
    pc,
    zs,
    xs,
    ys,
):
    j = lax.axis_index("strip")
    valid = whole(scalars_ref, 0)
    rows_all = strips * 16
    gather_pixels(strips, j, pc, pix_ref, below_ref, above_ref, mid_ref)
    zs[:, 0:4] = jnp.zeros((3, 4, 8, 128), F32)
    zs[:, 4 + rows_all :] = jnp.zeros((3, 4, 8, 128), F32)
    sub = iota((128, 128), 0)
    crow, cframe = iota((128, 32), 1) % 16, iota((128, 32), 1) // 16
    csub = iota((128, 32), 0)
    for s in range(strips):
        pixels, slots = received(recv_ref[s])
        frame, row = slots >> 4, slots & 15
        source = jnp.concatenate([pixels, pc[s]], axis=0).astype(BF16)
        hits = []
        for a in range(3):
            t = frame + 2 - a
            place = jnp.where(t < FRAMES, row * 8 + (t & 1) * 4 + (t >> 1), -1)
            hit = jnp.where(sub.reshape(16, 8, 128) == place[None], 1.0, 0.0).reshape(128, 128)
            ct = cframe - a
            cplace = jnp.where(ct >= 0, crow * 8 + (ct & 1) * 4 + (ct >> 1), -1)
            chit = jnp.where(csub == cplace, 1.0, 0.0)
            hits.append(jnp.concatenate([hit, chit], axis=1).astype(BF16))
        placed = dot(jnp.concatenate(hits, axis=0), source).reshape(3, 16, 8, 128)
        for a in range(3):
            zs[a, 4 + s * 16 : 4 + (s + 1) * 16] = placed[a]
    pixels, slots = received(recv_ref[j])
    goal = (slots >> 4) + 2 - valid
    place = jnp.where((goal >= 0) & (goal < 2), goal * 16 + (slots & 15), -1)
    hit = jnp.where(iota((4, 8, 128), 0) * 8 + iota((4, 8, 128), 1) == place[None], 1.0, 0.0)
    cgoal = iota((32, 32), 1) // 16 - valid
    cplace = jnp.where((cgoal >= 0) & (cgoal < 2), cgoal * 16 + iota((32, 32), 1) % 16, -1)
    chit = jnp.where(iota((32, 32), 0) == cplace, 1.0, 0.0)
    source = jnp.concatenate([pixels, pc[j]], axis=0).astype(BF16)
    fresh = dot(jnp.concatenate([hit.reshape(32, 128), chit], axis=1).astype(BF16), source)
    target = whole(scalars_ref, 1).astype(F32)
    pay_ref[0:16] = jnp.full((16, 128), target, F32).astype(BF16)
    pay_ref[16:48] = fresh.astype(BF16)
    high = rows_all + 4
    for b in range(3):
        for a in range(3):
            q = (b * 3 + a) * 48
            xs[2 : high + 2, :, q : q + 48] = zs[a, 1 + b : high + 1 + b, :, 0:48]
    patches = xs[2 : high + 2].reshape(high * 8, 432).astype(BF16)
    ys[...] = dot(patches, spread_matrix()).reshape(high, 8, 1024)
    full = ys[2 : 2 + rows_all].reshape(rows_all * 8, 1024).astype(BF16)
    base = j * 16
    first, second = ys[pl.ds(base, 11)], ys[pl.ds(base + 8, 11)]
    low = iota((11, 8, 1024), 1) < 4
    own_even = jnp.where(low, first, pltpu.roll(second, 4, 1))
    own_odd = jnp.where(low, pltpu.roll(first, 4, 1), second)
    own = jnp.concatenate([own_even, own_odd], axis=0).reshape(176, 1024).astype(BF16)
    weight = stem_weight_of(mid_ref)
    s1 = jnp.zeros((8, 256), F32)
    s2 = jnp.zeros((8, 256), F32)
    for chunk in range(8):
        out = dot(full[:, chunk * 128 : chunk * 128 + 128], weight).astype(BF16).astype(F32).reshape(rows_all, 8, 256)
        s1 = s1 + jnp.sum(out, axis=0)
        s2 = s2 + jnp.sum(out * out, axis=0)
        mine = dot(own[:, chunk * 128 : chunk * 128 + 128], weight).astype(BF16).astype(F32).reshape(2, 11, 8, 256)
        for i in range(2):
            stem[:, 2 * chunk + i] = mine[:, :, :, i * 128 : (i + 1) * 128]
    s1 = s1[:, 0:128] + s1[:, 128:256]
    s2 = s2[:, 0:128] + s2[:, 128:256]
    scale, shift = norm_rows(strips, s1, s2, gain_ref, bias_ref)
    low8 = iota((8, 128), 0) < 4
    scales = (
        jnp.where(low8, scale, pltpu.roll(scale, 4, 0)),
        jnp.where(low8, pltpu.roll(scale, 4, 0), scale),
    )
    shifts = (
        jnp.where(low8, shift, pltpu.roll(shift, 4, 0)),
        jnp.where(low8, pltpu.roll(shift, 4, 0), shift),
    )
    half = iota((11, 8, 128), 1) // 4
    line_of = j * 16 + iota((11, 8, 128), 0) - 2 + 8 * half
    inside = jnp.where((line_of >= 0) & (line_of < rows_all), 1.0, 0.0)

    def activate(w, carry):
        for p in range(2):
            act[p, w] = silu(stem[p, w] * scales[p] + shifts[p]) * inside
        return carry

    lax.fori_loop(0, 16, activate, 0, unroll=4)
    act_rows = act.reshape(2 * 16 * 11 * 8, 128)
    for i in range(2):
        for y in range(16):
            block = act_rows[pl.ds(row_at(valid - 2 + i, y), 16, stride=88)]
            block = jnp.where(valid + i < 2, old_ref[1, y].astype(F32), block)
            to = 48 + i * 256 + y * 16
            pay_ref[to : to + 16] = block.astype(BF16)


def last_kernel(
    after_ref,
    scalars_ref,
    act,
    stem,
    old_ref,
    res_old_ref,
    below_ref,
    above_ref,
    conv_ref,
    pay_ref,
    lines,
):
    del after_ref
    j = lax.axis_index("strip")
    valid = whole(scalars_ref, 0)
    act_rows = act.reshape(2 * 16 * 11 * 8, 128)
    stem_rows = stem.reshape(2 * 16 * 11 * 8, 128)
    column = iota((16, 128), 0)

    def side_by_side(m, y, block):
        before = jnp.where(column == 0, 0.0, pltpu.roll(block, 1, 0))
        after = jnp.where(column == 15, 0.0, pltpu.roll(block, 15, 0))
        lines[m, y + 1] = jnp.concatenate([before, block, after], axis=1).astype(BF16)

    for m in range(4):
        from_cache = valid - 2 + m

        @pl.when(from_cache >= 2)
        def _(m=m, from_cache=from_cache):
            for y in range(-1, 17):
                block = act_rows[pl.ds(row_at(from_cache - 2, y), 16, stride=88)]
                side_by_side(m, y, block)

        @pl.when(from_cache < 2)
        def _(m=m, from_cache=from_cache):
            f = jnp.clip(from_cache, 0, 1)
            has_above = jnp.where(j > 0, 1.0, 0.0)
            has_below = jnp.where(j < lax.axis_size("strip") - 1, 1.0, 0.0)
            side_by_side(m, -1, below_ref[2 * f + 1].astype(F32) * has_above)
            for y in range(16):
                side_by_side(m, y, old_ref[f, y].astype(F32))
            side_by_side(m, 16, above_ref[f].astype(F32) * has_below)

    zero = jnp.zeros((384, 128), BF16)

    def weight(a, b):
        if not 0 <= b <= 2:
            return zero
        return jnp.concatenate([conv_ref[a, b, e] for e in range(3)], axis=0)

    weights = jnp.concatenate(
        [
            jnp.concatenate([weight(a, y - k) for k in range(2)], axis=1)
            for y in range(4)
            for a in range(3)
        ],
        axis=0,
    )
    left = jnp.concatenate(
        [
            jnp.concatenate(
                [lines[i + a, 2 * k + y] for i in range(2) for k in range(8)], axis=0
            )
            for y in range(4)
            for a in range(3)
        ],
        axis=1,
    )
    out = dot(left, weights).reshape(2, 8, 16, 256)
    for i in range(2):
        for y in range(16):
            block = stem_rows[pl.ds(row_at(valid - 2 + i, y), 16, stride=88)]
            block = block + out[i, y // 2, :, y % 2 * 128 : y % 2 * 128 + 128]
            if i == 0:
                block = jnp.where(valid < 2, res_old_ref[1, y].astype(F32), block)
            to = i * 256 + y * 16
            pay_ref[to : to + 16] = block.astype(BF16)


def conv_kernel(
    strips,
    w0,
    after_ref,
    after_too_ref,
    act,
    stem,
    old_ref,
    below_ref,
    above_ref,
    conv_ref,
    out_ref,
    cache,
    act3,
):
    del after_ref, after_too_ref
    j = lax.axis_index("strip")
    widen_cache(strips, j, cache, old_ref, below_ref, above_ref)
    at0 = iota((11, 8, 128), 1) == 0
    at4 = iota((11, 8, 128), 1) == 4
    edge = 0 if w0 == 0 else 9
    act3[edge] = jnp.zeros(act3.shape[1:], BF16)
    shift = 1 if w0 == 0 else 1 - w0

    def arrange(w, carry):
        late = []
        for f in range(2):
            rows = [
                jnp.broadcast_to(cache[f, pl.ds(y * 16 + w, 1)], (8, 128)) for y in range(19)
            ]
            upper, lower = jnp.stack(rows[0:11], axis=0), jnp.stack(rows[8:19], axis=0)
            rolled = pltpu.roll(act[f, w], 1, 1)
            late.append(jnp.where(at0, upper, jnp.where(at4, lower, rolled)))
        even, odd = act[0, w], act[1, w]
        taps = ((late[0], late[1]), (late[1], even), (even, odd))
        for a in range(3):
            act3[w + shift, :, :, a * 128 : (a + 1) * 128] = jnp.concatenate(taps[a], axis=1).astype(BF16)
        return carry

    lax.fori_loop(max(w0 - 1, 0), min(w0 + 9, 16), arrange, 0, unroll=3)
    weights = pair_weight(conv_ref)
    outside = (j == 0) & (iota((9, 16, 128), 0) == 0) & (iota((9, 16, 128), 1) % 8 < 4)
    keep = jnp.where(outside, 0.0, 1.0)
    left = jnp.concatenate(
        [
            jnp.concatenate(
                [act3[2 * k + col, b : b + 9].reshape(144, 384) for k in range(4)],
                axis=0,
            )
            for col in range(4)
            for b in range(3)
        ],
        axis=1,
    )
    out = dot(left, weights).reshape(4, 9, 16, 256)
    for k in range(4):
        for n in range(2):
            w = w0 + 2 * k + n
            value = out[k, :, :, n * 128 : n * 128 + 128]
            value = value + jnp.concatenate([stem[0, w, 1:10], stem[1, w, 1:10]], axis=1)
            out_ref[w - w0] = (value * keep).astype(BF16)


def down_kernel(
    scalars_ref,
    part_ref,
    rest_ref,
    down_ref,
    res_cache_ref,
    below_ref,
    after_ref,
    lat_ref,
    rcache,
    res3,
    lat,
):
    del after_ref
    j = lax.axis_index("strip")
    valid = whole(scalars_ref, 0)
    rcache[...] = jnp.zeros(rcache.shape, F32)
    has_above = jnp.where(j > 0, 1.0, 0.0)
    for f in range(2):
        rcache[f, 0:16] = below_ref[4 + f].astype(F32) * has_above
        rcache[f, 16:272] = res_cache_ref[f].reshape(256, 128).astype(F32)
    at0 = iota((9, 8, 128), 1) == 0
    at4 = iota((9, 8, 128), 1) == 4
    res3[0] = jnp.zeros(res3.shape[1:], F32)

    for w0, ref in ((0, part_ref), (8, rest_ref)):

        def delay(w, carry, w0=w0, ref=ref):
            both = ref[w].astype(F32)
            even, odd = both[:, 0:8], both[:, 8:16]
            olds = []
            for f in range(2):
                rows = [
                    jnp.broadcast_to(rcache[f, pl.ds(y * 16 + w0 + w, 1)], (8, 128))
                    for y in range(17)
                ]
                olds.append((jnp.stack(rows[0:9], axis=0), jnp.stack(rows[8:17], axis=0)))
            at = w0 + w + 1
            for f, v in enumerate((even, odd)):
                rolled = pltpu.roll(v, 1, 1)
                late = jnp.where(at0, olds[f][0], jnp.where(at4, olds[f][1], rolled))
                res3[at, :, :, f * 128 : f * 128 + 128] = late
            res3[at, :, :, 256:384] = even
            return carry

        lax.fori_loop(0, 8, delay, 0, unroll=2)
    total = jnp.zeros((256, 256), F32)
    for b in range(3):
        for e in range(3):
            left = jnp.concatenate(
                [res3[2 * k + e, 2 * i + b] for k in range(8) for i in range(4)], axis=0
            ).astype(BF16)
            right = jnp.concatenate([down_ref[a, b, e] for a in range(3)], axis=0)
            total = total + dot(left, right)
    live = 2 * (iota((256, 256), 0) % 4) < valid
    total = jnp.where(live, total, 0.0)
    for o in range(2):
        lat[o] = total[:, o * 128 : (o + 1) * 128]
    for t in range(4):
        for h in range(2):
            for i in range(4):
                for o in range(2):
                    block = lat[o, pl.ds(i * 8 + h * 4 + t, 8, stride=32)]
                    lat_ref[t, h * 4 + i, :, o * 128 : (o + 1) * 128] = block.astype(BF16)


def partner(value, axis, stride):
    pairs = [(source, source ^ stride) for source in range(lax.axis_size(axis))]
    return lax.ppermute(value, axis, pairs)


def shifted(value, axis, by):
    size = lax.axis_size(axis)
    return lax.ppermute(value, axis, [(i, (i + by) % size) for i in range(size)])


def body(
    loader_rows,
    load_owner,
    load_slot,
    valid_frames,
    next_owner,
    pixel_cache,
    act_cache,
    res_cache,
    stem_weight,
    norm_gain,
    norm_bias,
    conv_weight,
    down_weight,
):
    streams = lax.axis_size("stream")
    strips = lax.axis_size("strip")
    stream_pos = lax.axis_index("stream")
    sections = streams.bit_length() - 1
    fill = loader_rows.shape[1]
    per = fill // streams
    pix, acts, ress = pixel_cache[0], act_cache[0], res_cache[0]
    mega = 1024 * 1024
    cost = pl.CostEstimate(flops=2 * 10**9, bytes_accessed=4 * mega, transcendentals=0)
    half_per = fill // streams // 2
    direct = half_per % 8 == 0
    line_shape = (strips, streams, half_per, 128) if direct else (fill // 2, 128)
    lines = pl.pallas_call(
        functools.partial(sort_kernel, streams),
        out_shape=jax.ShapeDtypeStruct(line_shape, BF16),
        in_specs=[VM] * 3,
        out_specs=VM,
        scratch_shapes=[pltpu.VMEM((128, 2 * fill), F32)],
        cost_estimate=cost,
    )(loader_rows[0].T, load_owner, load_slot)
    if not direct:
        lines = lines.reshape(1, streams, half_per, 128)
        lines = jnp.broadcast_to(lines, (strips, streams, half_per, 128))
    lines = lines.reshape(strips * streams, half_per, 128)
    recv = lax.all_to_all(lines, ("strip", "stream"), 0, 0, tiled=True)
    recv = recv.reshape(strips, fill // 2, 128)
    below, above, mid = pl.pallas_call(
        pack_kernel,
        out_shape=(
            jax.ShapeDtypeStruct((8, 16, 128), BF16),
            jax.ShapeDtypeStruct((4, 16, 128), BF16),
            jax.ShapeDtypeStruct((18, 16, 128), BF16),
        ),
        in_specs=[VM] * 2 + [ANY] * 2,
        out_specs=(VM,) * 3,
        scratch_shapes=[pltpu.VMEM((128, 256), F32), pltpu.SemaphoreType.DMA((6,))],
        compiler_params=pltpu.CompilerParams(vmem_limit_bytes=4 * mega),
    )(pix, stem_weight, acts, ress)
    below = shifted(below, "strip", 1)
    above = shifted(above, "strip", -1)
    mid = shifted(mid, "strip", 2)
    scalars = jnp.concatenate([valid_frames, next_owner, jnp.zeros((126,), jnp.int32)])
    rows_all = strips * 16
    window = jax.ShapeDtypeStruct((2, 16, 11, 8, 128), F32)
    first, act, stem = pl.pallas_call(
        functools.partial(stem_kernel, strips),
        out_shape=(jax.ShapeDtypeStruct((560, 128), BF16), window, window),
        in_specs=[VM] * 9,
        out_specs=(VM,) * 3,
        scratch_shapes=[
            pltpu.VMEM((strips, 32, 128), F32),
            pltpu.VMEM((3, rows_all + 8, 8, 128), F32),
            pltpu.VMEM((rows_all + 8, 8, 432), F32),
            pltpu.VMEM((rows_all + 4, 8, 1024), F32),
        ],
        compiler_params=pltpu.CompilerParams(vmem_limit_bytes=24 * mega),
        cost_estimate=cost,
    )(scalars, norm_gain, norm_bias, recv, pix, acts, below, above, mid)
    keeps = []

    def passed(value, bit):
        if bit == len(keeps):
            keeps.append((value[0:1].astype(jnp.int32) >> bit) & 1 == (stream_pos >> bit) & 1)
        return jnp.where(keeps[bit], value, partner(value, "stream", 1 << bit))

    first = passed(first, 0)
    second = pl.pallas_call(
        last_kernel,
        out_shape=jax.ShapeDtypeStruct((512, 128), BF16),
        in_specs=[ANY] + [VM] * 8,
        out_specs=VM,
        scratch_shapes=[pltpu.VMEM((4, 18, 16, 384), BF16)],
        compiler_params=pltpu.CompilerParams(vmem_limit_bytes=24 * mega),
        cost_estimate=cost,
    )(first, scalars, act, stem, acts, ress, below, above, conv_weight)
    second = passed(second, 0)

    def convolved(w0, after, after_too):
        return pl.pallas_call(
            functools.partial(conv_kernel, strips, w0),
            out_shape=jax.ShapeDtypeStruct((8, 9, 16, 128), BF16),
            in_specs=[ANY] * 2 + [VM] * 6,
            out_specs=VM,
            scratch_shapes=[
                pltpu.VMEM((2, 416, 128), F32),
                pltpu.VMEM((10, 11, 16, 384), BF16),
            ],
            compiler_params=pltpu.CompilerParams(vmem_limit_bytes=24 * mega),
            cost_estimate=cost,
        )(after, after_too, act, stem, acts, below, above, conv_weight)

    part = convolved(0, first, second)
    for bit in range(1, sections - 1):
        first = passed(first, bit)
    rest = convolved(8, first, part)
    for bit in range(1, sections - 1):
        second = passed(second, bit)
    latent = pl.pallas_call(
        down_kernel,
        out_shape=jax.ShapeDtypeStruct((4, 8, 8, 256), BF16),
        in_specs=[VM] * 6 + [ANY],
        out_specs=VM,
        scratch_shapes=[
            pltpu.VMEM((2, 384, 128), F32),
            pltpu.VMEM((17, 9, 8, 384), F32),
            pltpu.VMEM((2, 256, 128), F32),
        ],
        compiler_params=pltpu.CompilerParams(vmem_limit_bytes=24 * mega),
        cost_estimate=cost,
    )(scalars, part, rest, down_weight, ress, below, second)
    if sections > 1:
        first = passed(first, sections - 1)
        second = passed(second, sections - 1)
    new_pix = first[16:48, 0:48].reshape(1, 2, 16, 48)
    new_act = first[48:].reshape(1, 2, 16, 16, 128)
    return (latent[None], new_pix, new_act, second.reshape(1, 2, 16, 16, 128))


def solution(mesh):
    in_specs = (
        P("stream", "strip", None),
        P("stream", "strip"),
        P("stream", "strip"),
        P("stream"),
        P("stream"),
        P("stream", None, "strip", None),
        P("stream", None, "strip", None, None),
        P("stream", None, "strip", None, None),
        P(),
        P(),
        P(),
        P(),
        P(),
    )
    out_specs = (
        P("stream", None, "strip", None, None),
        P("stream", None, "strip", None),
        P("stream", None, "strip", None, None),
        P("stream", None, "strip", None, None),
    )
    return jax.shard_map(body, mesh=mesh, in_specs=in_specs, out_specs=out_specs, check_vma=False)
```

```python
import functools

import jax
import jax.numpy as jnp
from jax import lax
from jax.experimental import pallas as pl
from jax.experimental.pallas import tpu as pltpu
from jax.sharding import PartitionSpec as P

FRAMES = 8
GROUPS = 32
EPSILON = 1e-06
F32 = jnp.float32
BF16 = jnp.bfloat16
VM = pl.BlockSpec(memory_space=pltpu.VMEM)
ANY = pl.BlockSpec(memory_space=pl.ANY)


def iota(shape, axis):
    return lax.broadcasted_iota(jnp.int32, shape, axis)


def whole(scalars_ref, which):
    row = scalars_ref[...].astype(F32).reshape(1, 128)
    return jnp.sum(jnp.where(iota((1, 128), 1) == which, row, 0.0)).astype(jnp.int32)


def dot(a, b):
    return jnp.dot(a, b, preferred_element_type=F32)


def dot_nt(a, b):
    return lax.dot_general(a, b, (((1,), (1,)), ((), ())), preferred_element_type=F32)


def sort_kernel(streams, cols_ref, owner_ref, slot_ref, out_ref, wide):
    width, fill = cols_ref.shape
    half_per = fill // streams // 2
    lines = fill // 2
    wide[...] = jnp.zeros(wide.shape, F32)
    pixels, slots = cols_ref[...].astype(F32), slot_ref[...].astype(F32)
    for side in range(2):
        at = side * 64
        wide[at : at + width, side * fill : (side + 1) * fill] = pixels
        wide[at + width : at + width + 1, side * fill : (side + 1) * fill] = slots
    owner = owner_ref[...]
    hot = jnp.where(iota((streams, fill), 0) == owner, 1.0, 0.0)
    upper = jnp.where(iota((fill, fill), 0) <= iota((fill, fill), 1), 1.0, 0.0).astype(BF16)
    running = dot(hot.astype(BF16), upper)
    rank = jnp.sum(hot * running, axis=0, keepdims=True).astype(jnp.int32) - 1
    half = rank // half_per
    line = owner * half_per + rank - half * half_per
    line = jnp.concatenate([jnp.where(half == side, line, -1) for side in range(2)], axis=1)
    pick = jnp.where(iota((lines, 2 * fill), 0) == jnp.broadcast_to(line, (lines, 2 * fill)), 1.0, 0.0)
    out = dot_nt(pick.astype(BF16), wide[...].astype(BF16)).astype(BF16)
    if len(out_ref.shape) == 2:
        out_ref[...] = out
    else:
        for strip in range(out_ref.shape[0]):
            out_ref[strip] = out.reshape(out_ref.shape[1:])


def pack_kernel(pix_ref, sw_ref, act_ref, res_ref, down_ref, up_ref, mid_ref, weight_ref, sw, sems):
    copies = []
    for f in range(2):
        copies.append((act_ref.at[f, 14:16], down_ref.at[2 * f : 2 * f + 2]))
        copies.append((res_ref.at[f, 15:16], down_ref.at[4 + f : 5 + f]))
        copies.append((act_ref.at[f, 0:1], up_ref.at[f : f + 1]))
    copies = [pltpu.make_async_copy(a, b, sems.at[i]) for i, (a, b) in enumerate(copies)]
    for copy in copies:
        copy.start()
    pix = pix_ref[...].reshape(32, 48).astype(F32)
    pix = jnp.concatenate([pix, jnp.zeros((32, 80), F32)], axis=1)
    pix = pix.astype(BF16).reshape(2, 16, 128)
    down_ref[6:8] = pix
    up_ref[2:4] = pix
    mid_ref[...] = pix
    sw[...] = jnp.zeros(sw.shape, F32)
    for k in range(2):
        for e in range(3):
            for a in range(3):
                for b in range(3):
                    at = 27 * (k + e) + 9 * a + 3 * b
                    sw[at : at + 3, k * 128 : k * 128 + 128] = sw_ref[a, b, e].astype(F32)
    weight_ref[...] = sw[...].astype(BF16)
    for copy in copies:
        copy.wait()


def received(line):
    line = line.astype(F32)
    both = jnp.concatenate([line, pltpu.roll(line, 64, 1)], axis=0)
    slot_lane = jnp.where(iota((8, 128), 1) == 48, 1.0, 0.0).astype(BF16)
    slots = dot_nt(slot_lane, both.astype(BF16)).astype(jnp.int32)
    return jnp.where(iota((128, 128), 1) < 48, both, 0.0), slots


def gather_pixels(strips, j, pc, pix_ref, below_ref, above_ref, mid_ref):
    pc[j] = jnp.zeros((32, 128), F32)
    pc[j, :, 0:48] = pix_ref[...].reshape(32, 48).astype(F32)
    pc[lax.rem(j + strips - 1, strips)] = below_ref[6:8].reshape(32, 128).astype(F32)
    pc[lax.rem(j + 1, strips)] = above_ref[2:4].reshape(32, 128).astype(F32)
    pc[lax.rem(j + 2, strips)] = mid_ref[...].reshape(32, 128).astype(F32)


def widen_cache(strips, j, cache, old_ref, below_ref, above_ref):
    has_above = jnp.where(j > 0, 1.0, 0.0)
    has_below = jnp.where(j < strips - 1, 1.0, 0.0)
    for f in range(2):
        cache[f, 304:416] = jnp.zeros((112, 128), F32)
        cache[f, 32:288] = old_ref[f].reshape(256, 128).astype(F32)
        cache[f, 0:32] = below_ref[2 * f : 2 * f + 2].reshape(32, 128).astype(F32) * has_above
        cache[f, 288:304] = above_ref[f].astype(F32) * has_below


def spread_matrix():
    lanes = iota((8, 1024), 1)
    pair, m = lanes >> 7, lanes & 127
    col = (m * 2428) >> 16
    tap = m - 27 * col
    a = (tap * 7282) >> 16
    b = ((tap - 9 * a) * 21846) >> 16
    c = tap - 9 * a - 3 * b
    w = 2 * pair - 1 + col
    source = jnp.where((m < 108) & (w >= 0) & (w < 16), (b * 3 + a) * 48 + c * 16 + w, -1)
    line = iota((54, 8, 1024), 0) * 8 + iota((54, 8, 1024), 1)
    return jnp.where(line == source[None], 1.0, 0.0).reshape(432, 1024).astype(BF16)


def norm_rows(strips, s1, s2, gain_ref, bias_ref):
    same = jnp.where(iota((128, 128), 0) // 4 == iota((128, 128), 1) // 4, 1.0, 0.0)
    count = strips * 16 * 16 * 4
    exact = functools.partial(
        jnp.dot, preferred_element_type=F32, precision=lax.Precision.HIGHEST
    )
    mean = exact(s1, same) / count
    inv = lax.rsqrt(exact(s2, same) / count - mean * mean + EPSILON)
    scale = inv * gain_ref[...].reshape(1, 128)
    return scale, bias_ref[...].reshape(1, 128) - mean * scale


def silu(v):
    h = 0.5 * v
    return h + h * jnp.tanh(h)


def pair_weight(conv_ref):
    zero = jnp.zeros((384, 128), BF16)

    def weight(b, e):
        if not 0 <= e <= 2:
            return zero
        return jnp.concatenate([conv_ref[a, b, e] for a in range(3)], axis=0)

    return jnp.concatenate(
        [
            jnp.concatenate([weight(b, col - k) for k in range(2)], axis=1)
            for col in range(4)
            for b in range(3)
        ],
        axis=0,
    )


def row_at(t, y):
    t = jnp.maximum(t, 0)
    h = 1 if y >= 8 else 0
    return (t & 1) * (16 * 88) + (y + 2 - 8 * h) * 8 + h * 4 + (t >> 1)


def stem_kernel(
    strips,
    scalars_ref,
    gain_ref,
    bias_ref,
    recv_ref,
    pix_ref,
    old_ref,
    below_ref,
    above_ref,
    mid_ref,
    weight_ref,
    pay_ref,
    act,
    stem,
    pc,
    zs,
    xs,
    ys,
):
    j = lax.axis_index("strip")
    valid = whole(scalars_ref, 0)
    rows_all = strips * 16
    gather_pixels(strips, j, pc, pix_ref, below_ref, above_ref, mid_ref)
    zs[:, 0:4] = jnp.zeros((3, 4, 8, 128), F32)
    zs[:, 4 + rows_all :] = jnp.zeros((3, 4, 8, 128), F32)
    sub = iota((128, 128), 0)
    crow, cframe = iota((128, 32), 1) % 16, iota((128, 32), 1) // 16
    csub = iota((128, 32), 0)
    for s in range(strips):
        pixels, slots = received(recv_ref[s])
        frame, row = slots >> 4, slots & 15
        source = jnp.concatenate([pixels, pc[s]], axis=0).astype(BF16)
        hits = []
        for a in range(3):
            t = frame + 2 - a
            place = jnp.where(t < FRAMES, row * 8 + (t & 1) * 4 + (t >> 1), -1)
            hit = jnp.where(sub.reshape(16, 8, 128) == place[None], 1.0, 0.0).reshape(128, 128)
            ct = cframe - a
            cplace = jnp.where(ct >= 0, crow * 8 + (ct & 1) * 4 + (ct >> 1), -1)
            chit = jnp.where(csub == cplace, 1.0, 0.0)
            hits.append(jnp.concatenate([hit, chit], axis=1).astype(BF16))
        placed = dot(jnp.concatenate(hits, axis=0), source).reshape(3, 16, 8, 128)
        for a in range(3):
            zs[a, 4 + s * 16 : 4 + (s + 1) * 16] = placed[a]
    pixels, slots = received(recv_ref[j])
    goal = (slots >> 4) + 2 - valid
    place = jnp.where((goal >= 0) & (goal < 2), goal * 16 + (slots & 15), -1)
    hit = jnp.where(iota((4, 8, 128), 0) * 8 + iota((4, 8, 128), 1) == place[None], 1.0, 0.0)
    cgoal = iota((32, 32), 1) // 16 - valid
    cplace = jnp.where((cgoal >= 0) & (cgoal < 2), cgoal * 16 + iota((32, 32), 1) % 16, -1)
    chit = jnp.where(iota((32, 32), 0) == cplace, 1.0, 0.0)
    source = jnp.concatenate([pixels, pc[j]], axis=0).astype(BF16)
    fresh = dot(jnp.concatenate([hit.reshape(32, 128), chit], axis=1).astype(BF16), source)
    target = whole(scalars_ref, 1).astype(F32)
    pay_ref[0:16] = jnp.full((16, 128), target, F32).astype(BF16)
    pay_ref[16:48] = fresh.astype(BF16)
    high = rows_all + 4
    for b in range(3):
        for a in range(3):
            q = (b * 3 + a) * 48
            xs[2 : high + 2, :, q : q + 48] = zs[a, 1 + b : high + 1 + b, :, 0:48]
    patches = xs[2 : high + 2].reshape(high * 8, 432).astype(BF16)
    ys[...] = dot(patches, spread_matrix()).reshape(high, 8, 1024)
    full = ys[2 : 2 + rows_all].reshape(rows_all * 8, 1024).astype(BF16)
    base = j * 16
    first, second = ys[pl.ds(base, 11)], ys[pl.ds(base + 8, 11)]
    low = iota((11, 8, 1024), 1) < 4
    own_even = jnp.where(low, first, pltpu.roll(second, 4, 1))
    own_odd = jnp.where(low, pltpu.roll(first, 4, 1), second)
    own = jnp.concatenate([own_even, own_odd], axis=0).reshape(176, 1024).astype(BF16)
    weight = weight_ref[...]
    s1 = jnp.zeros((8, 256), F32)
    s2 = jnp.zeros((8, 256), F32)
    for chunk in range(8):
        out = dot(full[:, chunk * 128 : chunk * 128 + 128], weight).astype(BF16).astype(F32).reshape(rows_all, 8, 256)
        s1 = s1 + jnp.sum(out, axis=0)
        s2 = s2 + jnp.sum(out * out, axis=0)
        mine = dot(own[:, chunk * 128 : chunk * 128 + 128], weight).astype(BF16).astype(F32).reshape(2, 11, 8, 256)
        for i in range(2):
            stem[:, 2 * chunk + i] = mine[:, :, :, i * 128 : (i + 1) * 128]
    s1 = s1[:, 0:128] + s1[:, 128:256]
    s2 = s2[:, 0:128] + s2[:, 128:256]
    scale, shift = norm_rows(strips, s1, s2, gain_ref, bias_ref)
    low8 = iota((8, 128), 0) < 4
    scales = (
        jnp.where(low8, scale, pltpu.roll(scale, 4, 0)),
        jnp.where(low8, pltpu.roll(scale, 4, 0), scale),
    )
    shifts = (
        jnp.where(low8, shift, pltpu.roll(shift, 4, 0)),
        jnp.where(low8, pltpu.roll(shift, 4, 0), shift),
    )
    half = iota((11, 8, 128), 1) // 4
    line_of = j * 16 + iota((11, 8, 128), 0) - 2 + 8 * half
    inside = jnp.where((line_of >= 0) & (line_of < rows_all), 1.0, 0.0)

    def activate(w, carry):
        for p in range(2):
            act[p, w] = silu(stem[p, w] * scales[p] + shifts[p]) * inside
        return carry

    lax.fori_loop(0, 16, activate, 0, unroll=4)
    act_rows = act.reshape(2 * 16 * 11 * 8, 128)
    for i in range(2):
        for y in range(16):
            block = act_rows[pl.ds(row_at(valid - 2 + i, y), 16, stride=88)]
            block = jnp.where(valid + i < 2, old_ref[1, y].astype(F32), block)
            to = 48 + i * 256 + y * 16
            pay_ref[to : to + 16] = block.astype(BF16)


def last_kernel(
    after_ref,
    scalars_ref,
    act,
    stem,
    old_ref,
    res_old_ref,
    below_ref,
    above_ref,
    conv_ref,
    pay_ref,
    lines,
):
    del after_ref
    j = lax.axis_index("strip")
    valid = whole(scalars_ref, 0)
    act_rows = act.reshape(2 * 16 * 11 * 8, 128)
    stem_rows = stem.reshape(2 * 16 * 11 * 8, 128)
    column = iota((16, 128), 0)

    def side_by_side(m, y, block):
        before = jnp.where(column == 0, 0.0, pltpu.roll(block, 1, 0))
        after = jnp.where(column == 15, 0.0, pltpu.roll(block, 15, 0))
        lines[m, y + 1] = jnp.concatenate([before, block, after], axis=1).astype(BF16)

    for m in range(4):
        from_cache = valid - 2 + m

        @pl.when(from_cache >= 2)
        def _(m=m, from_cache=from_cache):
            for y in range(-1, 17):
                block = act_rows[pl.ds(row_at(from_cache - 2, y), 16, stride=88)]
                side_by_side(m, y, block)

        @pl.when(from_cache < 2)
        def _(m=m, from_cache=from_cache):
            f = jnp.clip(from_cache, 0, 1)
            has_above = jnp.where(j > 0, 1.0, 0.0)
            has_below = jnp.where(j < lax.axis_size("strip") - 1, 1.0, 0.0)
            side_by_side(m, -1, below_ref[2 * f + 1].astype(F32) * has_above)
            for y in range(16):
                side_by_side(m, y, old_ref[f, y].astype(F32))
            side_by_side(m, 16, above_ref[f].astype(F32) * has_below)

    zero = jnp.zeros((384, 128), BF16)

    def weight(a, b):
        if not 0 <= b <= 2:
            return zero
        return jnp.concatenate([conv_ref[a, b, e] for e in range(3)], axis=0)

    weights = jnp.concatenate(
        [
            jnp.concatenate([weight(a, y - k) for k in range(2)], axis=1)
            for y in range(4)
            for a in range(3)
        ],
        axis=0,
    )
    left = jnp.concatenate(
        [
            jnp.concatenate(
                [lines[i + a, 2 * k + y] for i in range(2) for k in range(8)], axis=0
            )
            for y in range(4)
            for a in range(3)
        ],
        axis=1,
    )
    out = dot(left, weights).reshape(2, 8, 16, 256)
    for i in range(2):
        for y in range(16):
            block = stem_rows[pl.ds(row_at(valid - 2 + i, y), 16, stride=88)]
            block = block + out[i, y // 2, :, y % 2 * 128 : y % 2 * 128 + 128]
            if i == 0:
                block = jnp.where(valid < 2, res_old_ref[1, y].astype(F32), block)
            to = i * 256 + y * 16
            pay_ref[to : to + 16] = block.astype(BF16)


def conv_kernel(
    strips,
    w0,
    after_ref,
    after_too_ref,
    act,
    stem,
    old_ref,
    below_ref,
    above_ref,
    conv_ref,
    out_ref,
    cache,
    act3,
):
    del after_ref, after_too_ref
    j = lax.axis_index("strip")
    widen_cache(strips, j, cache, old_ref, below_ref, above_ref)
    at0 = iota((11, 8, 128), 1) == 0
    at4 = iota((11, 8, 128), 1) == 4
    edge = 0 if w0 == 0 else 9
    act3[edge] = jnp.zeros(act3.shape[1:], BF16)
    shift = 1 if w0 == 0 else 1 - w0

    def arrange(w, carry):
        late = []
        for f in range(2):
            rows = [
                jnp.broadcast_to(cache[f, pl.ds(y * 16 + w, 1)], (8, 128)) for y in range(19)
            ]
            upper, lower = jnp.stack(rows[0:11], axis=0), jnp.stack(rows[8:19], axis=0)
            rolled = pltpu.roll(act[f, w], 1, 1)
            late.append(jnp.where(at0, upper, jnp.where(at4, lower, rolled)))
        even, odd = act[0, w], act[1, w]
        taps = ((late[0], late[1]), (late[1], even), (even, odd))
        for a in range(3):
            act3[w + shift, :, :, a * 128 : (a + 1) * 128] = jnp.concatenate(taps[a], axis=1).astype(BF16)
        return carry

    lax.fori_loop(max(w0 - 1, 0), min(w0 + 9, 16), arrange, 0, unroll=3)
    weights = pair_weight(conv_ref)
    outside = (j == 0) & (iota((9, 16, 128), 0) == 0) & (iota((9, 16, 128), 1) % 8 < 4)
    keep = jnp.where(outside, 0.0, 1.0)
    left = jnp.concatenate(
        [
            jnp.concatenate(
                [act3[2 * k + col, b : b + 9].reshape(144, 384) for k in range(4)],
                axis=0,
            )
            for col in range(4)
            for b in range(3)
        ],
        axis=1,
    )
    out = dot(left, weights).reshape(4, 9, 16, 256)
    for k in range(4):
        for n in range(2):
            w = w0 + 2 * k + n
            value = out[k, :, :, n * 128 : n * 128 + 128]
            value = value + jnp.concatenate([stem[0, w, 1:10], stem[1, w, 1:10]], axis=1)
            out_ref[w - w0] = (value * keep).astype(BF16)


def down_kernel(
    scalars_ref,
    part_ref,
    rest_ref,
    down_ref,
    res_cache_ref,
    below_ref,
    after_ref,
    lat_ref,
    rcache,
    res3,
    lat,
):
    del after_ref
    j = lax.axis_index("strip")
    valid = whole(scalars_ref, 0)
    rcache[...] = jnp.zeros(rcache.shape, F32)
    has_above = jnp.where(j > 0, 1.0, 0.0)
    for f in range(2):
        rcache[f, 0:16] = below_ref[4 + f].astype(F32) * has_above
        rcache[f, 16:272] = res_cache_ref[f].reshape(256, 128).astype(F32)
    at0 = iota((9, 8, 128), 1) == 0
    at4 = iota((9, 8, 128), 1) == 4
    res3[0] = jnp.zeros(res3.shape[1:], F32)

    for w0, ref in ((0, part_ref), (8, rest_ref)):

        def delay(w, carry, w0=w0, ref=ref):
            both = ref[w].astype(F32)
            even, odd = both[:, 0:8], both[:, 8:16]
            olds = []
            for f in range(2):
                rows = [
                    jnp.broadcast_to(rcache[f, pl.ds(y * 16 + w0 + w, 1)], (8, 128))
                    for y in range(17)
                ]
                olds.append((jnp.stack(rows[0:9], axis=0), jnp.stack(rows[8:17], axis=0)))
            at = w0 + w + 1
            for f, v in enumerate((even, odd)):
                rolled = pltpu.roll(v, 1, 1)
                late = jnp.where(at0, olds[f][0], jnp.where(at4, olds[f][1], rolled))
                res3[at, :, :, f * 128 : f * 128 + 128] = late
            res3[at, :, :, 256:384] = even
            return carry

        lax.fori_loop(0, 8, delay, 0, unroll=2)
    total = jnp.zeros((256, 256), F32)
    for b in range(3):
        for e in range(3):
            left = jnp.concatenate(
                [res3[2 * k + e, 2 * i + b] for k in range(8) for i in range(4)], axis=0
            ).astype(BF16)
            right = jnp.concatenate([down_ref[a, b, e] for a in range(3)], axis=0)
            total = total + dot(left, right)
    live = 2 * (iota((256, 256), 0) % 4) < valid
    total = jnp.where(live, total, 0.0)
    for o in range(2):
        lat[o] = total[:, o * 128 : (o + 1) * 128]
    for t in range(4):
        for h in range(2):
            for i in range(4):
                for o in range(2):
                    block = lat[o, pl.ds(i * 8 + h * 4 + t, 8, stride=32)]
                    lat_ref[t, h * 4 + i, :, o * 128 : (o + 1) * 128] = block.astype(BF16)


def partner(value, axis, stride):
    pairs = [(source, source ^ stride) for source in range(lax.axis_size(axis))]
    return lax.ppermute(value, axis, pairs)


def shifted(value, axis, by):
    size = lax.axis_size(axis)
    return lax.ppermute(value, axis, [(i, (i + by) % size) for i in range(size)])


def body(
    loader_rows,
    load_owner,
    load_slot,
    valid_frames,
    next_owner,
    pixel_cache,
    act_cache,
    res_cache,
    stem_weight,
    norm_gain,
    norm_bias,
    conv_weight,
    down_weight,
):
    streams = lax.axis_size("stream")
    strips = lax.axis_size("strip")
    stream_pos = lax.axis_index("stream")
    sections = streams.bit_length() - 1
    fill = loader_rows.shape[1]
    per = fill // streams
    pix, acts, ress = pixel_cache[0], act_cache[0], res_cache[0]
    mega = 1024 * 1024
    cost = pl.CostEstimate(flops=2 * 10**9, bytes_accessed=4 * mega, transcendentals=0)
    half_per = fill // streams // 2
    direct = half_per % 8 == 0
    line_shape = (strips, streams, half_per, 128) if direct else (fill // 2, 128)
    lines = pl.pallas_call(
        functools.partial(sort_kernel, streams),
        out_shape=jax.ShapeDtypeStruct(line_shape, BF16),
        in_specs=[VM] * 3,
        out_specs=VM,
        scratch_shapes=[pltpu.VMEM((128, 2 * fill), F32)],
        cost_estimate=cost,
    )(loader_rows[0].T, load_owner, load_slot)
    if not direct:
        lines = lines.reshape(1, streams, half_per, 128)
        lines = jnp.broadcast_to(lines, (strips, streams, half_per, 128))
    lines = lines.reshape(strips * streams, half_per, 128)
    recv = lax.all_to_all(lines, ("strip", "stream"), 0, 0, tiled=True)
    recv = recv.reshape(strips, fill // 2, 128)
    below, above, mid, weight = pl.pallas_call(
        pack_kernel,
        out_shape=(
            jax.ShapeDtypeStruct((8, 16, 128), BF16),
            jax.ShapeDtypeStruct((4, 16, 128), BF16),
            jax.ShapeDtypeStruct((2, 16, 128), BF16),
            jax.ShapeDtypeStruct((128, 256), BF16),
        ),
        in_specs=[VM] * 2 + [ANY] * 2,
        out_specs=(VM,) * 4,
        scratch_shapes=[pltpu.VMEM((128, 256), F32), pltpu.SemaphoreType.DMA((6,))],
        compiler_params=pltpu.CompilerParams(vmem_limit_bytes=4 * mega),
    )(pix, stem_weight, acts, ress)
    below = shifted(below, "strip", 1)
    above = shifted(above, "strip", -1)
    mid = shifted(mid, "strip", 2)
    scalars = jnp.concatenate([valid_frames, next_owner, jnp.zeros((126,), jnp.int32)])
    rows_all = strips * 16
    window = jax.ShapeDtypeStruct((2, 16, 11, 8, 128), F32)
    first, act, stem = pl.pallas_call(
        functools.partial(stem_kernel, strips),
        out_shape=(jax.ShapeDtypeStruct((560, 128), BF16), window, window),
        in_specs=[VM] * 10,
        out_specs=(VM,) * 3,
        scratch_shapes=[
            pltpu.VMEM((strips, 32, 128), F32),
            pltpu.VMEM((3, rows_all + 8, 8, 128), F32),
            pltpu.VMEM((rows_all + 8, 8, 432), F32),
            pltpu.VMEM((rows_all + 4, 8, 1024), F32),
        ],
        compiler_params=pltpu.CompilerParams(vmem_limit_bytes=24 * mega),
        cost_estimate=cost,
    )(scalars, norm_gain, norm_bias, recv, pix, acts, below, above, mid, weight)
    keeps = []

    def passed(value, bit):
        if bit == len(keeps):
            keeps.append((value[0:1].astype(jnp.int32) >> bit) & 1 == (stream_pos >> bit) & 1)
        return jnp.where(keeps[bit], value, partner(value, "stream", 1 << bit))

    first = passed(first, 0)
    second = pl.pallas_call(
        last_kernel,
        out_shape=jax.ShapeDtypeStruct((512, 128), BF16),
        in_specs=[ANY] + [VM] * 8,
        out_specs=VM,
        scratch_shapes=[pltpu.VMEM((4, 18, 16, 384), BF16)],
        compiler_params=pltpu.CompilerParams(vmem_limit_bytes=24 * mega),
        cost_estimate=cost,
    )(first, scalars, act, stem, acts, ress, below, above, conv_weight)
    second = passed(second, 0)

    def convolved(w0, after, after_too):
        return pl.pallas_call(
            functools.partial(conv_kernel, strips, w0),
            out_shape=jax.ShapeDtypeStruct((8, 9, 16, 128), BF16),
            in_specs=[ANY] * 2 + [VM] * 6,
            out_specs=VM,
            scratch_shapes=[
                pltpu.VMEM((2, 416, 128), F32),
                pltpu.VMEM((10, 11, 16, 384), BF16),
            ],
            compiler_params=pltpu.CompilerParams(vmem_limit_bytes=24 * mega),
            cost_estimate=cost,
        )(after, after_too, act, stem, acts, below, above, conv_weight)

    part = convolved(0, first, second)
    for bit in range(1, sections - 1):
        first = passed(first, bit)
    rest = convolved(8, first, part)
    for bit in range(1, sections - 1):
        second = passed(second, bit)
    latent = pl.pallas_call(
        down_kernel,
        out_shape=jax.ShapeDtypeStruct((4, 8, 8, 256), BF16),
        in_specs=[VM] * 6 + [ANY],
        out_specs=VM,
        scratch_shapes=[
            pltpu.VMEM((2, 384, 128), F32),
            pltpu.VMEM((17, 9, 8, 384), F32),
            pltpu.VMEM((2, 256, 128), F32),
        ],
        compiler_params=pltpu.CompilerParams(vmem_limit_bytes=24 * mega),
        cost_estimate=cost,
    )(scalars, part, rest, down_weight, ress, below, second)
    if sections > 1:
        first = passed(first, sections - 1)
        second = passed(second, sections - 1)
    new_pix = first[16:48, 0:48].reshape(1, 2, 16, 48)
    new_act = first[48:].reshape(1, 2, 16, 16, 128)
    return (latent[None], new_pix, new_act, second.reshape(1, 2, 16, 16, 128))


def solution(mesh):
    in_specs = (
        P("stream", "strip", None),
        P("stream", "strip"),
        P("stream", "strip"),
        P("stream"),
        P("stream"),
        P("stream", None, "strip", None),
        P("stream", None, "strip", None, None),
        P("stream", None, "strip", None, None),
        P(),
        P(),
        P(),
        P(),
        P(),
    )
    out_specs = (
        P("stream", None, "strip", None, None),
        P("stream", None, "strip", None),
        P("stream", None, "strip", None, None),
        P("stream", None, "strip", None, None),
    )
    return jax.shard_map(body, mesh=mesh, in_specs=in_specs, out_specs=out_specs, check_vma=False)
```

```python
import functools

import jax
import jax.numpy as jnp
from jax import lax
from jax.experimental import pallas as pl
from jax.experimental.pallas import tpu as pltpu
from jax.sharding import PartitionSpec as P

FRAMES = 8
GROUPS = 32
EPSILON = 1e-06
F32 = jnp.float32
BF16 = jnp.bfloat16
VM = pl.BlockSpec(memory_space=pltpu.VMEM)
ANY = pl.BlockSpec(memory_space=pl.ANY)


def iota(shape, axis):
    return lax.broadcasted_iota(jnp.int32, shape, axis)


def whole(scalars_ref, which):
    row = scalars_ref[...].astype(F32).reshape(1, 128)
    return jnp.sum(jnp.where(iota((1, 128), 1) == which, row, 0.0)).astype(jnp.int32)


def dot(a, b):
    return jnp.dot(a, b, preferred_element_type=F32)


def dot_nt(a, b):
    return lax.dot_general(a, b, (((1,), (1,)), ((), ())), preferred_element_type=F32)


def sort_kernel(streams, cols_ref, owner_ref, slot_ref, out_ref, wide):
    width, fill = cols_ref.shape
    half_per = fill // streams // 2
    lines = fill // 2
    wide[...] = jnp.zeros(wide.shape, F32)
    pixels, slots = cols_ref[...].astype(F32), slot_ref[...].astype(F32)
    for side in range(2):
        at = side * 64
        wide[at : at + width, side * fill : (side + 1) * fill] = pixels
        wide[at + width : at + width + 1, side * fill : (side + 1) * fill] = slots
    owner = owner_ref[...]
    hot = jnp.where(iota((streams, fill), 0) == owner, 1.0, 0.0)
    upper = jnp.where(iota((fill, fill), 0) <= iota((fill, fill), 1), 1.0, 0.0).astype(BF16)
    running = dot(hot.astype(BF16), upper)
    rank = jnp.sum(hot * running, axis=0, keepdims=True).astype(jnp.int32) - 1
    half = rank // half_per
    line = owner * half_per + rank - half * half_per
    line = jnp.concatenate([jnp.where(half == side, line, -1) for side in range(2)], axis=1)
    pick = jnp.where(iota((lines, 2 * fill), 0) == jnp.broadcast_to(line, (lines, 2 * fill)), 1.0, 0.0)
    out = dot_nt(pick.astype(BF16), wide[...].astype(BF16)).astype(BF16)
    if len(out_ref.shape) == 2:
        out_ref[...] = out
    else:
        for strip in range(out_ref.shape[0]):
            out_ref[strip] = out.reshape(out_ref.shape[1:])


def pack_kernel(pix_ref, sw_ref, act_ref, res_ref, down_ref, up_ref, mid_ref, weight_ref, sw, sems):
    copies = []
    for f in range(2):
        copies.append((act_ref.at[f, 14:16], down_ref.at[2 * f : 2 * f + 2]))
        copies.append((res_ref.at[f, 15:16], down_ref.at[4 + f : 5 + f]))
        copies.append((act_ref.at[f, 0:1], up_ref.at[f : f + 1]))
    copies = [pltpu.make_async_copy(a, b, sems.at[i]) for i, (a, b) in enumerate(copies)]
    for copy in copies:
        copy.start()
    pix = pix_ref[...].reshape(32, 48).astype(F32)
    pix = jnp.concatenate([pix, jnp.zeros((32, 80), F32)], axis=1)
    pix = pix.astype(BF16).reshape(2, 16, 128)
    down_ref[6:8] = pix
    up_ref[2:4] = pix
    mid_ref[...] = pix
    sw[...] = jnp.zeros(sw.shape, F32)
    for k in range(2):
        for e in range(3):
            for a in range(3):
                for b in range(3):
                    at = 27 * (k + e) + 9 * a + 3 * b
                    sw[at : at + 3, k * 128 : k * 128 + 128] = sw_ref[a, b, e].astype(F32)
    weight_ref[...] = sw[...].astype(BF16)
    for copy in copies:
        copy.wait()


def received(line):
    line = line.astype(F32)
    both = jnp.concatenate([line, pltpu.roll(line, 64, 1)], axis=0)
    slot_lane = jnp.where(iota((8, 128), 1) == 48, 1.0, 0.0).astype(BF16)
    slots = dot_nt(slot_lane, both.astype(BF16)).astype(jnp.int32)
    return jnp.where(iota((128, 128), 1) < 48, both, 0.0), slots


def gather_pixels(strips, j, pc, pix_ref, below_ref, above_ref, mid_ref):
    pc[j] = jnp.zeros((32, 128), F32)
    pc[j, :, 0:48] = pix_ref[...].reshape(32, 48).astype(F32)
    pc[lax.rem(j + strips - 1, strips)] = below_ref[6:8].reshape(32, 128).astype(F32)
    pc[lax.rem(j + 1, strips)] = above_ref[2:4].reshape(32, 128).astype(F32)
    pc[lax.rem(j + 2, strips)] = mid_ref[...].reshape(32, 128).astype(F32)


def widen_cache(strips, j, cache, old_ref, below_ref, above_ref):
    has_above = jnp.where(j > 0, 1.0, 0.0)
    has_below = jnp.where(j < strips - 1, 1.0, 0.0)
    for f in range(2):
        cache[f, 304:416] = jnp.zeros((112, 128), F32)
        cache[f, 32:288] = old_ref[f].reshape(256, 128).astype(F32)
        cache[f, 0:32] = below_ref[2 * f : 2 * f + 2].reshape(32, 128).astype(F32) * has_above
        cache[f, 288:304] = above_ref[f].astype(F32) * has_below


def spread_matrix():
    lanes = iota((8, 1024), 1)
    pair, m = lanes >> 7, lanes & 127
    col = (m * 2428) >> 16
    tap = m - 27 * col
    a = (tap * 7282) >> 16
    b = ((tap - 9 * a) * 21846) >> 16
    c = tap - 9 * a - 3 * b
    w = 2 * pair - 1 + col
    source = jnp.where((m < 108) & (w >= 0) & (w < 16), (b * 3 + a) * 48 + c * 16 + w, -1)
    line = iota((54, 8, 1024), 0) * 8 + iota((54, 8, 1024), 1)
    return jnp.where(line == source[None], 1.0, 0.0).reshape(432, 1024).astype(BF16)


def norm_rows(strips, s1, s2, gain_ref, bias_ref):
    same = jnp.where(iota((128, 128), 0) // 4 == iota((128, 128), 1) // 4, 1.0, 0.0)
    count = strips * 16 * 16 * 4
    exact = functools.partial(
        jnp.dot, preferred_element_type=F32, precision=lax.Precision.HIGHEST
    )
    mean = exact(s1, same) / count
    inv = lax.rsqrt(exact(s2, same) / count - mean * mean + EPSILON)
    scale = inv * gain_ref[...].reshape(1, 128)
    return scale, bias_ref[...].reshape(1, 128) - mean * scale


def frame_row(rows, t):
    t = jnp.maximum(t, 0)
    mine = iota((8, 128), 0) == (t & 1) * 4 + (t >> 1)
    return jnp.sum(jnp.where(mine, rows, 0.0), axis=0, keepdims=True)


def silu(v):
    h = 0.5 * v
    return h + h * jnp.tanh(h)


def pair_weight(conv_ref):
    zero = jnp.zeros((384, 128), BF16)

    def weight(b, e):
        if not 0 <= e <= 2:
            return zero
        return jnp.concatenate([conv_ref[a, b, e] for a in range(3)], axis=0)

    return jnp.concatenate(
        [
            jnp.concatenate([weight(b, col - k) for k in range(2)], axis=1)
            for col in range(4)
            for b in range(3)
        ],
        axis=0,
    )


def row_at(t, y):
    t = jnp.maximum(t, 0)
    h = 1 if y >= 8 else 0
    return (t & 1) * (16 * 88) + (y + 2 - 8 * h) * 8 + h * 4 + (t >> 1)


def stem_kernel(
    strips,
    scalars_ref,
    gain_ref,
    bias_ref,
    recv_ref,
    pix_ref,
    old_ref,
    below_ref,
    above_ref,
    mid_ref,
    weight_ref,
    pay_ref,
    norm_ref,
    stem,
    pc,
    zs,
    xs,
    ys,
):
    j = lax.axis_index("strip")
    valid = whole(scalars_ref, 0)
    rows_all = strips * 16
    gather_pixels(strips, j, pc, pix_ref, below_ref, above_ref, mid_ref)
    zs[:, 0:4] = jnp.zeros((3, 4, 8, 128), F32)
    zs[:, 4 + rows_all :] = jnp.zeros((3, 4, 8, 128), F32)
    sub = iota((128, 128), 0)
    crow, cframe = iota((128, 32), 1) % 16, iota((128, 32), 1) // 16
    csub = iota((128, 32), 0)
    arrived = [received(recv_ref[s]) for s in range(strips)]
    old_hits = []
    for a in range(3):
        ct = cframe - a
        cplace = jnp.where(ct >= 0, crow * 8 + (ct & 1) * 4 + (ct >> 1), -1)
        old_hits.append(jnp.where(csub == cplace, 1.0, 0.0))
    picks = []
    for _, slots in arrived:
        frame, row = slots >> 4, slots & 15
        hits = []
        for a in range(3):
            t = frame + 2 - a
            place = jnp.where(t < FRAMES, row * 8 + (t & 1) * 4 + (t >> 1), -1)
            hit = jnp.where(sub.reshape(16, 8, 128) == place[None], 1.0, 0.0).reshape(128, 128)
            hits.append(jnp.concatenate([hit, old_hits[a]], axis=1).astype(BF16))
        picks.append(jnp.concatenate(hits, axis=0))
    sources = [
        jnp.concatenate([arrived[s][0], pc[s]], axis=0).astype(BF16) for s in range(strips)
    ]
    placed = [dot(picks[s], sources[s]).reshape(3, 16, 8, 128) for s in range(strips)]
    for s in range(strips):
        for a in range(3):
            zs[a, 4 + s * 16 : 4 + (s + 1) * 16] = placed[s][a]
    pixels, slots = received(recv_ref[j])
    goal = (slots >> 4) + 2 - valid
    place = jnp.where((goal >= 0) & (goal < 2), goal * 16 + (slots & 15), -1)
    hit = jnp.where(iota((4, 8, 128), 0) * 8 + iota((4, 8, 128), 1) == place[None], 1.0, 0.0)
    cgoal = iota((32, 32), 1) // 16 - valid
    cplace = jnp.where((cgoal >= 0) & (cgoal < 2), cgoal * 16 + iota((32, 32), 1) % 16, -1)
    chit = jnp.where(iota((32, 32), 0) == cplace, 1.0, 0.0)
    source = jnp.concatenate([pixels, pc[j]], axis=0).astype(BF16)
    fresh = dot(jnp.concatenate([hit.reshape(32, 128), chit], axis=1).astype(BF16), source)
    target = whole(scalars_ref, 1).astype(F32)
    pay_ref[0:16] = jnp.full((16, 128), target, F32).astype(BF16)
    pay_ref[16:48] = fresh.astype(BF16)
    high = rows_all + 4
    for b in range(3):
        for a in range(3):
            q = (b * 3 + a) * 48
            xs[2 : high + 2, :, q : q + 48] = zs[a, 1 + b : high + 1 + b, :, 0:48]
    patches = xs[2 : high + 2].reshape(high * 8, 432).astype(BF16)
    ys[...] = dot(patches, spread_matrix()).reshape(high, 8, 1024)
    full = ys[2 : 2 + rows_all].reshape(rows_all * 8, 1024).astype(BF16)
    base = j * 16
    first, second = ys[pl.ds(base, 11)], ys[pl.ds(base + 8, 11)]
    low = iota((11, 8, 1024), 1) < 4
    own_even = jnp.where(low, first, pltpu.roll(second, 4, 1))
    own_odd = jnp.where(low, pltpu.roll(first, 4, 1), second)
    own = jnp.concatenate([own_even, own_odd], axis=0).reshape(176, 1024).astype(BF16)
    weight = weight_ref[...]
    s1 = jnp.zeros((8, 256), F32)
    s2 = jnp.zeros((8, 256), F32)
    for chunk in range(8):
        out = dot(full[:, chunk * 128 : chunk * 128 + 128], weight).astype(BF16).astype(F32).reshape(rows_all, 8, 256)
        s1 = s1 + jnp.sum(out, axis=0)
        s2 = s2 + jnp.sum(out * out, axis=0)
        mine = dot(own[:, chunk * 128 : chunk * 128 + 128], weight).astype(BF16).astype(F32).reshape(2, 11, 8, 256)
        for i in range(2):
            stem[:, 2 * chunk + i] = mine[:, :, :, i * 128 : (i + 1) * 128]
    s1 = s1[:, 0:128] + s1[:, 128:256]
    s2 = s2[:, 0:128] + s2[:, 128:256]
    scale, shift = norm_rows(strips, s1, s2, gain_ref, bias_ref)
    norm_ref[0] = scale
    norm_ref[1] = shift
    stem_rows = stem.reshape(2 * 16 * 11 * 8, 128)
    for i in range(2):
        t = valid - 2 + i
        scale_i, shift_i = frame_row(scale, t), frame_row(shift, t)
        for y in range(16):
            block = stem_rows[pl.ds(row_at(t, y), 16, stride=88)]
            block = silu(block * scale_i + shift_i)
            block = jnp.where(valid + i < 2, old_ref[1, y].astype(F32), block)
            to = 48 + i * 256 + y * 16
            pay_ref[to : to + 16] = block.astype(BF16)


def last_kernel(
    scalars_ref,
    norm_ref,
    stem,
    old_ref,
    res_old_ref,
    below_ref,
    above_ref,
    conv_ref,
    pay_ref,
    lines,
):
    j = lax.axis_index("strip")
    valid = whole(scalars_ref, 0)
    scale, shift = norm_ref[0], norm_ref[1]
    has_above = jnp.where(j > 0, 1.0, 0.0)
    has_below = jnp.where(j < lax.axis_size("strip") - 1, 1.0, 0.0)
    stem_rows = stem.reshape(2 * 16 * 11 * 8, 128)
    column = iota((16, 128), 0)

    def side_by_side(m, y, block):
        before = jnp.where(column == 0, 0.0, pltpu.roll(block, 1, 0))
        after = jnp.where(column == 15, 0.0, pltpu.roll(block, 15, 0))
        lines[m, y + 1] = jnp.concatenate([before, block, after], axis=1).astype(BF16)

    for m in range(4):
        from_cache = valid - 2 + m

        @pl.when(from_cache >= 2)
        def _(m=m, from_cache=from_cache):
            t = from_cache - 2
            scale_m, shift_m = frame_row(scale, t), frame_row(shift, t)
            for y in range(-1, 17):
                block = stem_rows[pl.ds(row_at(t, y), 16, stride=88)]
                block = silu(block * scale_m + shift_m)
                if y < 0:
                    block = block * has_above
                if y > 15:
                    block = block * has_below
                side_by_side(m, y, block)

        @pl.when(from_cache < 2)
        def _(m=m, from_cache=from_cache):
            f = jnp.clip(from_cache, 0, 1)
            side_by_side(m, -1, below_ref[2 * f + 1].astype(F32) * has_above)
            for y in range(16):
                side_by_side(m, y, old_ref[f, y].astype(F32))
            side_by_side(m, 16, above_ref[f].astype(F32) * has_below)

    zero = jnp.zeros((384, 128), BF16)

    def weight(a, b):
        if not 0 <= b <= 2:
            return zero
        return jnp.concatenate([conv_ref[a, b, e] for e in range(3)], axis=0)

    weights = jnp.concatenate(
        [
            jnp.concatenate([weight(a, y - k) for k in range(2)], axis=1)
            for y in range(4)
            for a in range(3)
        ],
        axis=0,
    )
    left = jnp.concatenate(
        [
            jnp.concatenate(
                [lines[i + a, 2 * k + y] for i in range(2) for k in range(8)], axis=0
            )
            for y in range(4)
            for a in range(3)
        ],
        axis=1,
    )
    out = dot(left, weights).reshape(2, 8, 16, 256)
    for i in range(2):
        for y in range(16):
            block = stem_rows[pl.ds(row_at(valid - 2 + i, y), 16, stride=88)]
            block = block + out[i, y // 2, :, y % 2 * 128 : y % 2 * 128 + 128]
            if i == 0:
                block = jnp.where(valid < 2, res_old_ref[1, y].astype(F32), block)
            pay_ref[i * 16 + y] = block


def seal_kernel(after_ref, value_ref, out_ref):
    del after_ref
    out_ref[...] = value_ref[...].reshape(512, 128).astype(BF16)


def conv_kernel(
    strips,
    w0,
    after_ref,
    after_too_ref,
    norm_ref,
    stem,
    old_ref,
    below_ref,
    above_ref,
    conv_ref,
    out_ref,
    cache,
    act3,
):
    del after_ref, after_too_ref
    j = lax.axis_index("strip")
    widen_cache(strips, j, cache, old_ref, below_ref, above_ref)
    low8 = iota((8, 128), 0) < 4
    scales, shifts = [], []
    for k, rows in enumerate((scales, shifts)):
        v = norm_ref[k]
        rows.append(jnp.where(low8, v, pltpu.roll(v, 4, 0)))
        rows.append(jnp.where(low8, pltpu.roll(v, 4, 0), v))
    half = iota((11, 8, 128), 1) // 4
    line_of = j * 16 + iota((11, 8, 128), 0) - 2 + 8 * half
    inside = jnp.where((line_of >= 0) & (line_of < strips * 16), 1.0, 0.0)
    at0 = iota((11, 8, 128), 1) == 0
    at4 = iota((11, 8, 128), 1) == 4
    edge = 0 if w0 == 0 else 9
    act3[edge] = jnp.zeros(act3.shape[1:], BF16)
    shift = 1 if w0 == 0 else 1 - w0

    def arrange(w, carry):
        late = []
        even, odd = [silu(stem[p, w] * scales[p] + shifts[p]) * inside for p in range(2)]
        for f in range(2):
            rows = [
                jnp.broadcast_to(cache[f, pl.ds(y * 16 + w, 1)], (8, 128)) for y in range(19)
            ]
            upper, lower = jnp.stack(rows[0:11], axis=0), jnp.stack(rows[8:19], axis=0)
            rolled = pltpu.roll((even, odd)[f], 1, 1)
            late.append(jnp.where(at0, upper, jnp.where(at4, lower, rolled)))
        taps = ((late[0], late[1]), (late[1], even), (even, odd))
        for a in range(3):
            act3[w + shift, :, :, a * 128 : (a + 1) * 128] = jnp.concatenate(taps[a], axis=1).astype(BF16)
        return carry

    lax.fori_loop(max(w0 - 1, 0), min(w0 + 9, 16), arrange, 0, unroll=9)
    weights = pair_weight(conv_ref)
    outside = (j == 0) & (iota((9, 16, 128), 0) == 0) & (iota((9, 16, 128), 1) % 8 < 4)
    keep = jnp.where(outside, 0.0, 1.0)
    left = jnp.concatenate(
        [
            jnp.concatenate(
                [act3[2 * k + col, b : b + 9].reshape(144, 384) for k in range(4)],
                axis=0,
            )
            for col in range(4)
            for b in range(3)
        ],
        axis=1,
    )
    out = dot(left, weights).reshape(4, 9, 16, 256)
    for k in range(4):
        for n in range(2):
            w = w0 + 2 * k + n
            value = out[k, :, :, n * 128 : n * 128 + 128]
            value = value + jnp.concatenate([stem[0, w, 1:10], stem[1, w, 1:10]], axis=1)
            out_ref[w - w0] = (value * keep).astype(BF16)


def down_kernel(
    scalars_ref,
    part_ref,
    rest_ref,
    down_ref,
    res_cache_ref,
    below_ref,
    after_ref,
    lat_ref,
    rcache,
    res3,
    lat,
):
    del after_ref
    j = lax.axis_index("strip")
    valid = whole(scalars_ref, 0)
    rcache[...] = jnp.zeros(rcache.shape, F32)
    has_above = jnp.where(j > 0, 1.0, 0.0)
    for f in range(2):
        rcache[f, 0:16] = below_ref[4 + f].astype(F32) * has_above
        rcache[f, 16:272] = res_cache_ref[f].reshape(256, 128).astype(F32)
    at0 = iota((9, 8, 128), 1) == 0
    at4 = iota((9, 8, 128), 1) == 4
    res3[0] = jnp.zeros(res3.shape[1:], F32)

    for w0, ref in ((0, part_ref), (8, rest_ref)):

        def delay(w, carry, w0=w0, ref=ref):
            both = ref[w].astype(F32)
            even, odd = both[:, 0:8], both[:, 8:16]
            olds = []
            for f in range(2):
                rows = [
                    jnp.broadcast_to(rcache[f, pl.ds(y * 16 + w0 + w, 1)], (8, 128))
                    for y in range(17)
                ]
                olds.append((jnp.stack(rows[0:9], axis=0), jnp.stack(rows[8:17], axis=0)))
            at = w0 + w + 1
            for f, v in enumerate((even, odd)):
                rolled = pltpu.roll(v, 1, 1)
                late = jnp.where(at0, olds[f][0], jnp.where(at4, olds[f][1], rolled))
                res3[at, :, :, f * 128 : f * 128 + 128] = late
            res3[at, :, :, 256:384] = even
            return carry

        lax.fori_loop(0, 8, delay, 0, unroll=2)
    total = jnp.zeros((256, 256), F32)
    for b in range(3):
        for e in range(3):
            left = jnp.concatenate(
                [res3[2 * k + e, 2 * i + b] for k in range(8) for i in range(4)], axis=0
            ).astype(BF16)
            right = jnp.concatenate([down_ref[a, b, e] for a in range(3)], axis=0)
            total = total + dot(left, right)
    live = 2 * (iota((256, 256), 0) % 4) < valid
    total = jnp.where(live, total, 0.0)
    for o in range(2):
        lat[o] = total[:, o * 128 : (o + 1) * 128]
    for t in range(4):
        for h in range(2):
            for i in range(4):
                for o in range(2):
                    block = lat[o, pl.ds(i * 8 + h * 4 + t, 8, stride=32)]
                    lat_ref[t, h * 4 + i, :, o * 128 : (o + 1) * 128] = block.astype(BF16)


def finish_kernel(
    bit, first_ref, first_in_ref, second_ref, second_in_ref, new_pix_ref, new_act_ref, new_res_ref
):
    target = first_ref[0:16].astype(jnp.int32)
    mine = (target >> bit) & 1 == (lax.axis_index("stream") >> bit) & 1
    mine = jnp.where(mine, 1.0, 0.0)[0:1] > 0.5

    def chosen(own_ref, in_ref, start, stop):
        own, other = own_ref[start:stop].astype(F32), in_ref[start:stop].astype(F32)
        return jnp.where(mine, own, other).astype(BF16)

    new_pix_ref[...] = chosen(first_ref, first_in_ref, 16, 48)[:, 0:48].reshape(2, 16, 48)
    new_act_ref[...] = chosen(first_ref, first_in_ref, 48, 560).reshape(2, 16, 16, 128)
    new_res_ref[...] = chosen(second_ref, second_in_ref, 0, 512).reshape(2, 16, 16, 128)


def partner(value, axis, stride):
    pairs = [(source, source ^ stride) for source in range(lax.axis_size(axis))]
    return lax.ppermute(value, axis, pairs)


def shifted(value, axis, by):
    size = lax.axis_size(axis)
    return lax.ppermute(value, axis, [(i, (i + by) % size) for i in range(size)])


def body(
    loader_rows,
    load_owner,
    load_slot,
    valid_frames,
    next_owner,
    pixel_cache,
    act_cache,
    res_cache,
    stem_weight,
    norm_gain,
    norm_bias,
    conv_weight,
    down_weight,
):
    streams = lax.axis_size("stream")
    strips = lax.axis_size("strip")
    stream_pos = lax.axis_index("stream")
    sections = streams.bit_length() - 1
    fill = loader_rows.shape[1]
    per = fill // streams
    pix, acts, ress = pixel_cache[0], act_cache[0], res_cache[0]
    mega = 1024 * 1024
    cost = pl.CostEstimate(flops=2 * 10**9, bytes_accessed=4 * mega, transcendentals=0)
    half_per = fill // streams // 2
    direct = half_per % 8 == 0
    line_shape = (strips, streams, half_per, 128) if direct else (fill // 2, 128)
    lines = pl.pallas_call(
        functools.partial(sort_kernel, streams),
        out_shape=jax.ShapeDtypeStruct(line_shape, BF16),
        in_specs=[VM] * 3,
        out_specs=VM,
        scratch_shapes=[pltpu.VMEM((128, 2 * fill), F32)],
        cost_estimate=cost,
    )(loader_rows[0].T, load_owner, load_slot)
    if not direct:
        lines = lines.reshape(1, streams, half_per, 128)
        lines = jnp.broadcast_to(lines, (strips, streams, half_per, 128))
    lines = lines.reshape(strips * streams, half_per, 128)
    recv = lax.all_to_all(lines, ("strip", "stream"), 0, 0, tiled=True)
    recv = recv.reshape(strips, fill // 2, 128)
    below, above, mid, weight = pl.pallas_call(
        pack_kernel,
        out_shape=(
            jax.ShapeDtypeStruct((8, 16, 128), BF16),
            jax.ShapeDtypeStruct((4, 16, 128), BF16),
            jax.ShapeDtypeStruct((2, 16, 128), BF16),
            jax.ShapeDtypeStruct((128, 256), BF16),
        ),
        in_specs=[VM] * 2 + [ANY] * 2,
        out_specs=(VM,) * 4,
        scratch_shapes=[pltpu.VMEM((128, 256), F32), pltpu.SemaphoreType.DMA((6,))],
        compiler_params=pltpu.CompilerParams(vmem_limit_bytes=4 * mega),
    )(pix, stem_weight, acts, ress)
    below = shifted(below, "strip", 1)
    above = shifted(above, "strip", -1)
    mid = shifted(mid, "strip", 2)
    scalars = jnp.concatenate([valid_frames, next_owner, jnp.zeros((126,), jnp.int32)])
    rows_all = strips * 16
    window = jax.ShapeDtypeStruct((2, 16, 11, 8, 128), F32)
    first, norm, stem = pl.pallas_call(
        functools.partial(stem_kernel, strips),
        out_shape=(
            jax.ShapeDtypeStruct((560, 128), BF16),
            jax.ShapeDtypeStruct((2, 8, 128), F32),
            window,
        ),
        in_specs=[VM] * 10,
        out_specs=(VM,) * 3,
        scratch_shapes=[
            pltpu.VMEM((strips, 32, 128), F32),
            pltpu.VMEM((3, rows_all + 8, 8, 128), F32),
            pltpu.VMEM((rows_all + 8, 8, 432), F32),
            pltpu.VMEM((rows_all + 4, 8, 1024), F32),
        ],
        compiler_params=pltpu.CompilerParams(vmem_limit_bytes=24 * mega),
        cost_estimate=cost,
    )(scalars, norm_gain, norm_bias, recv, pix, acts, below, above, mid, weight)
    keeps = []

    def passed(value, bit):
        if bit == len(keeps):
            keeps.append((value[0:1].astype(jnp.int32) >> bit) & 1 == (stream_pos >> bit) & 1)
        return jnp.where(keeps[bit], value, partner(value, "stream", 1 << bit))

    second = pl.pallas_call(
        last_kernel,
        out_shape=jax.ShapeDtypeStruct((32, 16, 128), F32),
        in_specs=[VM] * 8,
        out_specs=VM,
        scratch_shapes=[pltpu.VMEM((4, 18, 16, 384), BF16)],
        compiler_params=pltpu.CompilerParams(vmem_limit_bytes=24 * mega),
        cost_estimate=cost,
    )(scalars, norm, stem, acts, ress, below, above, conv_weight)
    first = passed(first, 0)
    second = pl.pallas_call(
        seal_kernel,
        out_shape=jax.ShapeDtypeStruct((512, 128), BF16),
        in_specs=[ANY, VM],
        out_specs=VM,
        compiler_params=pltpu.CompilerParams(vmem_limit_bytes=8 * mega),
    )(first, second)
    second = passed(second, 0)

    def convolved(w0, after, after_too):
        return pl.pallas_call(
            functools.partial(conv_kernel, strips, w0),
            out_shape=jax.ShapeDtypeStruct((8, 9, 16, 128), BF16),
            in_specs=[ANY] * 2 + [VM] * 6,
            out_specs=VM,
            scratch_shapes=[
                pltpu.VMEM((2, 416, 128), F32),
                pltpu.VMEM((10, 11, 16, 384), BF16),
            ],
            compiler_params=pltpu.CompilerParams(vmem_limit_bytes=24 * mega),
            cost_estimate=cost,
        )(after, after_too, norm, stem, acts, below, above, conv_weight)

    part = convolved(0, first, second)
    for bit in range(1, sections - 1):
        first = passed(first, bit)
    rest = convolved(8, first, part)
    for bit in range(1, sections - 1):
        second = passed(second, bit)
    latent = pl.pallas_call(
        down_kernel,
        out_shape=jax.ShapeDtypeStruct((4, 8, 8, 256), BF16),
        in_specs=[VM] * 6 + [ANY],
        out_specs=VM,
        scratch_shapes=[
            pltpu.VMEM((2, 384, 128), F32),
            pltpu.VMEM((17, 9, 8, 384), F32),
            pltpu.VMEM((2, 256, 128), F32),
        ],
        compiler_params=pltpu.CompilerParams(vmem_limit_bytes=24 * mega),
        cost_estimate=cost,
    )(scalars, part, rest, down_weight, ress, below, second)
    bit = sections - 1
    new_pix, new_act, new_res = pl.pallas_call(
        functools.partial(finish_kernel, bit),
        out_shape=(
            jax.ShapeDtypeStruct(pix.shape, BF16),
            jax.ShapeDtypeStruct(acts.shape, BF16),
            jax.ShapeDtypeStruct(ress.shape, BF16),
        ),
        in_specs=[VM] * 4,
        out_specs=(VM,) * 3,
        compiler_params=pltpu.CompilerParams(vmem_limit_bytes=8 * mega),
    )(
        first,
        partner(first, "stream", 1 << bit),
        second,
        partner(second, "stream", 1 << bit),
    )
    return (latent[None], new_pix[None], new_act[None], new_res[None])


def solution(mesh):
    in_specs = (
        P("stream", "strip", None),
        P("stream", "strip"),
        P("stream", "strip"),
        P("stream"),
        P("stream"),
        P("stream", None, "strip", None),
        P("stream", None, "strip", None, None),
        P("stream", None, "strip", None, None),
        P(),
        P(),
        P(),
        P(),
        P(),
    )
    out_specs = (
        P("stream", None, "strip", None, None),
        P("stream", None, "strip", None),
        P("stream", None, "strip", None, None),
        P("stream", None, "strip", None, None),
    )
    return jax.shard_map(body, mesh=mesh, in_specs=in_specs, out_specs=out_specs, check_vma=False)
```

```python
import functools

import jax
import jax.numpy as jnp
from jax import lax
from jax.experimental import pallas as pl
from jax.experimental.pallas import tpu as pltpu
from jax.sharding import PartitionSpec as P

FRAMES = 8
GROUPS = 32
EPSILON = 1e-06
F32 = jnp.float32
BF16 = jnp.bfloat16
VM = pl.BlockSpec(memory_space=pltpu.VMEM)
ANY = pl.BlockSpec(memory_space=pl.ANY)


def iota(shape, axis):
    return lax.broadcasted_iota(jnp.int32, shape, axis)


def whole(scalars_ref, which):
    row = scalars_ref[...].astype(F32).reshape(1, 128)
    return jnp.sum(jnp.where(iota((1, 128), 1) == which, row, 0.0)).astype(jnp.int32)


def dot(a, b):
    return jnp.dot(a, b, preferred_element_type=F32)


def dot_nt(a, b):
    return lax.dot_general(a, b, (((1,), (1,)), ((), ())), preferred_element_type=F32)


def sort_kernel(streams, cols_ref, owner_ref, slot_ref, out_ref, wide):
    width, fill = cols_ref.shape
    half_per = fill // streams // 2
    lines = fill // 2
    wide[...] = jnp.zeros(wide.shape, F32)
    pixels, slots = cols_ref[...].astype(F32), slot_ref[...].astype(F32)
    for side in range(2):
        at = side * 64
        wide[at : at + width, side * fill : (side + 1) * fill] = pixels
        wide[at + width : at + width + 1, side * fill : (side + 1) * fill] = slots
    owner = owner_ref[...]
    hot = jnp.where(iota((streams, fill), 0) == owner, 1.0, 0.0)
    upper = jnp.where(iota((fill, fill), 0) <= iota((fill, fill), 1), 1.0, 0.0).astype(BF16)
    running = dot(hot.astype(BF16), upper)
    rank = jnp.sum(hot * running, axis=0, keepdims=True).astype(jnp.int32) - 1
    half = rank // half_per
    line = owner * half_per + rank - half * half_per
    line = jnp.concatenate([jnp.where(half == side, line, -1) for side in range(2)], axis=1)
    pick = jnp.where(iota((lines, 2 * fill), 0) == jnp.broadcast_to(line, (lines, 2 * fill)), 1.0, 0.0)
    out = dot_nt(pick.astype(BF16), wide[...].astype(BF16)).astype(BF16)
    if len(out_ref.shape) == 2:
        out_ref[...] = out
    else:
        for strip in range(out_ref.shape[0]):
            out_ref[strip] = out.reshape(out_ref.shape[1:])


def pack_kernel(pix_ref, sw_ref, act_ref, res_ref, down_ref, up_ref, near_ref, mid_ref, weight_ref, sw, sems):
    copies = []
    for f in range(2):
        copies.append((act_ref.at[f, 14:16], down_ref.at[2 * f : 2 * f + 2]))
        copies.append((res_ref.at[f, 15:16], down_ref.at[4 + f : 5 + f]))
        copies.append((act_ref.at[f, 0:1], up_ref.at[f : f + 1]))
    copies = [pltpu.make_async_copy(a, b, sems.at[i]) for i, (a, b) in enumerate(copies)]
    for copy in copies:
        copy.start()
    pix = pix_ref[...].reshape(32, 48).astype(F32)
    pix = jnp.concatenate([pix, jnp.zeros((32, 80), F32)], axis=1)
    pix = pix.astype(BF16).reshape(2, 16, 128)
    near_ref[...] = pix
    up_ref[2:4] = pix
    mid_ref[...] = pix
    sw[...] = jnp.zeros(sw.shape, F32)
    for k in range(2):
        for e in range(3):
            for a in range(3):
                for b in range(3):
                    at = 27 * (k + e) + 9 * a + 3 * b
                    sw[at : at + 3, k * 128 : k * 128 + 128] = sw_ref[a, b, e].astype(F32)
    weight_ref[...] = sw[...].astype(BF16)
    for copy in copies:
        copy.wait()


def received(line):
    line = line.astype(F32)
    both = jnp.concatenate([line, pltpu.roll(line, 64, 1)], axis=0)
    slot_lane = jnp.where(iota((8, 128), 1) == 48, 1.0, 0.0).astype(BF16)
    slots = dot_nt(slot_lane, both.astype(BF16)).astype(jnp.int32)
    return jnp.where(iota((128, 128), 1) < 48, both, 0.0), slots


def gather_pixels(strips, j, pc, pix_ref, below_ref, above_ref, mid_ref):
    pc[j] = jnp.zeros((32, 128), F32)
    pc[j, :, 0:48] = pix_ref[...].reshape(32, 48).astype(F32)
    pc[lax.rem(j + strips - 1, strips)] = below_ref[...].reshape(32, 128).astype(F32)
    pc[lax.rem(j + 1, strips)] = above_ref[2:4].reshape(32, 128).astype(F32)
    pc[lax.rem(j + 2, strips)] = mid_ref[...].reshape(32, 128).astype(F32)


def widen_cache(strips, j, cache, old_ref, below_ref, above_ref):
    has_above = jnp.where(j > 0, 1.0, 0.0)
    has_below = jnp.where(j < strips - 1, 1.0, 0.0)
    for f in range(2):
        cache[f, 304:416] = jnp.zeros((112, 128), F32)
        cache[f, 32:288] = old_ref[f].reshape(256, 128).astype(F32)
        cache[f, 0:32] = below_ref[2 * f : 2 * f + 2].reshape(32, 128).astype(F32) * has_above
        cache[f, 288:304] = above_ref[f].astype(F32) * has_below


def spread_matrix():
    lanes = iota((8, 1024), 1)
    pair, m = lanes >> 7, lanes & 127
    col = (m * 2428) >> 16
    tap = m - 27 * col
    a = (tap * 7282) >> 16
    b = ((tap - 9 * a) * 21846) >> 16
    c = tap - 9 * a - 3 * b
    w = 2 * pair - 1 + col
    source = jnp.where((m < 108) & (w >= 0) & (w < 16), (b * 3 + a) * 48 + c * 16 + w, -1)
    line = iota((54, 8, 1024), 0) * 8 + iota((54, 8, 1024), 1)
    return jnp.where(line == source[None], 1.0, 0.0).reshape(432, 1024).astype(BF16)


def norm_rows(strips, s1, s2, gain_ref, bias_ref):
    same = jnp.where(iota((128, 128), 0) // 4 == iota((128, 128), 1) // 4, 1.0, 0.0)
    count = strips * 16 * 16 * 4
    exact = functools.partial(
        jnp.dot, preferred_element_type=F32, precision=lax.Precision.HIGHEST
    )
    mean = exact(s1, same) / count
    inv = lax.rsqrt(exact(s2, same) / count - mean * mean + EPSILON)
    scale = inv * gain_ref[...].reshape(1, 128)
    return scale, bias_ref[...].reshape(1, 128) - mean * scale


def frame_row(rows, t):
    t = jnp.maximum(t, 0)
    mine = iota((8, 128), 0) == (t & 1) * 4 + (t >> 1)
    return jnp.sum(jnp.where(mine, rows, 0.0), axis=0, keepdims=True)


def silu(v):
    h = 0.5 * v
    return h + h * jnp.tanh(h)


def pair_weight(conv_ref):
    zero = jnp.zeros((384, 128), BF16)

    def weight(b, e):
        if not 0 <= e <= 2:
            return zero
        return jnp.concatenate([conv_ref[a, b, e] for a in range(3)], axis=0)

    return jnp.concatenate(
        [
            jnp.concatenate([weight(b, col - k) for k in range(2)], axis=1)
            for col in range(4)
            for b in range(3)
        ],
        axis=0,
    )


def row_at(t, y):
    t = jnp.maximum(t, 0)
    h = 1 if y >= 8 else 0
    return (t & 1) * (16 * 88) + (y + 2 - 8 * h) * 8 + h * 4 + (t >> 1)


def stem_kernel(
    strips,
    scalars_ref,
    gain_ref,
    bias_ref,
    recv_ref,
    pix_ref,
    old_ref,
    below_ref,
    above_ref,
    mid_ref,
    weight_ref,
    pay_ref,
    norm_ref,
    stem,
    pc,
    zs,
    xs,
    ys,
):
    j = lax.axis_index("strip")
    valid = whole(scalars_ref, 0)
    rows_all = strips * 16
    gather_pixels(strips, j, pc, pix_ref, below_ref, above_ref, mid_ref)
    zs[:, 0:4] = jnp.zeros((3, 4, 8, 128), F32)
    zs[:, 4 + rows_all :] = jnp.zeros((3, 12, 8, 128), F32)
    sub = iota((128, 128), 0)
    crow, cframe = iota((128, 32), 1) % 16, iota((128, 32), 1) // 16
    csub = iota((128, 32), 0)
    arrived = [received(recv_ref[s]) for s in range(strips)]
    old_hits = []
    for a in range(3):
        ct = cframe - a
        cplace = jnp.where(ct >= 0, crow * 8 + (ct & 1) * 4 + (ct >> 1), -1)
        old_hits.append(jnp.where(csub == cplace, 1.0, 0.0))
    picks = []
    for _, slots in arrived:
        frame, row = slots >> 4, slots & 15
        hits = []
        for a in range(3):
            t = frame + 2 - a
            place = jnp.where(t < FRAMES, row * 8 + (t & 1) * 4 + (t >> 1), -1)
            hit = jnp.where(sub.reshape(16, 8, 128) == place[None], 1.0, 0.0).reshape(128, 128)
            hits.append(jnp.concatenate([hit, old_hits[a]], axis=1).astype(BF16))
        picks.append(jnp.concatenate(hits, axis=0))
    sources = [
        jnp.concatenate([arrived[s][0], pc[s]], axis=0).astype(BF16) for s in range(strips)
    ]
    placed = [dot(picks[s], sources[s]).reshape(3, 16, 8, 128) for s in range(strips)]
    for s in range(strips):
        for a in range(3):
            zs[a, 4 + s * 16 : 4 + (s + 1) * 16] = placed[s][a]
    target = whole(scalars_ref, 1).astype(F32)
    pay_ref[0:16] = jnp.full((16, 128), target, F32).astype(BF16)
    last = valid - 1
    line_rows = zs.reshape(3 * (rows_all + 16) * 8, 128)
    lines = []
    for a in range(3):
        at = (a * (rows_all + 16) + 3 + j * 16) * 8 + (last & 1) * 4 + (last >> 1)
        lines.append(line_rows[pl.ds(at, 24, stride=8)])
    none = jnp.zeros((8, 128), F32)
    left = jnp.where(iota((24, 128), 1) < 64, lines[0], pltpu.roll(lines[1], 64, 1))
    pay_ref[16:48] = jnp.concatenate([left, none], axis=0).astype(BF16)
    pay_ref[48:80] = jnp.concatenate([lines[2], none], axis=0).astype(BF16)
    high = rows_all + 4
    for b in range(3):
        for a in range(3):
            q = (b * 3 + a) * 48
            xs[2 : high + 2, :, q : q + 48] = zs[a, 1 + b : high + 1 + b, :, 0:48]
    patches = xs[2 : high + 2].reshape(high * 8, 432).astype(BF16)
    ys[...] = dot(patches, spread_matrix()).reshape(high, 8, 1024)
    full = ys[2 : 2 + rows_all].reshape(rows_all * 8, 1024).astype(BF16)
    base = j * 16
    first, second = ys[pl.ds(base, 11)], ys[pl.ds(base + 8, 11)]
    low = iota((11, 8, 1024), 1) < 4
    own_even = jnp.where(low, first, pltpu.roll(second, 4, 1))
    own_odd = jnp.where(low, pltpu.roll(first, 4, 1), second)
    own = jnp.concatenate([own_even, own_odd], axis=0).reshape(176, 1024).astype(BF16)
    weight = weight_ref[...]
    s1 = jnp.zeros((8, 256), F32)
    s2 = jnp.zeros((8, 256), F32)
    for chunk in range(8):
        out = dot(full[:, chunk * 128 : chunk * 128 + 128], weight).astype(BF16).astype(F32).reshape(rows_all, 8, 256)
        s1 = s1 + jnp.sum(out, axis=0)
        s2 = s2 + jnp.sum(out * out, axis=0)
        mine = dot(own[:, chunk * 128 : chunk * 128 + 128], weight).astype(BF16).astype(F32).reshape(2, 11, 8, 256)
        for i in range(2):
            stem[:, 2 * chunk + i] = mine[:, :, :, i * 128 : (i + 1) * 128]
    s1 = s1[:, 0:128] + s1[:, 128:256]
    s2 = s2[:, 0:128] + s2[:, 128:256]
    scale, shift = norm_rows(strips, s1, s2, gain_ref, bias_ref)
    norm_ref[0] = scale
    norm_ref[1] = shift
    stem_rows = stem.reshape(2 * 16 * 11 * 8, 128)
    t = valid - 2
    scale_t, shift_t = frame_row(scale, t), frame_row(shift, t)
    for y in range(16):
        block = silu(stem_rows[pl.ds(row_at(t, y), 16, stride=88)] * scale_t + shift_t)
        block = jnp.where(valid < 2, old_ref[1, y].astype(F32), block)
        pay_ref[80 + y * 16 : 96 + y * 16] = block.astype(BF16)
    pieces = []
    for row in (frame_row(scale, last), frame_row(shift, last)):
        for _ in range(3):
            piece = row.astype(BF16).astype(F32)
            pieces.append(piece)
            row = row - piece
    row16 = iota((16, 128), 0)
    norms = jnp.zeros((16, 128), F32)
    for n, piece in enumerate(pieces):
        norms = jnp.where(row16 == n, piece, norms)
    pay_ref[336:352] = norms.astype(BF16)


def last_kernel(
    scalars_ref,
    norm_ref,
    stem,
    old_ref,
    res_old_ref,
    below_ref,
    above_ref,
    conv_ref,
    pay_ref,
    lines,
):
    j = lax.axis_index("strip")
    valid = whole(scalars_ref, 0)
    scale, shift = norm_ref[0], norm_ref[1]
    has_above = jnp.where(j > 0, 1.0, 0.0)
    has_below = jnp.where(j < lax.axis_size("strip") - 1, 1.0, 0.0)
    stem_rows = stem.reshape(2 * 16 * 11 * 8, 128)
    column = iota((16, 128), 0)

    def side_by_side(m, y, block):
        before = jnp.where(column == 0, 0.0, pltpu.roll(block, 1, 0))
        after = jnp.where(column == 15, 0.0, pltpu.roll(block, 15, 0))
        lines[m, y + 1] = jnp.concatenate([before, block, after], axis=1).astype(BF16)

    for m in range(4):
        from_cache = valid - 2 + m

        @pl.when(from_cache >= 2)
        def _(m=m, from_cache=from_cache):
            t = from_cache - 2
            scale_m, shift_m = frame_row(scale, t), frame_row(shift, t)
            for y in range(-1, 17):
                block = stem_rows[pl.ds(row_at(t, y), 16, stride=88)]
                block = silu(block * scale_m + shift_m)
                if y < 0:
                    block = block * has_above
                if y > 15:
                    block = block * has_below
                side_by_side(m, y, block)

        @pl.when(from_cache < 2)
        def _(m=m, from_cache=from_cache):
            f = jnp.clip(from_cache, 0, 1)
            side_by_side(m, -1, below_ref[2 * f + 1].astype(F32) * has_above)
            for y in range(16):
                side_by_side(m, y, old_ref[f, y].astype(F32))
            side_by_side(m, 16, above_ref[f].astype(F32) * has_below)

    zero = jnp.zeros((384, 128), BF16)

    def weight(a, b):
        if not 0 <= b <= 2:
            return zero
        return jnp.concatenate([conv_ref[a, b, e] for e in range(3)], axis=0)

    weights = jnp.concatenate(
        [
            jnp.concatenate([weight(a, y - k) for k in range(2)], axis=1)
            for y in range(4)
            for a in range(3)
        ],
        axis=0,
    )
    left = jnp.concatenate(
        [
            jnp.concatenate(
                [lines[i + a, 2 * k + y] for i in range(2) for k in range(8)], axis=0
            )
            for y in range(4)
            for a in range(3)
        ],
        axis=1,
    )
    out = dot(left, weights).reshape(2, 8, 16, 256)
    for i in range(2):
        for y in range(16):
            block = stem_rows[pl.ds(row_at(valid - 2 + i, y), 16, stride=88)]
            block = block + out[i, y // 2, :, y % 2 * 128 : y % 2 * 128 + 128]
            if i == 0:
                block = jnp.where(valid < 2, res_old_ref[1, y].astype(F32), block)
            pay_ref[i * 16 + y] = block


def seal_kernel(after_ref, value_ref, out_ref):
    del after_ref
    out_ref[...] = value_ref[...].reshape(512, 128).astype(BF16)


def conv_kernel(
    strips,
    w0,
    after_ref,
    after_too_ref,
    norm_ref,
    stem,
    old_ref,
    below_ref,
    above_ref,
    conv_ref,
    out_ref,
    rows_ref,
    cache,
    act3,
):
    del after_too_ref
    rows_ref[...] = after_ref[0:16] if w0 == 0 else jnp.zeros((16, 128), BF16)
    j = lax.axis_index("strip")
    widen_cache(strips, j, cache, old_ref, below_ref, above_ref)
    low8 = iota((8, 128), 0) < 4
    scales, shifts = [], []
    for k, rows in enumerate((scales, shifts)):
        v = norm_ref[k]
        rows.append(jnp.where(low8, v, pltpu.roll(v, 4, 0)))
        rows.append(jnp.where(low8, pltpu.roll(v, 4, 0), v))
    half = iota((11, 8, 128), 1) // 4
    line_of = j * 16 + iota((11, 8, 128), 0) - 2 + 8 * half
    inside = jnp.where((line_of >= 0) & (line_of < strips * 16), 1.0, 0.0)
    at0 = iota((11, 8, 128), 1) == 0
    at4 = iota((11, 8, 128), 1) == 4
    edge = 0 if w0 == 0 else 9
    act3[edge] = jnp.zeros(act3.shape[1:], BF16)
    shift = 1 if w0 == 0 else 1 - w0

    def arrange(w, carry):
        late = []
        even, odd = [silu(stem[p, w] * scales[p] + shifts[p]) * inside for p in range(2)]
        for f in range(2):
            rows = [
                jnp.broadcast_to(cache[f, pl.ds(y * 16 + w, 1)], (8, 128)) for y in range(19)
            ]
            upper, lower = jnp.stack(rows[0:11], axis=0), jnp.stack(rows[8:19], axis=0)
            rolled = pltpu.roll((even, odd)[f], 1, 1)
            late.append(jnp.where(at0, upper, jnp.where(at4, lower, rolled)))
        taps = ((late[0], late[1]), (late[1], even), (even, odd))
        for a in range(3):
            act3[w + shift, :, :, a * 128 : (a + 1) * 128] = jnp.concatenate(taps[a], axis=1).astype(BF16)
        return carry

    lax.fori_loop(max(w0 - 1, 0), min(w0 + 9, 16), arrange, 0, unroll=9)
    weights = pair_weight(conv_ref)
    outside = (j == 0) & (iota((9, 16, 128), 0) == 0) & (iota((9, 16, 128), 1) % 8 < 4)
    keep = jnp.where(outside, 0.0, 1.0)
    left = jnp.concatenate(
        [
            jnp.concatenate(
                [act3[2 * k + col, b : b + 9].reshape(144, 384) for k in range(4)],
                axis=0,
            )
            for col in range(4)
            for b in range(3)
        ],
        axis=1,
    )
    out = dot(left, weights).reshape(4, 9, 16, 256)
    for k in range(4):
        for n in range(2):
            w = w0 + 2 * k + n
            value = out[k, :, :, n * 128 : n * 128 + 128]
            value = value + jnp.concatenate([stem[0, w, 1:10], stem[1, w, 1:10]], axis=1)
            out_ref[w - w0] = (value * keep).astype(BF16)


def down_kernel(
    scalars_ref,
    part_ref,
    rest_ref,
    down_ref,
    res_cache_ref,
    below_ref,
    after_ref,
    lat_ref,
    rcache,
    res3,
    lat,
):
    del after_ref
    j = lax.axis_index("strip")
    valid = whole(scalars_ref, 0)
    rcache[...] = jnp.zeros(rcache.shape, F32)
    has_above = jnp.where(j > 0, 1.0, 0.0)
    for f in range(2):
        rcache[f, 0:16] = below_ref[4 + f].astype(F32) * has_above
        rcache[f, 16:272] = res_cache_ref[f].reshape(256, 128).astype(F32)
    at0 = iota((9, 8, 128), 1) == 0
    at4 = iota((9, 8, 128), 1) == 4
    res3[0] = jnp.zeros(res3.shape[1:], F32)

    for w0, ref in ((0, part_ref), (8, rest_ref)):

        def delay(w, carry, w0=w0, ref=ref):
            both = ref[w].astype(F32)
            even, odd = both[:, 0:8], both[:, 8:16]
            olds = []
            for f in range(2):
                rows = [
                    jnp.broadcast_to(rcache[f, pl.ds(y * 16 + w0 + w, 1)], (8, 128))
                    for y in range(17)
                ]
                olds.append((jnp.stack(rows[0:9], axis=0), jnp.stack(rows[8:17], axis=0)))
            at = w0 + w + 1
            for f, v in enumerate((even, odd)):
                rolled = pltpu.roll(v, 1, 1)
                late = jnp.where(at0, olds[f][0], jnp.where(at4, olds[f][1], rolled))
                res3[at, :, :, f * 128 : f * 128 + 128] = late
            res3[at, :, :, 256:384] = even
            return carry

        lax.fori_loop(0, 8, delay, 0, unroll=8)
    total = jnp.zeros((256, 256), F32)
    for b in range(3):
        for e in range(3):
            left = jnp.concatenate(
                [res3[2 * k + e, 2 * i + b] for k in range(8) for i in range(4)], axis=0
            ).astype(BF16)
            right = jnp.concatenate([down_ref[a, b, e] for a in range(3)], axis=0)
            total = total + dot(left, right)
    live = 2 * (iota((256, 256), 0) % 4) < valid
    total = jnp.where(live, total, 0.0)
    for o in range(2):
        lat[o] = total[:, o * 128 : (o + 1) * 128]
    for t in range(4):
        for h in range(2):
            for i in range(4):
                for o in range(2):
                    block = lat[o, pl.ds(i * 8 + h * 4 + t, 8, stride=32)]
                    lat_ref[t, h * 4 + i, :, o * 128 : (o + 1) * 128] = block.astype(BF16)


def finish_kernel(
    bit,
    after_ref,
    first_ref,
    first_in_ref,
    weight_ref,
    new_pix_ref,
    new_act_ref,
    rows,
    patch,
    frame,
):
    del after_ref
    target = first_ref[0:16].astype(jnp.int32)
    mine = (target >> bit) & 1 == (lax.axis_index("stream") >> bit) & 1
    mine = jnp.where(mine, 1.0, 0.0)[0:1] > 0.5

    def chosen(start, stop):
        own, other = first_ref[start:stop].astype(F32), first_in_ref[start:stop].astype(F32)
        return jnp.where(mine, own, other)

    new_act_ref[0] = chosen(80, 336).astype(BF16).reshape(16, 16, 128)
    left = chosen(16, 48)
    rows[0] = left
    rows[1] = pltpu.roll(left, 64, 1)
    rows[2] = chosen(48, 80)
    for i in range(2):
        new_pix_ref[i] = rows[1 + i, 1:17, 0:48].astype(BF16)
    norms = chosen(336, 352)
    scale = norms[0:1] + norms[1:2] + norms[2:3]
    shift = norms[3:4] + norms[4:5] + norms[5:6]
    for b in range(3):
        for a in range(3):
            q = (b * 3 + a) * 48
            patch[:, q : q + 48] = rows[a, b : b + 16, 0:48]
    spread = dot(patch[...].astype(BF16), spread_matrix()).astype(BF16)
    weight = weight_ref[...]
    for chunk in range(8):
        out = dot(spread[:, chunk * 128 : chunk * 128 + 128], weight).astype(BF16).astype(F32)
        for n in range(2):
            at = (2 * chunk + n) * 16
            frame[at : at + 16] = silu(out[:, n * 128 : n * 128 + 128] * scale + shift)
    for y in range(16):
        new_act_ref[1, y] = frame[pl.ds(y, 16, stride=16)].astype(BF16)


def partner(value, axis, stride):
    pairs = [(source, source ^ stride) for source in range(lax.axis_size(axis))]
    return lax.ppermute(value, axis, pairs)


def shifted(value, axis, by):
    size = lax.axis_size(axis)
    return lax.ppermute(value, axis, [(i, (i + by) % size) for i in range(size)])


def body(
    loader_rows,
    load_owner,
    load_slot,
    valid_frames,
    next_owner,
    pixel_cache,
    act_cache,
    res_cache,
    stem_weight,
    norm_gain,
    norm_bias,
    conv_weight,
    down_weight,
):
    streams = lax.axis_size("stream")
    strips = lax.axis_size("strip")
    stream_pos = lax.axis_index("stream")
    sections = streams.bit_length() - 1
    fill = loader_rows.shape[1]
    per = fill // streams
    pix, acts, ress = pixel_cache[0], act_cache[0], res_cache[0]
    mega = 1024 * 1024
    cost = pl.CostEstimate(flops=2 * 10**9, bytes_accessed=4 * mega, transcendentals=0)
    half_per = fill // streams // 2
    direct = half_per % 8 == 0
    line_shape = (strips, streams, half_per, 128) if direct else (fill // 2, 128)
    lines = pl.pallas_call(
        functools.partial(sort_kernel, streams),
        out_shape=jax.ShapeDtypeStruct(line_shape, BF16),
        in_specs=[VM] * 3,
        out_specs=VM,
        scratch_shapes=[pltpu.VMEM((128, 2 * fill), F32)],
        cost_estimate=cost,
    )(loader_rows[0].T, load_owner, load_slot)
    if not direct:
        lines = lines.reshape(1, streams, half_per, 128)
        lines = jnp.broadcast_to(lines, (strips, streams, half_per, 128))
    lines = lines.reshape(strips * streams, half_per, 128)
    recv = lax.all_to_all(lines, ("strip", "stream"), 0, 0, tiled=True)
    recv = recv.reshape(strips, fill // 2, 128)
    below, above, near, mid, weight = pl.pallas_call(
        pack_kernel,
        out_shape=(
            jax.ShapeDtypeStruct((6, 16, 128), BF16),
            jax.ShapeDtypeStruct((4, 16, 128), BF16),
            jax.ShapeDtypeStruct((2, 16, 128), BF16),
            jax.ShapeDtypeStruct((2, 16, 128), BF16),
            jax.ShapeDtypeStruct((128, 256), BF16),
        ),
        in_specs=[VM] * 2 + [ANY] * 2,
        out_specs=(VM,) * 5,
        scratch_shapes=[pltpu.VMEM((128, 256), F32), pltpu.SemaphoreType.DMA((6,))],
        compiler_params=pltpu.CompilerParams(vmem_limit_bytes=4 * mega),
    )(pix, stem_weight, acts, ress)
    below = shifted(below, "strip", 1)
    near = shifted(near, "strip", 1)
    above = shifted(above, "strip", -1)
    mid = shifted(mid, "strip", 2)
    scalars = jnp.concatenate([valid_frames, next_owner, jnp.zeros((126,), jnp.int32)])
    rows_all = strips * 16
    window = jax.ShapeDtypeStruct((2, 16, 11, 8, 128), F32)
    first, norm, stem = pl.pallas_call(
        functools.partial(stem_kernel, strips),
        out_shape=(
            jax.ShapeDtypeStruct((352, 128), BF16),
            jax.ShapeDtypeStruct((2, 8, 128), F32),
            window,
        ),
        in_specs=[VM] * 10,
        out_specs=(VM,) * 3,
        scratch_shapes=[
            pltpu.VMEM((strips, 32, 128), F32),
            pltpu.VMEM((3, rows_all + 16, 8, 128), F32),
            pltpu.VMEM((rows_all + 8, 8, 432), F32),
            pltpu.VMEM((rows_all + 4, 8, 1024), F32),
        ],
        compiler_params=pltpu.CompilerParams(vmem_limit_bytes=24 * mega),
        cost_estimate=cost,
    )(scalars, norm_gain, norm_bias, recv, pix, acts, near, above, mid, weight)
    keeps = []

    def kept(rows, bit):
        return (rows[0:1].astype(jnp.int32) >> bit) & 1 == (stream_pos >> bit) & 1

    def passed(value, bit):
        if bit == len(keeps):
            keeps.append(kept(value, bit))
        return jnp.where(keeps[bit], value, partner(value, "stream", 1 << bit))

    second = pl.pallas_call(
        last_kernel,
        out_shape=jax.ShapeDtypeStruct((32, 16, 128), F32),
        in_specs=[VM] * 8,
        out_specs=VM,
        scratch_shapes=[pltpu.VMEM((4, 18, 16, 384), BF16)],
        compiler_params=pltpu.CompilerParams(vmem_limit_bytes=24 * mega),
        cost_estimate=cost,
    )(scalars, norm, stem, acts, ress, below, above, conv_weight)
    first = passed(first, 0)
    second = pl.pallas_call(
        seal_kernel,
        out_shape=jax.ShapeDtypeStruct((512, 128), BF16),
        in_specs=[ANY, VM],
        out_specs=VM,
        compiler_params=pltpu.CompilerParams(vmem_limit_bytes=8 * mega),
    )(first, second)
    second = passed(second, 0)

    def convolved(w0, after, after_too):
        return pl.pallas_call(
            functools.partial(conv_kernel, strips, w0),
            out_shape=(
                jax.ShapeDtypeStruct((8, 9, 16, 128), BF16),
                jax.ShapeDtypeStruct((16, 128), BF16),
            ),
            in_specs=[VM if w0 == 0 else ANY, ANY] + [VM] * 6,
            out_specs=(VM,) * 2,
            scratch_shapes=[
                pltpu.VMEM((2, 416, 128), F32),
                pltpu.VMEM((10, 11, 16, 384), BF16),
            ],
            compiler_params=pltpu.CompilerParams(vmem_limit_bytes=24 * mega),
            cost_estimate=cost,
        )(after, after_too, norm, stem, acts, below, above, conv_weight)

    part, rows = convolved(0, first, second)
    for bit in range(1, sections - 1):
        if bit == 1:
            keeps.append(kept(rows, bit))
        first = passed(first, bit)
    rest, _ = convolved(8, first, part)
    for bit in range(1, sections - 1):
        second = passed(second, bit)
    latent = pl.pallas_call(
        down_kernel,
        out_shape=jax.ShapeDtypeStruct((4, 8, 8, 256), BF16),
        in_specs=[VM] * 6 + [ANY],
        out_specs=VM,
        scratch_shapes=[
            pltpu.VMEM((2, 384, 128), F32),
            pltpu.VMEM((17, 9, 8, 384), F32),
            pltpu.VMEM((2, 256, 128), F32),
        ],
        compiler_params=pltpu.CompilerParams(vmem_limit_bytes=24 * mega),
        cost_estimate=cost,
    )(scalars, part, rest, down_weight, ress, below, second)
    bit = sections - 1
    if bit == len(keeps):
        keeps.append(kept(first, bit))
    new_pix, new_act = pl.pallas_call(
        functools.partial(finish_kernel, bit),
        out_shape=(
            jax.ShapeDtypeStruct(pix.shape, BF16),
            jax.ShapeDtypeStruct(acts.shape, BF16),
        ),
        in_specs=[ANY] + [VM] * 3,
        out_specs=(VM,) * 2,
        scratch_shapes=[
            pltpu.VMEM((3, 32, 128), F32),
            pltpu.VMEM((16, 432), F32),
            pltpu.VMEM((256, 128), F32),
        ],
        compiler_params=pltpu.CompilerParams(vmem_limit_bytes=8 * mega),
        cost_estimate=cost,
    )(second, first, partner(first, "stream", 1 << bit), weight)
    second = passed(second, bit)
    return (latent[None], new_pix[None], new_act[None], second.reshape(1, 2, 16, 16, 128))


def solution(mesh):
    in_specs = (
        P("stream", "strip", None),
        P("stream", "strip"),
        P("stream", "strip"),
        P("stream"),
        P("stream"),
        P("stream", None, "strip", None),
        P("stream", None, "strip", None, None),
        P("stream", None, "strip", None, None),
        P(),
        P(),
        P(),
        P(),
        P(),
    )
    out_specs = (
        P("stream", None, "strip", None, None),
        P("stream", None, "strip", None),
        P("stream", None, "strip", None, None),
        P("stream", None, "strip", None, None),
    )
    return jax.shard_map(body, mesh=mesh, in_specs=in_specs, out_specs=out_specs, check_vma=False)
```

```python
import functools

import jax
import jax.numpy as jnp
from jax import lax
from jax.experimental import pallas as pl
from jax.experimental.pallas import tpu as pltpu
from jax.sharding import PartitionSpec as P

FRAMES = 8
GROUPS = 32
EPSILON = 1e-06
F32 = jnp.float32
BF16 = jnp.bfloat16
VM = pl.BlockSpec(memory_space=pltpu.VMEM)
ANY = pl.BlockSpec(memory_space=pl.ANY)


def iota(shape, axis):
    return lax.broadcasted_iota(jnp.int32, shape, axis)


def whole(scalars_ref, which):
    row = scalars_ref[...].astype(F32).reshape(1, 128)
    return jnp.sum(jnp.where(iota((1, 128), 1) == which, row, 0.0)).astype(jnp.int32)


def dot(a, b):
    return jnp.dot(a, b, preferred_element_type=F32)


def dot_nt(a, b):
    return lax.dot_general(a, b, (((1,), (1,)), ((), ())), preferred_element_type=F32)


def sort_kernel(streams, cols_ref, owner_ref, slot_ref, out_ref, wide):
    width, fill = cols_ref.shape
    half_per = fill // streams // 2
    lines = fill // 2
    wide[...] = jnp.zeros(wide.shape, F32)
    pixels, slots = cols_ref[...].astype(F32), slot_ref[...].astype(F32)
    for side in range(2):
        at = side * 64
        wide[at : at + width, side * fill : (side + 1) * fill] = pixels
        wide[at + width : at + width + 1, side * fill : (side + 1) * fill] = slots
    owner = owner_ref[...]
    hot = jnp.where(iota((streams, fill), 0) == owner, 1.0, 0.0)
    upper = jnp.where(iota((fill, fill), 0) <= iota((fill, fill), 1), 1.0, 0.0).astype(BF16)
    running = dot(hot.astype(BF16), upper)
    rank = jnp.sum(hot * running, axis=0, keepdims=True).astype(jnp.int32) - 1
    half = rank // half_per
    line = owner * half_per + rank - half * half_per
    line = jnp.concatenate([jnp.where(half == side, line, -1) for side in range(2)], axis=1)
    pick = jnp.where(iota((lines, 2 * fill), 0) == jnp.broadcast_to(line, (lines, 2 * fill)), 1.0, 0.0)
    out = dot_nt(pick.astype(BF16), wide[...].astype(BF16)).astype(BF16)
    if len(out_ref.shape) == 2:
        out_ref[...] = out
    else:
        for strip in range(out_ref.shape[0]):
            out_ref[strip] = out.reshape(out_ref.shape[1:])


def pack_kernel(pix_ref, sw_ref, act_ref, res_ref, down_ref, up_ref, near_ref, mid_ref, weight_ref, sw, sems):
    copies = []
    for f in range(2):
        copies.append((act_ref.at[f, 14:16], down_ref.at[2 * f : 2 * f + 2]))
        copies.append((res_ref.at[f, 15:16], down_ref.at[4 + f : 5 + f]))
        copies.append((act_ref.at[f, 0:1], up_ref.at[f : f + 1]))
    copies = [pltpu.make_async_copy(a, b, sems.at[i]) for i, (a, b) in enumerate(copies)]
    for copy in copies:
        copy.start()
    pix = pix_ref[...].reshape(32, 48).astype(F32)
    pix = jnp.concatenate([pix, jnp.zeros((32, 80), F32)], axis=1)
    pix = pix.astype(BF16).reshape(2, 16, 128)
    near_ref[...] = pix
    up_ref[2:4] = pix
    mid_ref[...] = pix
    sw[...] = jnp.zeros(sw.shape, F32)
    for k in range(2):
        for e in range(3):
            for a in range(3):
                for b in range(3):
                    at = 27 * (k + e) + 9 * a + 3 * b
                    sw[at : at + 3, k * 128 : k * 128 + 128] = sw_ref[a, b, e].astype(F32)
    weight_ref[...] = sw[...].astype(BF16)
    for copy in copies:
        copy.wait()


def received(line):
    line = line.astype(F32)
    both = jnp.concatenate([line, pltpu.roll(line, 64, 1)], axis=0)
    slot_lane = jnp.where(iota((8, 128), 1) == 48, 1.0, 0.0).astype(BF16)
    slots = dot_nt(slot_lane, both.astype(BF16)).astype(jnp.int32)
    return jnp.where(iota((128, 128), 1) < 48, both, 0.0), slots


def gather_pixels(strips, j, pc, pix_ref, below_ref, above_ref, mid_ref):
    pc[j] = jnp.zeros((32, 128), F32)
    pc[j, :, 0:48] = pix_ref[...].reshape(32, 48).astype(F32)
    pc[lax.rem(j + strips - 1, strips)] = below_ref[...].reshape(32, 128).astype(F32)
    pc[lax.rem(j + 1, strips)] = above_ref[2:4].reshape(32, 128).astype(F32)
    pc[lax.rem(j + 2, strips)] = mid_ref[...].reshape(32, 128).astype(F32)


def widen_cache(strips, j, cache, old_ref, below_ref, above_ref):
    has_above = jnp.where(j > 0, 1.0, 0.0)
    has_below = jnp.where(j < strips - 1, 1.0, 0.0)
    for f in range(2):
        cache[f, 304:416] = jnp.zeros((112, 128), F32)
        cache[f, 32:288] = old_ref[f].reshape(256, 128).astype(F32)
        cache[f, 0:32] = below_ref[2 * f : 2 * f + 2].reshape(32, 128).astype(F32) * has_above
        cache[f, 288:304] = above_ref[f].astype(F32) * has_below


def spread_matrix():
    lanes = iota((8, 1024), 1)
    pair, m = lanes >> 7, lanes & 127
    col = (m * 2428) >> 16
    tap = m - 27 * col
    a = (tap * 7282) >> 16
    b = ((tap - 9 * a) * 21846) >> 16
    c = tap - 9 * a - 3 * b
    w = 2 * pair - 1 + col
    source = jnp.where((m < 108) & (w >= 0) & (w < 16), (b * 3 + a) * 48 + c * 16 + w, -1)
    line = iota((54, 8, 1024), 0) * 8 + iota((54, 8, 1024), 1)
    return jnp.where(line == source[None], 1.0, 0.0).reshape(432, 1024).astype(BF16)


def norm_rows(strips, s1, s2, gain_ref, bias_ref):
    same = jnp.where(iota((128, 128), 0) // 4 == iota((128, 128), 1) // 4, 1.0, 0.0)
    count = strips * 16 * 16 * 4
    exact = functools.partial(
        jnp.dot, preferred_element_type=F32, precision=lax.Precision.HIGHEST
    )
    mean = exact(s1, same) / count
    inv = lax.rsqrt(exact(s2, same) / count - mean * mean + EPSILON)
    scale = inv * gain_ref[...].reshape(1, 128)
    return scale, bias_ref[...].reshape(1, 128) - mean * scale


def frame_row(rows, t):
    t = jnp.maximum(t, 0)
    mine = iota((8, 128), 0) == (t & 1) * 4 + (t >> 1)
    return jnp.sum(jnp.where(mine, rows, 0.0), axis=0, keepdims=True)


def silu(v):
    h = 0.5 * v
    return h + h * jnp.tanh(h)


def pair_weight(conv_ref):
    zero = jnp.zeros((384, 128), BF16)

    def weight(b, e):
        if not 0 <= e <= 2:
            return zero
        return jnp.concatenate([conv_ref[a, b, e] for a in range(3)], axis=0)

    return jnp.concatenate(
        [
            jnp.concatenate([weight(b, col - k) for k in range(2)], axis=1)
            for col in range(4)
            for b in range(3)
        ],
        axis=0,
    )


def row_at(t, y):
    t = jnp.maximum(t, 0)
    h = 1 if y >= 8 else 0
    return (t & 1) * (16 * 88) + (y + 2 - 8 * h) * 8 + h * 4 + (t >> 1)


def stem_kernel(
    strips,
    scalars_ref,
    gain_ref,
    bias_ref,
    recv_ref,
    pix_ref,
    old_ref,
    below_ref,
    above_ref,
    mid_ref,
    weight_ref,
    pay_ref,
    norm_ref,
    stem,
    pc,
    zs,
    xs,
    ys,
):
    j = lax.axis_index("strip")
    valid = whole(scalars_ref, 0)
    rows_all = strips * 16
    gather_pixels(strips, j, pc, pix_ref, below_ref, above_ref, mid_ref)
    zs[:, 0:4] = jnp.zeros((3, 4, 8, 128), F32)
    zs[:, 4 + rows_all :] = jnp.zeros((3, 12, 8, 128), F32)
    sub = iota((128, 128), 0)
    crow, cframe = iota((128, 32), 1) % 16, iota((128, 32), 1) // 16
    csub = iota((128, 32), 0)
    arrived = [received(recv_ref[s]) for s in range(strips)]
    old_hits = []
    for a in range(3):
        ct = cframe - a
        cplace = jnp.where(ct >= 0, crow * 8 + (ct & 1) * 4 + (ct >> 1), -1)
        old_hits.append(jnp.where(csub == cplace, 1.0, 0.0))
    picks = []
    for _, slots in arrived:
        frame, row = slots >> 4, slots & 15
        hits = []
        for a in range(3):
            t = frame + 2 - a
            place = jnp.where(t < FRAMES, row * 8 + (t & 1) * 4 + (t >> 1), -1)
            hit = jnp.where(sub.reshape(16, 8, 128) == place[None], 1.0, 0.0).reshape(128, 128)
            hits.append(jnp.concatenate([hit, old_hits[a]], axis=1).astype(BF16))
        picks.append(jnp.concatenate(hits, axis=0))
    sources = [
        jnp.concatenate([arrived[s][0], pc[s]], axis=0).astype(BF16) for s in range(strips)
    ]
    placed = [dot(picks[s], sources[s]).reshape(3, 16, 8, 128) for s in range(strips)]
    for s in range(strips):
        for a in range(3):
            zs[a, 4 + s * 16 : 4 + (s + 1) * 16] = placed[s][a]
    target = whole(scalars_ref, 1).astype(F32)
    last = valid - 1
    line_rows = zs.reshape(3 * (rows_all + 16) * 8, 128)
    lines = []
    for a in range(3):
        at = (a * (rows_all + 16) + 3 + j * 16) * 8 + (last & 1) * 4 + (last >> 1)
        lines.append(line_rows[pl.ds(at, 24, stride=8)])
    none = jnp.zeros((8, 128), F32)
    left = jnp.where(iota((24, 128), 1) < 64, lines[0], pltpu.roll(lines[1], 64, 1))
    pay_ref[16:48] = jnp.concatenate([left, none], axis=0).astype(BF16)
    pay_ref[48:80] = jnp.concatenate([lines[2], none], axis=0).astype(BF16)
    high = rows_all + 4
    for b in range(3):
        for a in range(3):
            q = (b * 3 + a) * 48
            xs[2 : high + 2, :, q : q + 48] = zs[a, 1 + b : high + 1 + b, :, 0:48]
    patches = xs[2 : high + 2].reshape(high * 8, 432).astype(BF16)
    ys[...] = dot(patches, spread_matrix()).reshape(high, 8, 1024)
    full = ys[2 : 2 + rows_all].reshape(rows_all * 8, 1024).astype(BF16)
    base = j * 16
    first, second = ys[pl.ds(base, 11)], ys[pl.ds(base + 8, 11)]
    low = iota((11, 8, 1024), 1) < 4
    own_even = jnp.where(low, first, pltpu.roll(second, 4, 1))
    own_odd = jnp.where(low, pltpu.roll(first, 4, 1), second)
    own = jnp.concatenate([own_even, own_odd], axis=0).reshape(176, 1024).astype(BF16)
    weight = weight_ref[...]
    s1 = jnp.zeros((8, 256), F32)
    s2 = jnp.zeros((8, 256), F32)
    for chunk in range(8):
        out = dot(full[:, chunk * 128 : chunk * 128 + 128], weight).astype(BF16).astype(F32).reshape(rows_all, 8, 256)
        s1 = s1 + jnp.sum(out, axis=0)
        s2 = s2 + jnp.sum(out * out, axis=0)
        mine = dot(own[:, chunk * 128 : chunk * 128 + 128], weight).astype(BF16).astype(F32).reshape(2, 11, 8, 256)
        for i in range(2):
            stem[:, 2 * chunk + i] = mine[:, :, :, i * 128 : (i + 1) * 128]
    s1 = s1[:, 0:128] + s1[:, 128:256]
    s2 = s2[:, 0:128] + s2[:, 128:256]
    scale, shift = norm_rows(strips, s1, s2, gain_ref, bias_ref)
    norm_ref[0] = scale
    norm_ref[1] = shift
    stem_rows = stem.reshape(2 * 16 * 11 * 8, 128)
    t = valid - 2
    scale_t, shift_t = frame_row(scale, t), frame_row(shift, t)
    for y in range(16):
        block = silu(stem_rows[pl.ds(row_at(t, y), 16, stride=88)] * scale_t + shift_t)
        block = jnp.where(valid < 2, old_ref[1, y].astype(F32), block)
        pay_ref[80 + y * 16 : 96 + y * 16] = block.astype(BF16)
    pieces = []
    for row in (frame_row(scale, last), frame_row(shift, last)):
        for _ in range(3):
            piece = row.astype(BF16).astype(F32)
            pieces.append(piece)
            row = row - piece
    row16 = iota((16, 128), 0)
    norms = jnp.where(row16 == 0, target, 0.0)
    for n, piece in enumerate(pieces):
        norms = jnp.where(row16 == n + 1, piece, norms)
    pay_ref[0:16] = norms.astype(BF16)


def last_kernel(
    scalars_ref,
    norm_ref,
    stem,
    old_ref,
    res_old_ref,
    below_ref,
    above_ref,
    conv_ref,
    pay_ref,
    lines,
):
    j = lax.axis_index("strip")
    valid = whole(scalars_ref, 0)
    scale, shift = norm_ref[0], norm_ref[1]
    has_above = jnp.where(j > 0, 1.0, 0.0)
    has_below = jnp.where(j < lax.axis_size("strip") - 1, 1.0, 0.0)
    stem_rows = stem.reshape(2 * 16 * 11 * 8, 128)
    column = iota((16, 128), 0)

    def side_by_side(m, y, block):
        before = jnp.where(column == 0, 0.0, pltpu.roll(block, 1, 0))
        after = jnp.where(column == 15, 0.0, pltpu.roll(block, 15, 0))
        lines[m, y + 1] = jnp.concatenate([before, block, after], axis=1).astype(BF16)

    for m in range(4):
        from_cache = valid - 2 + m

        @pl.when(from_cache >= 2)
        def _(m=m, from_cache=from_cache):
            t = from_cache - 2
            scale_m, shift_m = frame_row(scale, t), frame_row(shift, t)
            for y in range(-1, 17):
                block = stem_rows[pl.ds(row_at(t, y), 16, stride=88)]
                block = silu(block * scale_m + shift_m)
                if y < 0:
                    block = block * has_above
                if y > 15:
                    block = block * has_below
                side_by_side(m, y, block)

        @pl.when(from_cache < 2)
        def _(m=m, from_cache=from_cache):
            f = jnp.clip(from_cache, 0, 1)
            side_by_side(m, -1, below_ref[2 * f + 1].astype(F32) * has_above)
            for y in range(16):
                side_by_side(m, y, old_ref[f, y].astype(F32))
            side_by_side(m, 16, above_ref[f].astype(F32) * has_below)

    zero = jnp.zeros((384, 128), BF16)

    def weight(a, b):
        if not 0 <= b <= 2:
            return zero
        return jnp.concatenate([conv_ref[a, b, e] for e in range(3)], axis=0)

    weights = jnp.concatenate(
        [
            jnp.concatenate([weight(a, y - k) for k in range(2)], axis=1)
            for y in range(4)
            for a in range(3)
        ],
        axis=0,
    )
    left = jnp.concatenate(
        [
            jnp.concatenate(
                [lines[i + a, 2 * k + y] for i in range(2) for k in range(8)], axis=0
            )
            for y in range(4)
            for a in range(3)
        ],
        axis=1,
    )
    out = dot(left, weights).reshape(2, 8, 16, 256)
    for i in range(2):
        for y in range(16):
            block = stem_rows[pl.ds(row_at(valid - 2 + i, y), 16, stride=88)]
            block = block + out[i, y // 2, :, y % 2 * 128 : y % 2 * 128 + 128]
            if i == 0:
                block = jnp.where(valid < 2, res_old_ref[1, y].astype(F32), block)
            pay_ref[i * 16 + y] = block


def seal_kernel(after_ref, value_ref, out_ref):
    del after_ref
    out_ref[...] = value_ref[...].reshape(512, 128).astype(BF16)


def conv_kernel(
    strips,
    w0,
    after_ref,
    after_too_ref,
    norm_ref,
    stem,
    old_ref,
    below_ref,
    above_ref,
    conv_ref,
    out_ref,
    rows_ref,
    cache,
    act3,
):
    del after_too_ref
    rows_ref[...] = after_ref[0:16] if w0 == 0 else jnp.zeros((16, 128), BF16)
    j = lax.axis_index("strip")
    widen_cache(strips, j, cache, old_ref, below_ref, above_ref)
    low8 = iota((8, 128), 0) < 4
    scales, shifts = [], []
    for k, rows in enumerate((scales, shifts)):
        v = norm_ref[k]
        rows.append(jnp.where(low8, v, pltpu.roll(v, 4, 0)))
        rows.append(jnp.where(low8, pltpu.roll(v, 4, 0), v))
    half = iota((11, 8, 128), 1) // 4
    line_of = j * 16 + iota((11, 8, 128), 0) - 2 + 8 * half
    inside = jnp.where((line_of >= 0) & (line_of < strips * 16), 1.0, 0.0)
    at0 = iota((11, 8, 128), 1) == 0
    at4 = iota((11, 8, 128), 1) == 4
    edge = 0 if w0 == 0 else 9
    act3[edge] = jnp.zeros(act3.shape[1:], BF16)
    shift = 1 if w0 == 0 else 1 - w0

    def arrange(w, carry):
        late = []
        even, odd = [silu(stem[p, w] * scales[p] + shifts[p]) * inside for p in range(2)]
        for f in range(2):
            rows = [
                jnp.broadcast_to(cache[f, pl.ds(y * 16 + w, 1)], (8, 128)) for y in range(19)
            ]
            upper, lower = jnp.stack(rows[0:11], axis=0), jnp.stack(rows[8:19], axis=0)
            rolled = pltpu.roll((even, odd)[f], 1, 1)
            late.append(jnp.where(at0, upper, jnp.where(at4, lower, rolled)))
        taps = ((late[0], late[1]), (late[1], even), (even, odd))
        for a in range(3):
            act3[w + shift, :, :, a * 128 : (a + 1) * 128] = jnp.concatenate(taps[a], axis=1).astype(BF16)
        return carry

    lax.fori_loop(max(w0 - 1, 0), min(w0 + 9, 16), arrange, 0, unroll=9)
    weights = pair_weight(conv_ref)
    outside = (j == 0) & (iota((9, 16, 128), 0) == 0) & (iota((9, 16, 128), 1) % 8 < 4)
    keep = jnp.where(outside, 0.0, 1.0)
    left = jnp.concatenate(
        [
            jnp.concatenate(
                [act3[2 * k + col, b : b + 9].reshape(144, 384) for k in range(4)],
                axis=0,
            )
            for col in range(4)
            for b in range(3)
        ],
        axis=1,
    )
    out = dot(left, weights).reshape(4, 9, 16, 256)
    for k in range(4):
        for n in range(2):
            w = w0 + 2 * k + n
            value = out[k, :, :, n * 128 : n * 128 + 128]
            value = value + jnp.concatenate([stem[0, w, 1:10], stem[1, w, 1:10]], axis=1)
            out_ref[w - w0] = (value * keep).astype(BF16)


def down_kernel(
    scalars_ref,
    part_ref,
    rest_ref,
    down_ref,
    res_cache_ref,
    below_ref,
    after_ref,
    lat_ref,
    rcache,
    res3,
    lat,
):
    del after_ref
    j = lax.axis_index("strip")
    valid = whole(scalars_ref, 0)
    rcache[...] = jnp.zeros(rcache.shape, F32)
    has_above = jnp.where(j > 0, 1.0, 0.0)
    for f in range(2):
        rcache[f, 0:16] = below_ref[4 + f].astype(F32) * has_above
        rcache[f, 16:272] = res_cache_ref[f].reshape(256, 128).astype(F32)
    at0 = iota((9, 8, 128), 1) == 0
    at4 = iota((9, 8, 128), 1) == 4
    res3[0] = jnp.zeros(res3.shape[1:], F32)

    for w0, ref in ((0, part_ref), (8, rest_ref)):

        def delay(w, carry, w0=w0, ref=ref):
            both = ref[w].astype(F32)
            even, odd = both[:, 0:8], both[:, 8:16]
            olds = []
            for f in range(2):
                rows = [
                    jnp.broadcast_to(rcache[f, pl.ds(y * 16 + w0 + w, 1)], (8, 128))
                    for y in range(17)
                ]
                olds.append((jnp.stack(rows[0:9], axis=0), jnp.stack(rows[8:17], axis=0)))
            at = w0 + w + 1
            for f, v in enumerate((even, odd)):
                rolled = pltpu.roll(v, 1, 1)
                late = jnp.where(at0, olds[f][0], jnp.where(at4, olds[f][1], rolled))
                res3[at, :, :, f * 128 : f * 128 + 128] = late
            res3[at, :, :, 256:384] = even
            return carry

        lax.fori_loop(0, 8, delay, 0, unroll=8)
    total = jnp.zeros((256, 256), F32)
    for b in range(3):
        for e in range(3):
            left = jnp.concatenate(
                [res3[2 * k + e, 2 * i + b] for k in range(8) for i in range(4)], axis=0
            ).astype(BF16)
            right = jnp.concatenate([down_ref[a, b, e] for a in range(3)], axis=0)
            total = total + dot(left, right)
    live = 2 * (iota((256, 256), 0) % 4) < valid
    total = jnp.where(live, total, 0.0)
    for o in range(2):
        lat[o] = total[:, o * 128 : (o + 1) * 128]
    for t in range(4):
        for h in range(2):
            for i in range(4):
                for o in range(2):
                    block = lat[o, pl.ds(i * 8 + h * 4 + t, 8, stride=32)]
                    lat_ref[t, h * 4 + i, :, o * 128 : (o + 1) * 128] = block.astype(BF16)


def finish_kernel(
    bit,
    after_ref,
    first_ref,
    first_in_ref,
    weight_ref,
    new_pix_ref,
    new_act_ref,
    rows,
    patch,
    frame,
):
    del after_ref
    target = first_ref[0:16].astype(F32).astype(jnp.int32)
    mine = (target >> bit) & 1 == (lax.axis_index("stream") >> bit) & 1
    mine = jnp.where(mine, 1.0, 0.0)[0:1] > 0.5

    def chosen(start, stop):
        own, other = first_ref[start:stop].astype(F32), first_in_ref[start:stop].astype(F32)
        return jnp.where(mine, own, other)

    new_act_ref[0] = chosen(80, 336).astype(BF16).reshape(16, 16, 128)
    left = chosen(16, 48)
    rows[0] = left
    rows[1] = pltpu.roll(left, 64, 1)
    rows[2] = chosen(48, 80)
    for i in range(2):
        new_pix_ref[i] = rows[1 + i, 1:17, 0:48].astype(BF16)
    norms = chosen(0, 16)
    scale = norms[1:2] + norms[2:3] + norms[3:4]
    shift = norms[4:5] + norms[5:6] + norms[6:7]
    for b in range(3):
        for a in range(3):
            q = (b * 3 + a) * 48
            patch[:, q : q + 48] = rows[a, b : b + 16, 0:48]
    spread = dot(patch[...].astype(BF16), spread_matrix()).astype(BF16)
    weight = weight_ref[...]
    for chunk in range(8):
        out = dot(spread[:, chunk * 128 : chunk * 128 + 128], weight).astype(BF16).astype(F32)
        for n in range(2):
            at = (2 * chunk + n) * 16
            frame[at : at + 16] = silu(out[:, n * 128 : n * 128 + 128] * scale + shift)
    for y in range(16):
        new_act_ref[1, y] = frame[pl.ds(y, 16, stride=16)].astype(BF16)


def partner(value, axis, stride):
    pairs = [(source, source ^ stride) for source in range(lax.axis_size(axis))]
    return lax.ppermute(value, axis, pairs)


def shifted(value, axis, by):
    size = lax.axis_size(axis)
    return lax.ppermute(value, axis, [(i, (i + by) % size) for i in range(size)])


def body(
    loader_rows,
    load_owner,
    load_slot,
    valid_frames,
    next_owner,
    pixel_cache,
    act_cache,
    res_cache,
    stem_weight,
    norm_gain,
    norm_bias,
    conv_weight,
    down_weight,
):
    streams = lax.axis_size("stream")
    strips = lax.axis_size("strip")
    stream_pos = lax.axis_index("stream")
    sections = streams.bit_length() - 1
    fill = loader_rows.shape[1]
    per = fill // streams
    pix, acts, ress = pixel_cache[0], act_cache[0], res_cache[0]
    mega = 1024 * 1024
    cost = pl.CostEstimate(flops=2 * 10**9, bytes_accessed=4 * mega, transcendentals=0)
    half_per = fill // streams // 2
    direct = half_per % 8 == 0
    line_shape = (strips, streams, half_per, 128) if direct else (fill // 2, 128)
    lines = pl.pallas_call(
        functools.partial(sort_kernel, streams),
        out_shape=jax.ShapeDtypeStruct(line_shape, BF16),
        in_specs=[VM] * 3,
        out_specs=VM,
        scratch_shapes=[pltpu.VMEM((128, 2 * fill), F32)],
        cost_estimate=cost,
    )(loader_rows[0].T, load_owner, load_slot)
    if not direct:
        lines = lines.reshape(1, streams, half_per, 128)
        lines = jnp.broadcast_to(lines, (strips, streams, half_per, 128))
    lines = lines.reshape(strips * streams, half_per, 128)
    recv = lax.all_to_all(lines, ("strip", "stream"), 0, 0, tiled=True)
    recv = recv.reshape(strips, fill // 2, 128)
    below, above, near, mid, weight = pl.pallas_call(
        pack_kernel,
        out_shape=(
            jax.ShapeDtypeStruct((6, 16, 128), BF16),
            jax.ShapeDtypeStruct((4, 16, 128), BF16),
            jax.ShapeDtypeStruct((2, 16, 128), BF16),
            jax.ShapeDtypeStruct((2, 16, 128), BF16),
            jax.ShapeDtypeStruct((128, 256), BF16),
        ),
        in_specs=[VM] * 2 + [ANY] * 2,
        out_specs=(VM,) * 5,
        scratch_shapes=[pltpu.VMEM((128, 256), F32), pltpu.SemaphoreType.DMA((6,))],
        compiler_params=pltpu.CompilerParams(vmem_limit_bytes=4 * mega),
    )(pix, stem_weight, acts, ress)
    below = shifted(below, "strip", 1)
    near = shifted(near, "strip", 1)
    above = shifted(above, "strip", -1)
    mid = shifted(mid, "strip", 2)
    scalars = jnp.concatenate([valid_frames, next_owner, jnp.zeros((126,), jnp.int32)])
    rows_all = strips * 16
    window = jax.ShapeDtypeStruct((2, 16, 11, 8, 128), F32)
    first, norm, stem = pl.pallas_call(
        functools.partial(stem_kernel, strips),
        out_shape=(
            jax.ShapeDtypeStruct((336, 128), BF16),
            jax.ShapeDtypeStruct((2, 8, 128), F32),
            window,
        ),
        in_specs=[VM] * 10,
        out_specs=(VM,) * 3,
        scratch_shapes=[
            pltpu.VMEM((strips, 32, 128), F32),
            pltpu.VMEM((3, rows_all + 16, 8, 128), F32),
            pltpu.VMEM((rows_all + 8, 8, 432), F32),
            pltpu.VMEM((rows_all + 4, 8, 1024), F32),
        ],
        compiler_params=pltpu.CompilerParams(vmem_limit_bytes=24 * mega),
        cost_estimate=cost,
    )(scalars, norm_gain, norm_bias, recv, pix, acts, near, above, mid, weight)
    keeps = []

    def kept(rows, bit):
        return (rows[0:1].astype(jnp.int32) >> bit) & 1 == (stream_pos >> bit) & 1

    def passed(value, bit):
        if bit == len(keeps):
            keeps.append(kept(value, bit))
        return jnp.where(keeps[bit], value, partner(value, "stream", 1 << bit))

    second = pl.pallas_call(
        last_kernel,
        out_shape=jax.ShapeDtypeStruct((32, 16, 128), F32),
        in_specs=[VM] * 8,
        out_specs=VM,
        scratch_shapes=[pltpu.VMEM((4, 18, 16, 384), BF16)],
        compiler_params=pltpu.CompilerParams(vmem_limit_bytes=24 * mega),
        cost_estimate=cost,
    )(scalars, norm, stem, acts, ress, below, above, conv_weight)
    first = passed(first, 0)
    second = pl.pallas_call(
        seal_kernel,
        out_shape=jax.ShapeDtypeStruct((512, 128), BF16),
        in_specs=[ANY, VM],
        out_specs=VM,
        compiler_params=pltpu.CompilerParams(vmem_limit_bytes=8 * mega),
    )(first, second)
    second = passed(second, 0)

    def convolved(w0, after, after_too):
        return pl.pallas_call(
            functools.partial(conv_kernel, strips, w0),
            out_shape=(
                jax.ShapeDtypeStruct((8, 9, 16, 128), BF16),
                jax.ShapeDtypeStruct((16, 128), BF16),
            ),
            in_specs=[VM if w0 == 0 else ANY, ANY] + [VM] * 6,
            out_specs=(VM,) * 2,
            scratch_shapes=[
                pltpu.VMEM((2, 416, 128), F32),
                pltpu.VMEM((10, 11, 16, 384), BF16),
            ],
            compiler_params=pltpu.CompilerParams(vmem_limit_bytes=24 * mega),
            cost_estimate=cost,
        )(after, after_too, norm, stem, acts, below, above, conv_weight)

    part, rows = convolved(0, first, second)
    for bit in range(1, sections - 1):
        if bit == 1:
            keeps.append(kept(rows, bit))
        first = passed(first, bit)
    rest, _ = convolved(8, first, part)
    for bit in range(1, sections - 1):
        second = passed(second, bit)
    latent = pl.pallas_call(
        down_kernel,
        out_shape=jax.ShapeDtypeStruct((4, 8, 8, 256), BF16),
        in_specs=[VM] * 6 + [ANY],
        out_specs=VM,
        scratch_shapes=[
            pltpu.VMEM((2, 384, 128), F32),
            pltpu.VMEM((17, 9, 8, 384), F32),
            pltpu.VMEM((2, 256, 128), F32),
        ],
        compiler_params=pltpu.CompilerParams(vmem_limit_bytes=24 * mega),
        cost_estimate=cost,
    )(scalars, part, rest, down_weight, ress, below, second)
    bit = sections - 1
    if bit == len(keeps):
        keeps.append(kept(first, bit))
    new_pix, new_act = pl.pallas_call(
        functools.partial(finish_kernel, bit),
        out_shape=(
            jax.ShapeDtypeStruct(pix.shape, BF16),
            jax.ShapeDtypeStruct(acts.shape, BF16),
        ),
        in_specs=[ANY] + [VM] * 3,
        out_specs=(VM,) * 2,
        scratch_shapes=[
            pltpu.VMEM((3, 32, 128), F32),
            pltpu.VMEM((16, 432), F32),
            pltpu.VMEM((256, 128), F32),
        ],
        compiler_params=pltpu.CompilerParams(vmem_limit_bytes=8 * mega),
        cost_estimate=cost,
    )(second, first, partner(first, "stream", 1 << bit), weight)
    second = passed(second, bit)
    return (latent[None], new_pix[None], new_act[None], second.reshape(1, 2, 16, 16, 128))


def solution(mesh):
    in_specs = (
        P("stream", "strip", None),
        P("stream", "strip"),
        P("stream", "strip"),
        P("stream"),
        P("stream"),
        P("stream", None, "strip", None),
        P("stream", None, "strip", None, None),
        P("stream", None, "strip", None, None),
        P(),
        P(),
        P(),
        P(),
        P(),
    )
    out_specs = (
        P("stream", None, "strip", None, None),
        P("stream", None, "strip", None),
        P("stream", None, "strip", None, None),
        P("stream", None, "strip", None, None),
    )
    return jax.shard_map(body, mesh=mesh, in_specs=in_specs, out_specs=out_specs, check_vma=False)
```

```python
import functools

import jax
import jax.numpy as jnp
from jax import lax
from jax.experimental import pallas as pl
from jax.experimental.pallas import tpu as pltpu
from jax.sharding import PartitionSpec as P

FRAMES = 8
GROUPS = 32
EPSILON = 1e-06
F32 = jnp.float32
BF16 = jnp.bfloat16
VM = pl.BlockSpec(memory_space=pltpu.VMEM)
ANY = pl.BlockSpec(memory_space=pl.ANY)


def iota(shape, axis):
    return lax.broadcasted_iota(jnp.int32, shape, axis)


def whole(scalars_ref, which):
    row = scalars_ref[...].astype(F32).reshape(1, 128)
    return jnp.sum(jnp.where(iota((1, 128), 1) == which, row, 0.0)).astype(jnp.int32)


def dot(a, b):
    return jnp.dot(a, b, preferred_element_type=F32)


def dot_nt(a, b):
    return lax.dot_general(a, b, (((1,), (1,)), ((), ())), preferred_element_type=F32)


def sort_kernel(streams, cols_ref, owner_ref, slot_ref, out_ref, wide):
    width, fill = cols_ref.shape
    half_per = fill // streams // 2
    lines = fill // 2
    wide[...] = jnp.zeros(wide.shape, F32)
    pixels, slots = cols_ref[...].astype(F32), slot_ref[...].astype(F32)
    for side in range(2):
        at = side * 64
        wide[at : at + width, side * fill : (side + 1) * fill] = pixels
        wide[at + width : at + width + 1, side * fill : (side + 1) * fill] = slots
    owner = owner_ref[...]
    hot = jnp.where(iota((streams, fill), 0) == owner, 1.0, 0.0)
    upper = jnp.where(iota((fill, fill), 0) <= iota((fill, fill), 1), 1.0, 0.0).astype(BF16)
    running = dot(hot.astype(BF16), upper)
    rank = jnp.sum(hot * running, axis=0, keepdims=True).astype(jnp.int32) - 1
    half = rank // half_per
    line = owner * half_per + rank - half * half_per
    line = jnp.concatenate([jnp.where(half == side, line, -1) for side in range(2)], axis=1)
    pick = jnp.where(iota((lines, 2 * fill), 0) == jnp.broadcast_to(line, (lines, 2 * fill)), 1.0, 0.0)
    out = dot_nt(pick.astype(BF16), wide[...].astype(BF16)).astype(BF16)
    if len(out_ref.shape) == 2:
        out_ref[...] = out
    else:
        for strip in range(out_ref.shape[0]):
            out_ref[strip] = out.reshape(out_ref.shape[1:])


def pack_kernel(pix_ref, sw_ref, act_ref, res_ref, down_ref, up_ref, near_ref, mid_ref, weight_ref, sw, sems):
    copies = []
    for f in range(2):
        copies.append((act_ref.at[f, 14:16], down_ref.at[2 * f : 2 * f + 2]))
        copies.append((res_ref.at[f, 15:16], down_ref.at[4 + f : 5 + f]))
        copies.append((act_ref.at[f, 0:1], up_ref.at[f : f + 1]))
    copies = [pltpu.make_async_copy(a, b, sems.at[i]) for i, (a, b) in enumerate(copies)]
    for copy in copies:
        copy.start()
    pix = pix_ref[...].reshape(32, 48).astype(F32)
    pix = jnp.concatenate([pix, jnp.zeros((32, 80), F32)], axis=1)
    pix = pix.astype(BF16).reshape(2, 16, 128)
    near_ref[...] = pix
    up_ref[2:4] = pix
    mid_ref[...] = pix
    sw[...] = jnp.zeros(sw.shape, F32)
    for k in range(2):
        for e in range(3):
            for a in range(3):
                for b in range(3):
                    at = 27 * (k + e) + 9 * a + 3 * b
                    sw[at : at + 3, k * 128 : k * 128 + 128] = sw_ref[a, b, e].astype(F32)
    weight_ref[...] = sw[...].astype(BF16)
    for copy in copies:
        copy.wait()


def received(line):
    line = line.astype(F32)
    both = jnp.concatenate([line, pltpu.roll(line, 64, 1)], axis=0)
    slot_lane = jnp.where(iota((8, 128), 1) == 48, 1.0, 0.0).astype(BF16)
    slots = dot_nt(slot_lane, both.astype(BF16)).astype(jnp.int32)
    return jnp.where(iota((128, 128), 1) < 48, both, 0.0), slots


def gather_pixels(strips, j, pc, pix_ref, below_ref, above_ref, mid_ref):
    pc[j] = jnp.zeros((32, 128), F32)
    pc[j, :, 0:48] = pix_ref[...].reshape(32, 48).astype(F32)
    pc[lax.rem(j + strips - 1, strips)] = below_ref[...].reshape(32, 128).astype(F32)
    pc[lax.rem(j + 1, strips)] = above_ref[2:4].reshape(32, 128).astype(F32)
    pc[lax.rem(j + 2, strips)] = mid_ref[...].reshape(32, 128).astype(F32)


def widen_cache(strips, j, cache, old_ref, below_ref, above_ref):
    has_above = jnp.where(j > 0, 1.0, 0.0)
    has_below = jnp.where(j < strips - 1, 1.0, 0.0)
    for f in range(2):
        cache[f, 304:416] = jnp.zeros((112, 128), F32)
        cache[f, 32:288] = old_ref[f].reshape(256, 128).astype(F32)
        cache[f, 0:32] = below_ref[2 * f : 2 * f + 2].reshape(32, 128).astype(F32) * has_above
        cache[f, 288:304] = above_ref[f].astype(F32) * has_below


def spread_matrix():
    lanes = iota((8, 1024), 1)
    pair, m = lanes >> 7, lanes & 127
    col = (m * 2428) >> 16
    tap = m - 27 * col
    a = (tap * 7282) >> 16
    b = ((tap - 9 * a) * 21846) >> 16
    c = tap - 9 * a - 3 * b
    w = 2 * pair - 1 + col
    source = jnp.where((m < 108) & (w >= 0) & (w < 16), (b * 3 + a) * 48 + c * 16 + w, -1)
    line = iota((54, 8, 1024), 0) * 8 + iota((54, 8, 1024), 1)
    return jnp.where(line == source[None], 1.0, 0.0).reshape(432, 1024).astype(BF16)


def norm_rows(strips, s1, s2, gain_ref, bias_ref):
    same = jnp.where(iota((128, 128), 0) // 4 == iota((128, 128), 1) // 4, 1.0, 0.0)
    count = strips * 16 * 16 * 4
    exact = functools.partial(
        jnp.dot, preferred_element_type=F32, precision=lax.Precision.HIGHEST
    )
    mean = exact(s1, same) / count
    inv = lax.rsqrt(exact(s2, same) / count - mean * mean + EPSILON)
    scale = inv * gain_ref[...].reshape(1, 128)
    return scale, bias_ref[...].reshape(1, 128) - mean * scale


def frame_row(rows, t):
    t = jnp.maximum(t, 0)
    mine = iota((8, 128), 0) == (t & 1) * 4 + (t >> 1)
    return jnp.sum(jnp.where(mine, rows, 0.0), axis=0, keepdims=True)


def silu(v):
    h = 0.5 * v
    return h + h * jnp.tanh(h)


def pair_weight(conv_ref):
    zero = jnp.zeros((384, 128), BF16)

    def weight(b, e):
        if not 0 <= e <= 2:
            return zero
        return jnp.concatenate([conv_ref[a, b, e] for a in range(3)], axis=0)

    return jnp.concatenate(
        [
            jnp.concatenate([weight(b, col - k) for k in range(2)], axis=1)
            for col in range(4)
            for b in range(3)
        ],
        axis=0,
    )


def row_at(t, y):
    t = jnp.maximum(t, 0)
    h = 1 if y >= 8 else 0
    return (t & 1) * (16 * 88) + (y + 2 - 8 * h) * 8 + h * 4 + (t >> 1)


def stem_kernel(
    strips,
    scalars_ref,
    gain_ref,
    bias_ref,
    recv_ref,
    pix_ref,
    old_ref,
    below_ref,
    above_ref,
    mid_ref,
    weight_ref,
    pay_ref,
    norm_ref,
    stem,
    pc,
    zs,
    xs,
    ys,
):
    j = lax.axis_index("strip")
    valid = whole(scalars_ref, 0)
    rows_all = strips * 16
    gather_pixels(strips, j, pc, pix_ref, below_ref, above_ref, mid_ref)
    zs[:, 0:4] = jnp.zeros((3, 4, 8, 128), F32)
    zs[:, 4 + rows_all :] = jnp.zeros((3, 12, 8, 128), F32)
    sub = iota((128, 128), 0)
    crow, cframe = iota((128, 32), 1) % 16, iota((128, 32), 1) // 16
    csub = iota((128, 32), 0)
    arrived = [received(recv_ref[s]) for s in range(strips)]
    old_hits = []
    for a in range(3):
        ct = cframe - a
        cplace = jnp.where(ct >= 0, crow * 8 + (ct & 1) * 4 + (ct >> 1), -1)
        old_hits.append(jnp.where(csub == cplace, 1.0, 0.0))
    picks = []
    for _, slots in arrived:
        frame, row = slots >> 4, slots & 15
        hits = []
        for a in range(3):
            t = frame + 2 - a
            place = jnp.where(t < FRAMES, row * 8 + (t & 1) * 4 + (t >> 1), -1)
            hit = jnp.where(sub.reshape(16, 8, 128) == place[None], 1.0, 0.0).reshape(128, 128)
            hits.append(jnp.concatenate([hit, old_hits[a]], axis=1).astype(BF16))
        picks.append(jnp.concatenate(hits, axis=0))
    sources = [
        jnp.concatenate([arrived[s][0], pc[s]], axis=0).astype(BF16) for s in range(strips)
    ]
    placed = [dot(picks[s], sources[s]).reshape(3, 16, 8, 128) for s in range(strips)]
    for s in range(strips):
        for a in range(3):
            zs[a, 4 + s * 16 : 4 + (s + 1) * 16] = placed[s][a]
    target = whole(scalars_ref, 1).astype(F32)
    last = valid - 1
    line_rows = zs.reshape(3 * (rows_all + 16) * 8, 128)
    lines = []
    for a in range(3):
        at = (a * (rows_all + 16) + 3 + j * 16) * 8 + (last & 1) * 4 + (last >> 1)
        lines.append(line_rows[pl.ds(at, 24, stride=8)])
    left = jnp.where(iota((24, 128), 1) < 64, lines[0], pltpu.roll(lines[1], 64, 1))
    pay_ref[16:64] = jnp.concatenate([left, lines[2]], axis=0).astype(BF16)
    high = rows_all + 4
    for b in range(3):
        for a in range(3):
            q = (b * 3 + a) * 48
            xs[2 : high + 2, :, q : q + 48] = zs[a, 1 + b : high + 1 + b, :, 0:48]
    patches = xs[2 : high + 2].reshape(high * 8, 432).astype(BF16)
    ys[...] = dot(patches, spread_matrix()).reshape(high, 8, 1024)
    full = ys[2 : 2 + rows_all].reshape(rows_all * 8, 1024).astype(BF16)
    base = j * 16
    first, second = ys[pl.ds(base, 11)], ys[pl.ds(base + 8, 11)]
    low = iota((11, 8, 1024), 1) < 4
    own_even = jnp.where(low, first, pltpu.roll(second, 4, 1))
    own_odd = jnp.where(low, pltpu.roll(first, 4, 1), second)
    own = jnp.concatenate([own_even, own_odd], axis=0).reshape(176, 1024).astype(BF16)
    weight = weight_ref[...]
    s1 = jnp.zeros((8, 256), F32)
    s2 = jnp.zeros((8, 256), F32)
    for chunk in range(8):
        out = dot(full[:, chunk * 128 : chunk * 128 + 128], weight).astype(BF16).astype(F32).reshape(rows_all, 8, 256)
        s1 = s1 + jnp.sum(out, axis=0)
        s2 = s2 + jnp.sum(out * out, axis=0)
        mine = dot(own[:, chunk * 128 : chunk * 128 + 128], weight).astype(BF16).astype(F32).reshape(2, 11, 8, 256)
        for i in range(2):
            stem[:, 2 * chunk + i] = mine[:, :, :, i * 128 : (i + 1) * 128]
    s1 = s1[:, 0:128] + s1[:, 128:256]
    s2 = s2[:, 0:128] + s2[:, 128:256]
    scale, shift = norm_rows(strips, s1, s2, gain_ref, bias_ref)
    norm_ref[0] = scale
    norm_ref[1] = shift
    stem_rows = stem.reshape(2 * 16 * 11 * 8, 128)
    t = valid - 2
    scale_t, shift_t = frame_row(scale, t), frame_row(shift, t)
    for y in range(16):
        block = silu(stem_rows[pl.ds(row_at(t, y), 16, stride=88)] * scale_t + shift_t)
        block = jnp.where(valid < 2, old_ref[1, y].astype(F32), block)
        pay_ref[64 + y * 16 : 80 + y * 16] = block.astype(BF16)
    pieces = []
    for row in (frame_row(scale, last), frame_row(shift, last)):
        for _ in range(3):
            piece = row.astype(BF16).astype(F32)
            pieces.append(piece)
            row = row - piece
    row16 = iota((16, 128), 0)
    norms = jnp.where(row16 == 0, target, 0.0)
    for n, piece in enumerate(pieces):
        norms = jnp.where(row16 == n + 1, piece, norms)
    pay_ref[0:16] = norms.astype(BF16)


def last_kernel(
    scalars_ref,
    norm_ref,
    stem,
    old_ref,
    res_old_ref,
    below_ref,
    above_ref,
    conv_ref,
    pay_ref,
    lines,
):
    j = lax.axis_index("strip")
    valid = whole(scalars_ref, 0)
    scale, shift = norm_ref[0], norm_ref[1]
    has_above = jnp.where(j > 0, 1.0, 0.0)
    has_below = jnp.where(j < lax.axis_size("strip") - 1, 1.0, 0.0)
    stem_rows = stem.reshape(2 * 16 * 11 * 8, 128)
    column = iota((16, 128), 0)

    def side_by_side(m, y, block):
        before = jnp.where(column == 0, 0.0, pltpu.roll(block, 1, 0))
        after = jnp.where(column == 15, 0.0, pltpu.roll(block, 15, 0))
        lines[m, y + 1] = jnp.concatenate([before, block, after], axis=1).astype(BF16)

    for m in range(4):
        from_cache = valid - 2 + m

        @pl.when(from_cache >= 2)
        def _(m=m, from_cache=from_cache):
            t = from_cache - 2
            scale_m, shift_m = frame_row(scale, t), frame_row(shift, t)
            for y in range(-1, 17):
                block = stem_rows[pl.ds(row_at(t, y), 16, stride=88)]
                block = silu(block * scale_m + shift_m)
                if y < 0:
                    block = block * has_above
                if y > 15:
                    block = block * has_below
                side_by_side(m, y, block)

        @pl.when(from_cache < 2)
        def _(m=m, from_cache=from_cache):
            f = jnp.clip(from_cache, 0, 1)
            side_by_side(m, -1, below_ref[2 * f + 1].astype(F32) * has_above)
            for y in range(16):
                side_by_side(m, y, old_ref[f, y].astype(F32))
            side_by_side(m, 16, above_ref[f].astype(F32) * has_below)

    zero = jnp.zeros((384, 128), BF16)

    def weight(a, b):
        if not 0 <= b <= 2:
            return zero
        return jnp.concatenate([conv_ref[a, b, e] for e in range(3)], axis=0)

    weights = jnp.concatenate(
        [
            jnp.concatenate([weight(a, y - k) for k in range(2)], axis=1)
            for y in range(4)
            for a in range(3)
        ],
        axis=0,
    )
    left = jnp.concatenate(
        [
            jnp.concatenate(
                [lines[i + a, 2 * k + y] for i in range(2) for k in range(8)], axis=0
            )
            for y in range(4)
            for a in range(3)
        ],
        axis=1,
    )
    out = dot(left, weights).reshape(2, 8, 16, 256)
    for i in range(2):
        for y in range(16):
            block = stem_rows[pl.ds(row_at(valid - 2 + i, y), 16, stride=88)]
            block = block + out[i, y // 2, :, y % 2 * 128 : y % 2 * 128 + 128]
            if i == 0:
                block = jnp.where(valid < 2, res_old_ref[1, y].astype(F32), block)
            pay_ref[i * 16 + y] = block


def seal_kernel(after_ref, value_ref, out_ref):
    del after_ref
    out_ref[...] = value_ref[...].reshape(512, 128).astype(BF16)


def conv_kernel(
    strips,
    w0,
    after_ref,
    after_too_ref,
    norm_ref,
    stem,
    old_ref,
    below_ref,
    above_ref,
    conv_ref,
    out_ref,
    rows_ref,
    cache,
    act3,
):
    del after_too_ref
    rows_ref[...] = after_ref[0:16] if w0 == 0 else jnp.zeros((16, 128), BF16)
    j = lax.axis_index("strip")
    widen_cache(strips, j, cache, old_ref, below_ref, above_ref)
    low8 = iota((8, 128), 0) < 4
    scales, shifts = [], []
    for k, rows in enumerate((scales, shifts)):
        v = norm_ref[k]
        rows.append(jnp.where(low8, v, pltpu.roll(v, 4, 0)))
        rows.append(jnp.where(low8, pltpu.roll(v, 4, 0), v))
    half = iota((11, 8, 128), 1) // 4
    line_of = j * 16 + iota((11, 8, 128), 0) - 2 + 8 * half
    inside = jnp.where((line_of >= 0) & (line_of < strips * 16), 1.0, 0.0)
    at0 = iota((11, 8, 128), 1) == 0
    at4 = iota((11, 8, 128), 1) == 4
    edge = 0 if w0 == 0 else 9
    act3[edge] = jnp.zeros(act3.shape[1:], BF16)
    shift = 1 if w0 == 0 else 1 - w0

    def arrange(w, carry):
        late = []
        even, odd = [silu(stem[p, w] * scales[p] + shifts[p]) * inside for p in range(2)]
        for f in range(2):
            rows = [
                jnp.broadcast_to(cache[f, pl.ds(y * 16 + w, 1)], (8, 128)) for y in range(19)
            ]
            upper, lower = jnp.stack(rows[0:11], axis=0), jnp.stack(rows[8:19], axis=0)
            rolled = pltpu.roll((even, odd)[f], 1, 1)
            late.append(jnp.where(at0, upper, jnp.where(at4, lower, rolled)))
        taps = ((late[0], late[1]), (late[1], even), (even, odd))
        for a in range(3):
            act3[w + shift, :, :, a * 128 : (a + 1) * 128] = jnp.concatenate(taps[a], axis=1).astype(BF16)
        return carry

    lax.fori_loop(max(w0 - 1, 0), min(w0 + 9, 16), arrange, 0, unroll=9)
    weights = pair_weight(conv_ref)
    outside = (j == 0) & (iota((9, 16, 128), 0) == 0) & (iota((9, 16, 128), 1) % 8 < 4)
    keep = jnp.where(outside, 0.0, 1.0)
    left = jnp.concatenate(
        [
            jnp.concatenate(
                [act3[2 * k + col, b : b + 9].reshape(144, 384) for k in range(4)],
                axis=0,
            )
            for col in range(4)
            for b in range(3)
        ],
        axis=1,
    )
    out = dot(left, weights).reshape(4, 9, 16, 256)
    for k in range(4):
        for n in range(2):
            w = w0 + 2 * k + n
            value = out[k, :, :, n * 128 : n * 128 + 128]
            value = value + jnp.concatenate([stem[0, w, 1:10], stem[1, w, 1:10]], axis=1)
            out_ref[w - w0] = (value * keep).astype(BF16)


def down_kernel(
    scalars_ref,
    part_ref,
    rest_ref,
    down_ref,
    res_cache_ref,
    below_ref,
    after_ref,
    lat_ref,
    rcache,
    res3,
    lat,
):
    del after_ref
    j = lax.axis_index("strip")
    valid = whole(scalars_ref, 0)
    rcache[...] = jnp.zeros(rcache.shape, F32)
    has_above = jnp.where(j > 0, 1.0, 0.0)
    for f in range(2):
        rcache[f, 0:16] = below_ref[4 + f].astype(F32) * has_above
        rcache[f, 16:272] = res_cache_ref[f].reshape(256, 128).astype(F32)
    at0 = iota((9, 8, 128), 1) == 0
    at4 = iota((9, 8, 128), 1) == 4
    res3[0] = jnp.zeros(res3.shape[1:], F32)

    for w0, ref in ((0, part_ref), (8, rest_ref)):

        def delay(w, carry, w0=w0, ref=ref):
            both = ref[w].astype(F32)
            even, odd = both[:, 0:8], both[:, 8:16]
            olds = []
            for f in range(2):
                rows = [
                    jnp.broadcast_to(rcache[f, pl.ds(y * 16 + w0 + w, 1)], (8, 128))
                    for y in range(17)
                ]
                olds.append((jnp.stack(rows[0:9], axis=0), jnp.stack(rows[8:17], axis=0)))
            at = w0 + w + 1
            for f, v in enumerate((even, odd)):
                rolled = pltpu.roll(v, 1, 1)
                late = jnp.where(at0, olds[f][0], jnp.where(at4, olds[f][1], rolled))
                res3[at, :, :, f * 128 : f * 128 + 128] = late
            res3[at, :, :, 256:384] = even
            return carry

        lax.fori_loop(0, 8, delay, 0, unroll=8)
    total = jnp.zeros((256, 256), F32)
    for b in range(3):
        for e in range(3):
            left = jnp.concatenate(
                [res3[2 * k + e, 2 * i + b] for k in range(8) for i in range(4)], axis=0
            ).astype(BF16)
            right = jnp.concatenate([down_ref[a, b, e] for a in range(3)], axis=0)
            total = total + dot(left, right)
    live = 2 * (iota((256, 256), 0) % 4) < valid
    total = jnp.where(live, total, 0.0)
    for o in range(2):
        lat[o] = total[:, o * 128 : (o + 1) * 128]
    for t in range(4):
        for h in range(2):
            for i in range(4):
                for o in range(2):
                    block = lat[o, pl.ds(i * 8 + h * 4 + t, 8, stride=32)]
                    lat_ref[t, h * 4 + i, :, o * 128 : (o + 1) * 128] = block.astype(BF16)


def finish_kernel(
    bit,
    after_ref,
    first_ref,
    first_in_ref,
    weight_ref,
    new_pix_ref,
    new_act_ref,
    rows,
    patch,
    frame,
):
    del after_ref
    target = first_ref[0:16].astype(F32).astype(jnp.int32)
    mine = (target >> bit) & 1 == (lax.axis_index("stream") >> bit) & 1
    mine = jnp.where(mine, 1.0, 0.0)[0:1] > 0.5

    def chosen(start, stop):
        own, other = first_ref[start:stop].astype(F32), first_in_ref[start:stop].astype(F32)
        return jnp.where(mine, own, other)

    new_act_ref[0] = chosen(64, 320).astype(BF16).reshape(16, 16, 128)
    lines = chosen(16, 64)
    left = lines[0:24]
    rows[0] = left
    rows[1] = pltpu.roll(left, 64, 1)
    rows[2] = lines[24:48]
    for i in range(2):
        new_pix_ref[i] = rows[1 + i, 1:17, 0:48].astype(BF16)
    norms = chosen(0, 16)
    scale = norms[1:2] + norms[2:3] + norms[3:4]
    shift = norms[4:5] + norms[5:6] + norms[6:7]
    for b in range(3):
        for a in range(3):
            q = (b * 3 + a) * 48
            patch[:, q : q + 48] = rows[a, b : b + 16, 0:48]
    spread = dot(patch[...].astype(BF16), spread_matrix()).astype(BF16)
    weight = weight_ref[...]
    for chunk in range(8):
        out = dot(spread[:, chunk * 128 : chunk * 128 + 128], weight).astype(BF16).astype(F32)
        for n in range(2):
            at = (2 * chunk + n) * 16
            frame[at : at + 16] = silu(out[:, n * 128 : n * 128 + 128] * scale + shift)
    for y in range(16):
        new_act_ref[1, y] = frame[pl.ds(y, 16, stride=16)].astype(BF16)


def partner(value, axis, stride):
    pairs = [(source, source ^ stride) for source in range(lax.axis_size(axis))]
    return lax.ppermute(value, axis, pairs)


def shifted(value, axis, by):
    size = lax.axis_size(axis)
    return lax.ppermute(value, axis, [(i, (i + by) % size) for i in range(size)])


def body(
    loader_rows,
    load_owner,
    load_slot,
    valid_frames,
    next_owner,
    pixel_cache,
    act_cache,
    res_cache,
    stem_weight,
    norm_gain,
    norm_bias,
    conv_weight,
    down_weight,
):
    streams = lax.axis_size("stream")
    strips = lax.axis_size("strip")
    stream_pos = lax.axis_index("stream")
    sections = streams.bit_length() - 1
    fill = loader_rows.shape[1]
    per = fill // streams
    pix, acts, ress = pixel_cache[0], act_cache[0], res_cache[0]
    mega = 1024 * 1024
    cost = pl.CostEstimate(flops=2 * 10**9, bytes_accessed=4 * mega, transcendentals=0)
    half_per = fill // streams // 2
    direct = half_per % 8 == 0
    line_shape = (strips, streams, half_per, 128) if direct else (fill // 2, 128)
    lines = pl.pallas_call(
        functools.partial(sort_kernel, streams),
        out_shape=jax.ShapeDtypeStruct(line_shape, BF16),
        in_specs=[VM] * 3,
        out_specs=VM,
        scratch_shapes=[pltpu.VMEM((128, 2 * fill), F32)],
        cost_estimate=cost,
    )(loader_rows[0].T, load_owner, load_slot)
    if not direct:
        lines = lines.reshape(1, streams, half_per, 128)
        lines = jnp.broadcast_to(lines, (strips, streams, half_per, 128))
    lines = lines.reshape(strips * streams, half_per, 128)
    recv = lax.all_to_all(lines, ("strip", "stream"), 0, 0, tiled=True)
    recv = recv.reshape(strips, fill // 2, 128)
    below, above, near, mid, weight = pl.pallas_call(
        pack_kernel,
        out_shape=(
            jax.ShapeDtypeStruct((6, 16, 128), BF16),
            jax.ShapeDtypeStruct((4, 16, 128), BF16),
            jax.ShapeDtypeStruct((2, 16, 128), BF16),
            jax.ShapeDtypeStruct((2, 16, 128), BF16),
            jax.ShapeDtypeStruct((128, 256), BF16),
        ),
        in_specs=[VM] * 2 + [ANY] * 2,
        out_specs=(VM,) * 5,
        scratch_shapes=[pltpu.VMEM((128, 256), F32), pltpu.SemaphoreType.DMA((6,))],
        compiler_params=pltpu.CompilerParams(vmem_limit_bytes=4 * mega),
    )(pix, stem_weight, acts, ress)
    below = shifted(below, "strip", 1)
    near = shifted(near, "strip", 1)
    above = shifted(above, "strip", -1)
    mid = shifted(mid, "strip", 2)
    scalars = jnp.concatenate([valid_frames, next_owner, jnp.zeros((126,), jnp.int32)])
    rows_all = strips * 16
    window = jax.ShapeDtypeStruct((2, 16, 11, 8, 128), F32)
    first, norm, stem = pl.pallas_call(
        functools.partial(stem_kernel, strips),
        out_shape=(
            jax.ShapeDtypeStruct((320, 128), BF16),
            jax.ShapeDtypeStruct((2, 8, 128), F32),
            window,
        ),
        in_specs=[VM] * 10,
        out_specs=(VM,) * 3,
        scratch_shapes=[
            pltpu.VMEM((strips, 32, 128), F32),
            pltpu.VMEM((3, rows_all + 16, 8, 128), F32),
            pltpu.VMEM((rows_all + 8, 8, 432), F32),
            pltpu.VMEM((rows_all + 4, 8, 1024), F32),
        ],
        compiler_params=pltpu.CompilerParams(vmem_limit_bytes=24 * mega),
        cost_estimate=cost,
    )(scalars, norm_gain, norm_bias, recv, pix, acts, near, above, mid, weight)
    keeps = []

    def kept(rows, bit):
        return (rows[0:1].astype(jnp.int32) >> bit) & 1 == (stream_pos >> bit) & 1

    def passed(value, bit):
        if bit == len(keeps):
            keeps.append(kept(value, bit))
        return jnp.where(keeps[bit], value, partner(value, "stream", 1 << bit))

    second = pl.pallas_call(
        last_kernel,
        out_shape=jax.ShapeDtypeStruct((32, 16, 128), F32),
        in_specs=[VM] * 8,
        out_specs=VM,
        scratch_shapes=[pltpu.VMEM((4, 18, 16, 384), BF16)],
        compiler_params=pltpu.CompilerParams(vmem_limit_bytes=24 * mega),
        cost_estimate=cost,
    )(scalars, norm, stem, acts, ress, below, above, conv_weight)
    first = passed(first, 0)
    second = pl.pallas_call(
        seal_kernel,
        out_shape=jax.ShapeDtypeStruct((512, 128), BF16),
        in_specs=[ANY, VM],
        out_specs=VM,
        compiler_params=pltpu.CompilerParams(vmem_limit_bytes=8 * mega),
    )(first, second)
    second = passed(second, 0)

    def convolved(w0, after, after_too):
        return pl.pallas_call(
            functools.partial(conv_kernel, strips, w0),
            out_shape=(
                jax.ShapeDtypeStruct((8, 9, 16, 128), BF16),
                jax.ShapeDtypeStruct((16, 128), BF16),
            ),
            in_specs=[VM if w0 == 0 else ANY, ANY] + [VM] * 6,
            out_specs=(VM,) * 2,
            scratch_shapes=[
                pltpu.VMEM((2, 416, 128), F32),
                pltpu.VMEM((10, 11, 16, 384), BF16),
            ],
            compiler_params=pltpu.CompilerParams(vmem_limit_bytes=24 * mega),
            cost_estimate=cost,
        )(after, after_too, norm, stem, acts, below, above, conv_weight)

    part, rows = convolved(0, first, second)
    for bit in range(1, sections - 1):
        if bit == 1:
            keeps.append(kept(rows, bit))
        first = passed(first, bit)
    rest, _ = convolved(8, first, part)
    for bit in range(1, sections - 1):
        second = passed(second, bit)
    latent = pl.pallas_call(
        down_kernel,
        out_shape=jax.ShapeDtypeStruct((4, 8, 8, 256), BF16),
        in_specs=[VM] * 6 + [ANY],
        out_specs=VM,
        scratch_shapes=[
            pltpu.VMEM((2, 384, 128), F32),
            pltpu.VMEM((17, 9, 8, 384), F32),
            pltpu.VMEM((2, 256, 128), F32),
        ],
        compiler_params=pltpu.CompilerParams(vmem_limit_bytes=24 * mega),
        cost_estimate=cost,
    )(scalars, part, rest, down_weight, ress, below, second)
    bit = sections - 1
    if bit == len(keeps):
        keeps.append(kept(first, bit))
    new_pix, new_act = pl.pallas_call(
        functools.partial(finish_kernel, bit),
        out_shape=(
            jax.ShapeDtypeStruct(pix.shape, BF16),
            jax.ShapeDtypeStruct(acts.shape, BF16),
        ),
        in_specs=[ANY] + [VM] * 3,
        out_specs=(VM,) * 2,
        scratch_shapes=[
            pltpu.VMEM((3, 24, 128), F32),
            pltpu.VMEM((16, 432), F32),
            pltpu.VMEM((256, 128), F32),
        ],
        compiler_params=pltpu.CompilerParams(vmem_limit_bytes=8 * mega),
        cost_estimate=cost,
    )(second, first, partner(first, "stream", 1 << bit), weight)
    second = passed(second, bit)
    return (latent[None], new_pix[None], new_act[None], second.reshape(1, 2, 16, 16, 128))


def solution(mesh):
    in_specs = (
        P("stream", "strip", None),
        P("stream", "strip"),
        P("stream", "strip"),
        P("stream"),
        P("stream"),
        P("stream", None, "strip", None),
        P("stream", None, "strip", None, None),
        P("stream", None, "strip", None, None),
        P(),
        P(),
        P(),
        P(),
        P(),
    )
    out_specs = (
        P("stream", None, "strip", None, None),
        P("stream", None, "strip", None),
        P("stream", None, "strip", None, None),
        P("stream", None, "strip", None, None),
    )
    return jax.shard_map(body, mesh=mesh, in_specs=in_specs, out_specs=out_specs, check_vma=False)
```
